128 devices in a mesh: row: 16 (over y_lo, x, core), col: 8 (over z, y_hi).
Axes of the slice: x: 4, y: 4 (y_hi: 2, y_lo: 2; y = y_hi * 2 + y_lo), z: 4, core: 2. Of those that a mesh axis runs over, the one named last changes fastest.
Arguments:
- features: bfloat16 [65536, 128], P(('row', 'col')), may hold values from -6 to 6
- degree: int32 [65536], P(('row', 'col')), may hold values from 32 to 512
- cotangent: bfloat16 [65536, 256], P(('row', 'col')), may hold values from -24 to 24
- weight: bfloat16 [128, 256], replicated, may hold values from -0.5 to 0.5
- layer_bias: float32 [256], replicated, may hold values from -3 to 3
- patterns: bfloat16 [64, 128, 128], replicated, may hold values from 0 to 1, as said below
- tile_row: int32 [16, 8, 512], P('row', 'col'), may hold values from 0 to 31
- tile_col: int32 [16, 8, 512], P('row', 'col'), may hold values from 0 to 63
- tile_pattern: int32 [16, 8, 512], P('row', 'col'), may hold values from 0 to 63
- tile_weight: int32 [16, 8, 512], P('row', 'col'), may hold values from 1 to 4
- tile_count: int32 [16, 8], P('row', 'col'), may hold values from 64 to 512, as said below
Outputs:
- activations: bfloat16 [65536, 256], P(('row', 'col'))
- grad_features: bfloat16 [65536, 128], P(('row', 'col'))
- grad_weight: float32 [128, 256], replicated
- grad_bias: float32 [256], replicated
The draws below stay inside these ranges and needn't reach their ends.
Inputs may be any that keep to these rules, and one draw needn't show every extreme that they name: `tile_row`: slots may name the same tile position more than once; such tiles add. `tile_count`: 512 is reached at some grid position in every draw. `patterns`: entries are 0 or 1.
All inputs are finite; a program needn't handle non-finite values.
Results may differ from the reference program's by a relative error of at most 0.0058.
Values may be sent and summed in bfloat16 or wider, within the bound.
No kernel may reach another device: no remote copies, remote signals or barrier semaphores. Data moves between devices by JAX's collectives and lax.ppermute only.
A program may use at most 128 MiB of HBM per device.

```python
import math
import jax
import jax.numpy as jnp
from jax import lax

F = 128
HID = 256
TILE = 128
PATTERNS = 64
NODE_DEV = 512
TPD = 512
NODES = 65536
TROWS = 32
TCOLS = 64
N_ROW = 16
N_COL = 8


def draw_cotangent(key, part):
    key = jax.random.fold_in(key, 11)
    rising = 1.0 + 2.0 * jnp.arange(NODES, dtype=jnp.float32) / NODES
    drawn = jax.random.normal(key, (NODES, HID), jnp.float32) * rising[:, None]
    return drawn.astype(jnp.bfloat16)


def draw_patterns(key, part):
    key = jax.random.fold_in(key, 12)
    tile_marks = jax.random.bernoulli(key, 0.025, (PATTERNS, TILE, TILE))
    return tile_marks.astype(jnp.float32).astype(jnp.bfloat16)


def draw_tile_count(key, part):
    key = jax.random.fold_in(key, 13)
    draw_one, draw_two, busiest_key = jax.random.split(key, 3)
    least_live = TPD // 8
    span_width = TPD - least_live + 1
    first_draw = jax.random.randint(draw_one, (N_ROW, N_COL), 0, span_width)
    second = jax.random.randint(draw_two, (N_ROW, N_COL), 0, span_width)
    counted = least_live + first_draw * second // span_width
    busiest = jax.random.randint(busiest_key, (), 0, N_ROW * N_COL)
    flattened = counted.reshape(-1).at[busiest].set(TPD)
    return flattened.reshape(N_ROW, N_COL).astype(jnp.int32)


def plant(values, key, smallest, top_value):
    dims = values.shape
    spot = [jax.random.randint(jax.random.fold_in(key, axis), (), 0, dims[axis]) for axis in range(len(dims))]
    values = values.at[tuple(spot)].set(smallest)
    longest = dims.index(max(dims))
    spot[longest] = (spot[longest] + 1) % dims[longest]
    return values.at[tuple(spot)].set(top_value)


def level_of(stream_key, extent, shards, smallest, largest):
    factor_of, own = 1.0, jax.random.fold_in(stream_key, 6)
    for dim, blocks in shards:
        steps = jnp.exp(jax.random.uniform(jax.random.fold_in(own, dim), (blocks,), jnp.float32, smallest / len(shards), largest / len(shards)))
        factor_of = factor_of * jnp.repeat(steps, extent[dim] // blocks).reshape([-1 if axis == dim else 1 for axis in range(len(extent))])
    return factor_of


def noise(key, shape, deviation, reach, pieces=(), held_as=jnp.bfloat16):
    values = deviation * jax.random.normal(key, shape, jnp.float32)
    if pieces:
        values = values * level_of(key, shape, pieces, -0.22, 0.18)
    return jnp.clip(values, -reach, reach).astype(held_as)


def setup_inputs(seed: int = 0) -> dict:
    key_list = jax.random.split(jax.random.key(seed), 12)
    features = noise(key_list[0], (NODES, F), 1.0, 6.0, ((0, 128),))
    degree = plant(jax.random.randint(key_list[1], (NODES,), 32, 513), jax.random.fold_in(key_list[1], 1), 32, 512).astype(jnp.int32)
    cotangent = draw_cotangent(jax.random.fold_in(key_list[11], 71), 0)
    weight = noise(key_list[3], (F, HID), F ** -0.5, 0.5)
    layer_bias = noise(key_list[4], (HID,), 0.5, 3.0, (), jnp.float32)
    patterns = draw_patterns(jax.random.fold_in(key_list[11], 71), 0)
    tile_row = plant(jax.random.randint(key_list[6], (N_ROW, N_COL, TPD), 0, TROWS), jax.random.fold_in(key_list[6], 1), 0, TROWS - 1).astype(jnp.int32)
    tile_col = plant(jax.random.randint(key_list[7], (N_ROW, N_COL, TPD), 0, TCOLS), jax.random.fold_in(key_list[7], 1), 0, TCOLS - 1).astype(jnp.int32)
    tile_pattern = plant(jax.random.randint(key_list[8], (N_ROW, N_COL, TPD), 0, PATTERNS), jax.random.fold_in(key_list[8], 1), 0, PATTERNS - 1).astype(jnp.int32)
    tile_weight = plant(jax.random.randint(key_list[9], (N_ROW, N_COL, TPD), 1, 5), jax.random.fold_in(key_list[9], 1), 1, 4).astype(jnp.int32)
    tile_count = draw_tile_count(jax.random.fold_in(key_list[11], 71), 0)
    return {"features": features, "degree": degree, "cotangent": cotangent, "weight": weight, "layer_bias": layer_bias, "patterns": patterns, "tile_row": tile_row, "tile_col": tile_col, "tile_pattern": tile_pattern, "tile_weight": tile_weight, "tile_count": tile_count}


def gelu_slope(values, upstream):
    return jax.vjp(lambda inner: jax.nn.gelu(inner, approximate=True), values)[1](upstream)[0]

def block_product(panel_tiles, sources, targets, pattern_ids, multiples, live_mask, patterns, target_count, transposed):
    factor = jnp.where(live_mask, multiples, 0).astype(jnp.float32)
    matrices = patterns[pattern_ids].astype(jnp.float32) * factor[:, None, None]
    blocks = panel_tiles[sources].astype(jnp.float32)
    if transposed:
        products = jnp.einsum('kba,kbh->kah', matrices, blocks, precision=lax.Precision.HIGHEST)
    else:
        products = jnp.einsum('kab,kbh->kah', matrices, blocks, precision=lax.Precision.HIGHEST)
    return jax.ops.segment_sum(products, targets, num_segments=target_count)

def reference(features, degree, cotangent, weight, layer_bias, patterns, tile_row, tile_col, tile_pattern, tile_weight, tile_count):
    inv_root = lax.rsqrt(degree.astype(jnp.float32))
    scaled = (inv_root[:, None] * jnp.dot(features, weight, preferred_element_type=jnp.float32)).astype(jnp.bfloat16)
    node_grid = scaled.reshape(N_ROW, N_COL, NODE_DEV, HID)
    live_all = jnp.arange(TPD, dtype=jnp.int32)[None, None, :] < tile_count[:, :, None]

    def row_block(row_index):

        def add_column(running, col_index):
            panel_tiles = node_grid[:, col_index].reshape(TCOLS, TILE, HID)
            partial_term = block_product(panel_tiles, tile_col[row_index, col_index], tile_row[row_index, col_index], tile_pattern[row_index, col_index], tile_weight[row_index, col_index], live_all[row_index, col_index], patterns, TROWS, False)
            return (running + partial_term, None)
        running, _ = lax.scan(add_column, jnp.zeros((TROWS, TILE, HID), jnp.float32), jnp.arange(N_COL, dtype=jnp.int32))
        return running
    summed = lax.map(row_block, jnp.arange(N_ROW, dtype=jnp.int32)).reshape(NODES, HID)
    pre_act = inv_root[:, None] * summed + layer_bias[None, :]
    activations = jax.nn.gelu(pre_act, approximate=True).astype(jnp.bfloat16)
    slope = gelu_slope(pre_act, cotangent.astype(jnp.float32))
    upstream = (inv_root[:, None] * slope).astype(jnp.bfloat16)
    row_panels = upstream.reshape(N_ROW, N_COL * NODE_DEV, HID)

    def column_block(col_index):

        def add_row(running, row_index):
            panel_tiles = row_panels[row_index].reshape(TROWS, TILE, HID)
            partial_term = block_product(panel_tiles, tile_row[row_index, col_index], tile_col[row_index, col_index], tile_pattern[row_index, col_index], tile_weight[row_index, col_index], live_all[row_index, col_index], patterns, TCOLS, True)
            return (running + partial_term, None)
        running, _ = lax.scan(add_row, jnp.zeros((TCOLS, TILE, HID), jnp.float32), jnp.arange(N_ROW, dtype=jnp.int32))
        return running
    back_sums = lax.map(column_block, jnp.arange(N_COL, dtype=jnp.int32))
    back_sums = back_sums.reshape(N_COL, N_ROW, NODE_DEV, HID).transpose(1, 0, 2, 3).reshape(NODES, HID)
    grad_hidden = (inv_root[:, None] * back_sums).astype(jnp.bfloat16)
    grad_features = lax.dot_general(grad_hidden, weight, (((1,), (1,)), ((), ())), preferred_element_type=jnp.float32).astype(jnp.bfloat16)
    scale_factor = 1.0 / math.sqrt(NODES)
    grad_weight = lax.dot_general(features, grad_hidden, (((0,), (0,)), ((), ())), preferred_element_type=jnp.float32) * scale_factor
    grad_bias = lax.optimization_barrier(jnp.sum(slope, axis=0)) * scale_factor
    return (activations, grad_features, grad_weight, grad_bias)
```

```python
import math

import jax
import jax.numpy as jnp
from jax import lax
from jax.experimental import pallas as pl
from jax.experimental.pallas import tpu as pltpu
from jax.sharding import PartitionSpec as P

GROUP = 8
VMEM_LIMIT = 48 * 1024 * 1024
ROOT_2_PI = math.sqrt(2.0 / math.pi)
CUBIC = 0.044715


def tile_sums_kernel(
    count_ref, source_ref, target_ref, pattern_ref, multiple_ref, patterns_ref, panel_ref, out_ref
):
    edge = patterns_ref.shape[1]
    live = count_ref[0, 0]
    out_ref[...] = jnp.zeros_like(out_ref)

    def one_group(group, carry):
        terms = []
        for member in range(GROUP):
            slot = group * GROUP + member
            factor = jnp.where(slot < live, multiple_ref[slot], 0).astype(jnp.float32)
            tile = patterns_ref[pattern_ref[slot]]
            start = pl.multiple_of(source_ref[slot] * edge, edge)
            block = panel_ref[pl.ds(start, edge), :]
            product = jnp.dot(tile, block, preferred_element_type=jnp.float32)
            terms.append((target_ref[slot], factor, product))
        for target, factor, product in terms:
            rows = pl.ds(pl.multiple_of(target * edge, edge), edge)
            out_ref[rows, :] += factor * product
        return carry

    lax.fori_loop(0, (live + GROUP - 1) // GROUP, one_group, 0)


def tile_sums(count, sources, targets, pattern_ids, multiples, patterns, panel, target_count):
    smem = pl.BlockSpec(memory_space=pltpu.SMEM)
    vmem = pl.BlockSpec(memory_space=pltpu.VMEM)
    edge = patterns.shape[1]
    width = panel.shape[1]
    slots = sources.shape[0]
    return pl.pallas_call(
        tile_sums_kernel,
        out_shape=jax.ShapeDtypeStruct((target_count * edge, width), jnp.float32),
        in_specs=[smem] * 5 + [vmem] * 2,
        out_specs=vmem,
        compiler_params=pltpu.CompilerParams(vmem_limit_bytes=VMEM_LIMIT),
        cost_estimate=pl.CostEstimate(
            flops=2 * slots * edge * edge * width,
            bytes_accessed=patterns.size * 2 + panel.size * 2 + target_count * edge * width * 4,
            transcendentals=0,
        ),
    )(count, sources, targets, pattern_ids, multiples, patterns, panel)


def split_product(left, right, dims):
    high = left.astype(jnp.bfloat16)
    low = (left - high.astype(jnp.float32)).astype(jnp.bfloat16)
    return lax.dot_general(
        high, right, (dims, ((), ())), preferred_element_type=jnp.float32
    ) + lax.dot_general(low, right, (dims, ((), ())), preferred_element_type=jnp.float32)


def middle_kernel(
    sums_ref, degree_ref, cotangent_ref, weight_ref, bias_ref, act_ref, spread_ref, grads_ref
):
    inv_root = lax.rsqrt(degree_ref[...].astype(jnp.float32))
    sums = sums_ref[...]
    weight = weight_ref[...]
    pre_act = inv_root * split_product(sums, weight, ((1,), (0,))) + bias_ref[...]
    square = pre_act * pre_act
    bent = jnp.tanh(ROOT_2_PI * (pre_act + CUBIC * (pre_act * square)))
    half = 0.5 * (1.0 + bent)
    act_ref[...] = (pre_act * half).astype(jnp.bfloat16)
    rise = 0.5 * pre_act * (1.0 - bent * bent) * (ROOT_2_PI * (1.0 + 3.0 * CUBIC * square))
    slope = cotangent_ref[...].astype(jnp.float32) * (half + rise)
    upstream = (inv_root * slope).astype(jnp.bfloat16)
    spread_ref[...] = lax.dot_general(
        upstream, weight, (((1,), (1,)), ((), ())), preferred_element_type=jnp.float32
    ).astype(jnp.bfloat16)
    feature_count = weight.shape[0]
    grads_ref[:feature_count, :] = split_product(sums, upstream, ((0,), (0,)))
    bias_row = jnp.sum(slope, axis=0, keepdims=True)
    row_ids = lax.broadcasted_iota(jnp.int32, (8, bias_row.shape[1]), 0)
    grads_ref[feature_count:, :] = jnp.where(row_ids == 0, bias_row, 0.0)


def middle(sums, degree, cotangent, weight, bias):
    vmem = pl.BlockSpec(memory_space=pltpu.VMEM)
    nodes, hidden = cotangent.shape
    feature_count = weight.shape[0]
    return pl.pallas_call(
        middle_kernel,
        out_shape=(
            jax.ShapeDtypeStruct((nodes, hidden), jnp.bfloat16),
            jax.ShapeDtypeStruct((nodes, feature_count), jnp.bfloat16),
            jax.ShapeDtypeStruct((feature_count + 8, hidden), jnp.float32),
        ),
        in_specs=[vmem] * 5,
        out_specs=(vmem,) * 3,
        compiler_params=pltpu.CompilerParams(vmem_limit_bytes=VMEM_LIMIT),
    )(sums, degree[:, None], cotangent, weight, bias[None, :])


def per_device(
    features,
    degree,
    cotangent,
    weight,
    layer_bias,
    patterns,
    tile_row,
    tile_col,
    tile_pattern,
    tile_weight,
    tile_count,
):
    node_dev = features.shape[0]
    row_devices = lax.axis_size("row")
    col_devices = lax.axis_size("col")
    tile_edge = patterns.shape[1]
    rows_local = tile_row[0, 0]
    cols_local = tile_col[0, 0]
    pattern_local = tile_pattern[0, 0]
    weight_local = tile_weight[0, 0]
    turned = jnp.swapaxes(patterns, 1, 2)
    inv_root = lax.rsqrt(degree.astype(jnp.float32))

    scaled = (inv_root[:, None] * features.astype(jnp.float32)).astype(jnp.bfloat16)
    col_panel = lax.all_gather(scaled, "row", axis=0, tiled=True)
    row_partial = tile_sums(
        tile_count,
        cols_local,
        rows_local,
        pattern_local,
        weight_local,
        patterns,
        col_panel,
        col_devices * node_dev // tile_edge,
    )
    own_sums = lax.psum_scatter(row_partial, "col", scatter_dimension=0, tiled=True)
    activations, spread, grads = middle(own_sums, degree, cotangent, weight, layer_bias)
    grads_total = lax.psum(grads, ("row", "col"))
    row_panel = lax.all_gather(spread, "col", axis=0, tiled=True)
    col_partial = tile_sums(
        tile_count,
        rows_local,
        cols_local,
        pattern_local,
        weight_local,
        turned,
        row_panel,
        row_devices * node_dev // tile_edge,
    )
    own_back = lax.psum_scatter(col_partial, "row", scatter_dimension=0, tiled=True)
    grad_features = (inv_root[:, None] * own_back).astype(jnp.bfloat16)
    scale_factor = 1.0 / math.sqrt(node_dev * row_devices * col_devices)
    feature_count = weight.shape[0]
    return (
        activations,
        grad_features,
        grads_total[:feature_count] * scale_factor,
        grads_total[feature_count] * scale_factor,
    )


def solution(mesh):
    in_specs = (
        P(("row", "col"), None),
        P(("row", "col")),
        P(("row", "col"), None),
        P(),
        P(),
        P(),
        P("row", "col", None),
        P("row", "col", None),
        P("row", "col", None),
        P("row", "col", None),
        P("row", "col"),
    )
    out_specs = (P(("row", "col"), None), P(("row", "col"), None), P(), P())
    return jax.shard_map(
        per_device, mesh=mesh, in_specs=in_specs, out_specs=out_specs, check_vma=False
    )
```

```python
import functools
import math

import jax
import jax.numpy as jnp
from jax import lax
from jax.experimental import pallas as pl
from jax.experimental.pallas import tpu as pltpu
from jax.sharding import PartitionSpec as P

GROUP = 8
VMEM_LIMIT = 48 * 1024 * 1024
ROOT_2_PI = math.sqrt(2.0 / math.pi)
CUBIC = 0.044715
BIAS_ROWS = 16
ANY = pl.BlockSpec(memory_space=pl.ANY)
VMEM = pl.BlockSpec(memory_space=pltpu.VMEM)
SMEM = pl.BlockSpec(memory_space=pltpu.SMEM)
PARAMS = pltpu.CompilerParams(vmem_limit_bytes=VMEM_LIMIT)


def pack_slots(tile_row, tile_col, tile_pattern, tile_weight, live, per_shard, core):
    shard = tile_col // per_shard
    half = (shard % 2) ^ core
    place = (half * 8 + shard // 2) * per_shard + tile_col % per_shard
    slots = tile_col.shape[0]
    factor = jnp.where(jnp.arange(slots, dtype=jnp.int32) < live, tile_weight, 0)
    return place | (tile_row << 6) | (tile_pattern << 11) | (factor << 17)


def unpack_slot(word):
    return word & 63, (word >> 6) & 31, (word >> 11) & 63, (word >> 17).astype(jnp.float32)


def root_columns(degree):
    rows = lax.rsqrt(degree.astype(jnp.float32))
    rows = jnp.concatenate([rows, jnp.ones((8 - rows.shape[0], rows.shape[1]), jnp.float32)], 0)
    return rows.T


def scale_kernel(features_ref, degree_ref, out_ref):
    roots = root_columns(degree_ref[...])
    edge = degree_ref.shape[1]
    for tile in range(degree_ref.shape[0]):
        rows = pl.ds(tile * edge, edge)
        scaled = features_ref[rows, :].astype(jnp.float32) * roots[:, tile : tile + 1]
        scaled = scaled.astype(jnp.bfloat16)
        for copy in range(out_ref.shape[0]):
            out_ref[copy, rows, :] = scaled


def forward_kernel(live_ref, slots_ref, patterns_ref, own_ref, other_ref, out_ref, panel, sums, sems):
    edge = patterns_ref.shape[1]
    half = own_ref.shape[0]
    copies = (
        pltpu.make_async_copy(own_ref, panel.at[pl.ds(0, half)], sems.at[0]),
        pltpu.make_async_copy(other_ref, panel.at[pl.ds(half, half)], sems.at[1]),
    )
    for copy in copies:
        copy.start()
    sums[...] = jnp.zeros_like(sums)
    for copy in copies:
        copy.wait()

    def one_group(group, carry):
        terms = []
        for member in range(GROUP):
            place, row, pattern, factor = unpack_slot(slots_ref[group * GROUP + member])
            block = panel[pl.ds(pl.multiple_of(place * edge, edge), edge), :]
            product = jnp.dot(patterns_ref[pattern], block, preferred_element_type=jnp.float32)
            terms.append((row, factor, product))
        for row, factor, product in terms:
            rows = pl.ds(pl.multiple_of(row * edge, edge), edge)
            sums[rows, :] += factor * product
        return carry

    lax.fori_loop(0, (live_ref[0, 0] + GROUP - 1) // GROUP, one_group, 0)
    out_ref[...] = sums[...].astype(jnp.bfloat16)


def backward_kernel(live_ref, slots_ref, patterns_ref, spread_ref, keep_ref, send_ref, sums):
    edge = patterns_ref.shape[1]
    shards, rows_in_shard, _ = spread_ref.shape
    half = sums.shape[0] // 2
    extra = keep_ref.shape[0] - half
    own = rows_in_shard - extra
    per_shard = own // edge
    sums[...] = jnp.zeros_like(sums)

    def one_group(group, carry):
        terms = []
        for member in range(GROUP):
            place, row, pattern, factor = unpack_slot(slots_ref[group * GROUP + member])
            start = pl.multiple_of((row % per_shard) * edge, edge)
            block = spread_ref[row // per_shard, pl.ds(start, edge), :]
            product = jnp.dot(block, patterns_ref[pattern], preferred_element_type=jnp.float32)
            terms.append((place, factor, product))
        for place, factor, product in terms:
            rows = pl.ds(pl.multiple_of(place * edge, edge), edge)
            sums[rows, :] += factor * product
        return carry

    lax.fori_loop(0, (live_ref[0, 0] + GROUP - 1) // GROUP, one_group, 0)
    keep_ref[:half, :] = sums[:half, :]
    send_ref[:half, :] = sums[half:, :].astype(jnp.bfloat16)
    grads = spread_ref[0, own:, :].astype(jnp.float32)
    for shard in range(1, shards):
        grads += spread_ref[shard, own:, :].astype(jnp.float32)
    grads = grads.astype(jnp.bfloat16)
    keep_ref[half:, :] = grads.astype(jnp.float32)
    send_ref[half:, :] = grads


def split_product(left, right, dims):
    high = left.astype(jnp.bfloat16)
    low = (left - high.astype(jnp.float32)).astype(jnp.bfloat16)
    return lax.dot_general(
        high, right, (dims, ((), ())), preferred_element_type=jnp.float32
    ) + lax.dot_general(low, right, (dims, ((), ())), preferred_element_type=jnp.float32)


def middle_kernel(parts_ref, degree_ref, cotangent_ref, weight_ref, bias_ref, act_ref, out_ref):
    tiles, edge = degree_ref.shape
    shards, nodes, feature_count = parts_ref.shape
    weight = weight_ref[...]
    roots = root_columns(degree_ref[...])
    grads = jnp.zeros(weight.shape, jnp.float32)
    bias_row = jnp.zeros(bias_ref.shape, jnp.float32)
    for tile in range(tiles):
        rows = pl.ds(tile * edge, edge)
        sums = parts_ref[0, rows, :].astype(jnp.float32)
        for shard in range(1, shards):
            sums += parts_ref[shard, rows, :].astype(jnp.float32)
        inv_root = roots[:, tile : tile + 1]
        pre_act = inv_root * split_product(sums, weight, ((1,), (0,))) + bias_ref[...]
        square = pre_act * pre_act
        bent = jnp.tanh(ROOT_2_PI * (pre_act + CUBIC * (pre_act * square)))
        half = 0.5 * (1.0 + bent)
        act_ref[rows, :] = (pre_act * half).astype(jnp.bfloat16)
        rise = 0.5 * pre_act * (1.0 - bent * bent) * (ROOT_2_PI * (1.0 + 3.0 * CUBIC * square))
        slope = cotangent_ref[rows, :].astype(jnp.float32) * (half + rise)
        upstream = (inv_root * slope).astype(jnp.bfloat16)
        spread = lax.dot_general(
            weight, upstream, (((1,), (1,)), ((), ())), preferred_element_type=jnp.float32
        ).astype(jnp.bfloat16)
        for shard in range(shards):
            out_ref[shard, rows, :] = spread
        grads += split_product(sums, upstream, ((0,), (0,)))
        bias_row += jnp.sum(slope, axis=0, keepdims=True)
    width = out_ref.shape[2]
    pieces = [grads[:, start : start + width] for start in range(0, grads.shape[1], width)]
    bias_high = bias_row.astype(jnp.bfloat16).astype(jnp.float32)
    row_ids = lax.broadcasted_iota(jnp.int32, (BIAS_ROWS, width), 0)
    bias_block = jnp.zeros((BIAS_ROWS, width), jnp.float32)
    place = 0
    for start in range(0, grads.shape[1], width):
        for part in (bias_high, bias_row - bias_high):
            bias_block = jnp.where(row_ids == place, part[:, start : start + width], bias_block)
            place += 1
    pieces.append(bias_block)
    tail = jnp.concatenate(pieces, 0).astype(jnp.bfloat16)
    for shard in range(shards):
        out_ref[shard, pl.ds(nodes, tail.shape[0]), :] = tail


def join_kernel(keep_ref, got_ref, out_ref):
    shards, rows_in_shard, _ = out_ref.shape
    extra = keep_ref.shape[0] - (keep_ref.shape[0] // shards // 128 * 128) * shards
    own = rows_in_shard - extra
    for shard in range(shards):
        rows = pl.ds(shard * own, own)
        total = keep_ref[rows, :] + got_ref[rows, :].astype(jnp.float32)
        out_ref[shard, pl.ds(0, own), :] = total.astype(jnp.bfloat16)
    rows = pl.ds(shards * own, extra)
    tail = (keep_ref[rows, :] + got_ref[rows, :].astype(jnp.float32)).astype(jnp.bfloat16)
    for shard in range(shards):
        out_ref[shard, pl.ds(own, extra), :] = tail


def last_kernel(scale_factor, parts_ref, degree_ref, features_ref, grads_ref, bias_ref):
    tiles, edge = degree_ref.shape
    shards, _, width = parts_ref.shape
    own = tiles * edge
    roots = lax.rsqrt(degree_ref[...].astype(jnp.float32))
    for tile in range(tiles):
        rows = pl.ds(tile * edge, edge)
        total = parts_ref[0, rows, :].astype(jnp.float32)
        for shard in range(1, shards):
            total += parts_ref[shard, rows, :].astype(jnp.float32)
        features_ref[rows, :] = (total * roots[tile : tile + 1, :]).T.astype(jnp.bfloat16)
    tail = parts_ref[0, own:, :].astype(jnp.float32)
    for shard in range(1, shards):
        tail += parts_ref[shard, own:, :].astype(jnp.float32)
    tail = tail * scale_factor
    height, columns = grads_ref.shape
    pieces = columns // width
    for piece in range(pieces):
        lanes = pl.ds(piece * width, width)
        grads_ref[:, lanes] = tail[piece * height : (piece + 1) * height, :]
        start = pieces * height + 2 * piece
        bias_ref[:, lanes] = tail[start : start + 1, :] + tail[start + 1 : start + 2, :]


def per_device(
    features,
    degree,
    cotangent,
    weight,
    layer_bias,
    patterns,
    tile_row,
    tile_col,
    tile_pattern,
    tile_weight,
    tile_count,
):
    node_dev, feature_count = features.shape
    hidden = weight.shape[1]
    row_devices = lax.axis_size("row")
    col_devices = lax.axis_size("col")
    chips = row_devices // 2
    edge = patterns.shape[1]
    per_shard = node_dev // edge
    core = lax.axis_index("row") % 2
    same_core = [list(range(first, row_devices, 2)) for first in range(2)]
    swap = [(index, index ^ 1) for index in range(row_devices)]
    across_chips = functools.partial(
        lax.all_to_all,
        axis_name="row",
        split_axis=0,
        concat_axis=0,
        axis_index_groups=same_core,
    )
    across_cols = functools.partial(lax.all_to_all, axis_name="col", split_axis=0, concat_axis=0)
    extra = hidden * feature_count // edge + BIAS_ROWS
    half = chips * node_dev
    bf16, f32 = jnp.bfloat16, jnp.float32
    shape = jax.ShapeDtypeStruct
    degree_tiles = degree.reshape(per_shard, edge)
    slots = pack_slots(
        tile_row[0, 0],
        tile_col[0, 0],
        tile_pattern[0, 0],
        tile_weight[0, 0],
        tile_count[0, 0],
        per_shard,
        core,
    )
    tile_cost = pl.CostEstimate(
        flops=2 * slots.shape[0] * edge * edge * feature_count,
        bytes_accessed=patterns.size * 2 + 4 * half * feature_count * 2,
        transcendentals=0,
    )

    scaled = pl.pallas_call(
        scale_kernel,
        out_shape=shape((chips, node_dev, feature_count), bf16),
        in_specs=[VMEM] * 2,
        out_specs=VMEM,
        compiler_params=PARAMS,
    )(features, degree_tiles)
    own_panel = across_chips(scaled).reshape(half, feature_count)
    other_panel = lax.ppermute(own_panel, "row", swap)
    row_part = pl.pallas_call(
        forward_kernel,
        out_shape=shape((col_devices * node_dev, feature_count), bf16),
        in_specs=[SMEM] * 2 + [VMEM] + [ANY] * 2,
        out_specs=VMEM,
        scratch_shapes=[
            pltpu.VMEM((2 * half, feature_count), bf16),
            pltpu.VMEM((col_devices * node_dev, feature_count), f32),
            pltpu.SemaphoreType.DMA((2,)),
        ],
        compiler_params=PARAMS,
        cost_estimate=tile_cost,
    )(tile_count, slots, patterns, own_panel, other_panel)
    parts = across_cols(row_part.reshape(col_devices, node_dev, feature_count))
    activations, spread = pl.pallas_call(
        middle_kernel,
        out_shape=(
            shape((node_dev, hidden), bf16),
            shape((col_devices, node_dev + extra, edge), bf16),
        ),
        in_specs=[VMEM] * 5,
        out_specs=(VMEM,) * 2,
        compiler_params=PARAMS,
    )(parts, degree_tiles, cotangent, weight, layer_bias[None, :])
    spread_all = across_cols(spread)
    keep, send = pl.pallas_call(
        backward_kernel,
        out_shape=(shape((half + extra, edge), f32), shape((half + extra, edge), bf16)),
        in_specs=[SMEM] * 2 + [VMEM] * 2,
        out_specs=(VMEM,) * 2,
        scratch_shapes=[pltpu.VMEM((2 * half, edge), f32)],
        compiler_params=PARAMS,
        cost_estimate=tile_cost,
    )(tile_count, slots, patterns, spread_all)
    got = lax.ppermute(send, "row", swap)
    joined = pl.pallas_call(
        join_kernel,
        out_shape=shape((chips, node_dev + extra, edge), bf16),
        in_specs=[VMEM] * 2,
        out_specs=VMEM,
        compiler_params=PARAMS,
    )(keep, got)
    back_parts = across_chips(joined)
    scale_factor = 1.0 / math.sqrt(node_dev * row_devices * col_devices)
    grad_features, grad_weight, grad_bias = pl.pallas_call(
        functools.partial(last_kernel, scale_factor),
        out_shape=(
            shape((node_dev, feature_count), bf16),
            shape((feature_count, hidden), f32),
            shape((1, hidden), f32),
        ),
        in_specs=[VMEM] * 2,
        out_specs=(VMEM,) * 3,
        compiler_params=PARAMS,
    )(back_parts, degree_tiles)
    return (activations, grad_features, grad_weight, grad_bias[0])


def solution(mesh):
    in_specs = (
        P(("row", "col"), None),
        P(("row", "col")),
        P(("row", "col"), None),
        P(),
        P(),
        P(),
        P("row", "col", None),
        P("row", "col", None),
        P("row", "col", None),
        P("row", "col", None),
        P("row", "col"),
    )
    out_specs = (P(("row", "col"), None), P(("row", "col"), None), P(), P())
    return jax.shard_map(
        per_device, mesh=mesh, in_specs=in_specs, out_specs=out_specs, check_vma=False
    )
```

```python
import functools
import math

import jax
import jax.numpy as jnp
from jax import lax
from jax.experimental import pallas as pl
from jax.experimental.pallas import tpu as pltpu
from jax.sharding import PartitionSpec as P

GROUP = 64
VMEM_LIMIT = 20 * 1024 * 1024
ROOT_2_PI = math.sqrt(2.0 / math.pi)
CUBIC = 0.044715
BIAS_ROWS = 16
ANY = pl.BlockSpec(memory_space=pl.ANY)
VMEM = pl.BlockSpec(memory_space=pltpu.VMEM)
SMEM = pl.BlockSpec(memory_space=pltpu.SMEM)
PARAMS = pltpu.CompilerParams(vmem_limit_bytes=VMEM_LIMIT)


def pack_slots(tile_row, tile_col, tile_pattern, tile_weight, live, per_shard, core):
    shard = tile_col // per_shard
    half = (shard % 2) ^ core
    place = (half * 8 + shard // 2) * per_shard + tile_col % per_shard
    slots = tile_col.shape[0]
    factor = jnp.where(jnp.arange(slots, dtype=jnp.int32) < live, tile_weight, 0)
    return place | (tile_row << 6) | (tile_pattern << 11) | (factor << 17)


def unpack_slot(word):
    return word & 63, (word >> 6) & 31, (word >> 11) & 63, (word >> 17).astype(jnp.float32)


def root_columns(degree):
    rows = lax.rsqrt(degree.astype(jnp.float32))
    rows = jnp.concatenate([rows, jnp.ones((8 - rows.shape[0], rows.shape[1]), jnp.float32)], 0)
    return rows.T


def scale_kernel(features_ref, degree_ref, out_ref):
    roots = root_columns(degree_ref[...])
    edge = degree_ref.shape[1]
    for tile in range(degree_ref.shape[0]):
        rows = pl.ds(tile * edge, edge)
        scaled = features_ref[rows, :].astype(jnp.float32) * roots[:, tile : tile + 1]
        scaled = scaled.astype(jnp.bfloat16)
        for copy in range(out_ref.shape[0]):
            out_ref[copy, rows, :] = scaled


def forward_kernel(live_ref, slots_ref, patterns_ref, own_ref, other_ref, out_ref, panel, sums, sems):
    edge = patterns_ref.shape[1]
    half = own_ref.shape[0]
    copies = (
        pltpu.make_async_copy(own_ref, panel.at[pl.ds(0, half)], sems.at[0]),
        pltpu.make_async_copy(other_ref, panel.at[pl.ds(half, half)], sems.at[1]),
    )
    for copy in copies:
        copy.start()
    sums[...] = jnp.zeros_like(sums)
    for copy in copies:
        copy.wait()

    def one_group(group, carry):
        terms = []
        for member in range(GROUP):
            place, row, pattern, factor = unpack_slot(slots_ref[group * GROUP + member])
            block = panel[pl.ds(pl.multiple_of(place * edge, edge), edge), :]
            product = jnp.dot(patterns_ref[pattern], block, preferred_element_type=jnp.float32)
            terms.append((row, factor, product))
        for row, factor, product in terms:
            rows = pl.ds(pl.multiple_of(row * edge, edge), edge)
            sums[rows, :] += factor * product
        return carry

    lax.fori_loop(0, (live_ref[0, 0] + GROUP - 1) // GROUP, one_group, 0)
    out_ref[...] = sums[...].astype(jnp.bfloat16)


def backward_kernel(live_ref, slots_ref, patterns_ref, spread_ref, keep_ref, send_ref, sums):
    edge = patterns_ref.shape[1]
    shards, rows_in_shard, _ = spread_ref.shape
    half = sums.shape[0] // 2
    extra = keep_ref.shape[0] - half
    own = rows_in_shard - extra
    per_shard = own // edge
    sums[...] = jnp.zeros_like(sums)

    def one_group(group, carry):
        terms = []
        for member in range(GROUP):
            place, row, pattern, factor = unpack_slot(slots_ref[group * GROUP + member])
            start = pl.multiple_of((row % per_shard) * edge, edge)
            block = spread_ref[row // per_shard, pl.ds(start, edge), :]
            product = jnp.dot(block, patterns_ref[pattern], preferred_element_type=jnp.float32)
            terms.append((place, factor, product))
        for place, factor, product in terms:
            rows = pl.ds(pl.multiple_of(place * edge, edge), edge)
            sums[rows, :] += factor * product
        return carry

    lax.fori_loop(0, (live_ref[0, 0] + GROUP - 1) // GROUP, one_group, 0)
    keep_ref[:half, :] = sums[:half, :]
    send_ref[:half, :] = sums[half:, :].astype(jnp.bfloat16)
    grads = spread_ref[0, own:, :].astype(jnp.float32)
    for shard in range(1, shards):
        grads += spread_ref[shard, own:, :].astype(jnp.float32)
    grads = grads.astype(jnp.bfloat16)
    keep_ref[half:, :] = grads.astype(jnp.float32)
    send_ref[half:, :] = grads


def split_product(left, right, dims):
    high = left.astype(jnp.bfloat16)
    low = (left - high.astype(jnp.float32)).astype(jnp.bfloat16)
    return lax.dot_general(
        high, right, (dims, ((), ())), preferred_element_type=jnp.float32
    ) + lax.dot_general(low, right, (dims, ((), ())), preferred_element_type=jnp.float32)


def middle_kernel(parts_ref, degree_ref, cotangent_ref, weight_ref, bias_ref, act_ref, out_ref):
    tiles, edge = degree_ref.shape
    shards, nodes, feature_count = parts_ref.shape
    weight = weight_ref[...]
    roots = root_columns(degree_ref[...])
    grads = jnp.zeros(weight.shape, jnp.float32)
    bias_row = jnp.zeros(bias_ref.shape, jnp.float32)
    for tile in range(tiles):
        rows = pl.ds(tile * edge, edge)
        sums = parts_ref[0, rows, :].astype(jnp.float32)
        for shard in range(1, shards):
            sums += parts_ref[shard, rows, :].astype(jnp.float32)
        inv_root = roots[:, tile : tile + 1]
        pre_act = inv_root * split_product(sums, weight, ((1,), (0,))) + bias_ref[...]
        square = pre_act * pre_act
        bent = jnp.tanh(ROOT_2_PI * (pre_act + CUBIC * (pre_act * square)))
        half = 0.5 * (1.0 + bent)
        act_ref[rows, :] = (pre_act * half).astype(jnp.bfloat16)
        rise = 0.5 * pre_act * (1.0 - bent * bent) * (ROOT_2_PI * (1.0 + 3.0 * CUBIC * square))
        slope = cotangent_ref[rows, :].astype(jnp.float32) * (half + rise)
        upstream = (inv_root * slope).astype(jnp.bfloat16)
        spread = lax.dot_general(
            weight, upstream, (((1,), (1,)), ((), ())), preferred_element_type=jnp.float32
        ).astype(jnp.bfloat16)
        for shard in range(shards):
            out_ref[shard, rows, :] = spread
        grads += split_product(sums, upstream, ((0,), (0,)))
        bias_row += jnp.sum(slope, axis=0, keepdims=True)
    width = out_ref.shape[2]
    pieces = [grads[:, start : start + width] for start in range(0, grads.shape[1], width)]
    bias_high = bias_row.astype(jnp.bfloat16).astype(jnp.float32)
    row_ids = lax.broadcasted_iota(jnp.int32, (BIAS_ROWS, width), 0)
    bias_block = jnp.zeros((BIAS_ROWS, width), jnp.float32)
    place = 0
    for start in range(0, grads.shape[1], width):
        for part in (bias_high, bias_row - bias_high):
            bias_block = jnp.where(row_ids == place, part[:, start : start + width], bias_block)
            place += 1
    stacked = jnp.concatenate(pieces, 0).astype(jnp.bfloat16)
    segment = stacked.shape[0] // shards
    bias_block = bias_block.astype(jnp.bfloat16)
    for shard in range(shards):
        out_ref[shard, pl.ds(nodes, segment), :] = stacked[shard * segment : (shard + 1) * segment]
        out_ref[shard, pl.ds(nodes + segment, BIAS_ROWS), :] = bias_block


def join_kernel(keep_ref, got_ref, out_ref):
    shards, rows_in_shard, _ = out_ref.shape
    extra = keep_ref.shape[0] - (keep_ref.shape[0] // shards // 128 * 128) * shards
    own = rows_in_shard - extra
    for shard in range(shards):
        rows = pl.ds(shard * own, own)
        total = keep_ref[rows, :] + got_ref[rows, :].astype(jnp.float32)
        out_ref[shard, pl.ds(0, own), :] = total.astype(jnp.bfloat16)
    rows = pl.ds(shards * own, extra)
    tail = (keep_ref[rows, :] + got_ref[rows, :].astype(jnp.float32)).astype(jnp.bfloat16)
    for shard in range(shards):
        out_ref[shard, pl.ds(own, extra), :] = tail


def last_kernel(scale_factor, parts_ref, degree_ref, features_ref, segment_ref, bias_ref):
    tiles, edge = degree_ref.shape
    shards, _, width = parts_ref.shape
    own = tiles * edge
    roots = lax.rsqrt(degree_ref[...].astype(jnp.float32))
    for tile in range(tiles):
        rows = pl.ds(tile * edge, edge)
        total = parts_ref[0, rows, :].astype(jnp.float32)
        for shard in range(1, shards):
            total += parts_ref[shard, rows, :].astype(jnp.float32)
        features_ref[rows, :] = (total * roots[tile : tile + 1, :]).T.astype(jnp.bfloat16)
    tail = parts_ref[0, own:, :].astype(jnp.float32)
    for shard in range(1, shards):
        tail += parts_ref[shard, own:, :].astype(jnp.float32)
    tail = tail * scale_factor
    copies, height, _ = segment_ref.shape
    for copy in range(copies):
        segment_ref[copy] = tail[:height, :]
    for piece in range(bias_ref.shape[1] // width):
        start = height + 2 * piece
        bias_ref[:, pl.ds(piece * width, width)] = (
            tail[start : start + 1, :] + tail[start + 1 : start + 2, :]
        )


def lay_out_kernel(segments_ref, grads_ref):
    shards, height, width = segments_ref.shape
    for piece in range(grads_ref.shape[1] // width):
        for part in range(grads_ref.shape[0] // height):
            shard = piece * (grads_ref.shape[0] // height) + part
            grads_ref[pl.ds(part * height, height), pl.ds(piece * width, width)] = segments_ref[shard]


def per_device(
    features,
    degree,
    cotangent,
    weight,
    layer_bias,
    patterns,
    tile_row,
    tile_col,
    tile_pattern,
    tile_weight,
    tile_count,
):
    node_dev, feature_count = features.shape
    hidden = weight.shape[1]
    row_devices = lax.axis_size("row")
    col_devices = lax.axis_size("col")
    chips = row_devices // 2
    edge = patterns.shape[1]
    per_shard = node_dev // edge
    core = lax.axis_index("row") % 2
    same_core = [list(range(first, row_devices, 2)) for first in range(2)]
    swap = [(index, index ^ 1) for index in range(row_devices)]
    across_chips = functools.partial(
        lax.all_to_all,
        axis_name="row",
        split_axis=0,
        concat_axis=0,
        axis_index_groups=same_core,
    )
    across_cols = functools.partial(lax.all_to_all, axis_name="col", split_axis=0, concat_axis=0)
    segment = hidden * feature_count // edge // col_devices
    extra = segment + BIAS_ROWS
    half = chips * node_dev
    bf16, f32 = jnp.bfloat16, jnp.float32
    shape = jax.ShapeDtypeStruct
    degree_tiles = degree.reshape(per_shard, edge)
    slots = pack_slots(
        tile_row[0, 0],
        tile_col[0, 0],
        tile_pattern[0, 0],
        tile_weight[0, 0],
        tile_count[0, 0],
        per_shard,
        core,
    )
    tile_cost = pl.CostEstimate(
        flops=2 * slots.shape[0] * edge * edge * feature_count,
        bytes_accessed=patterns.size * 2 + 4 * half * feature_count * 2,
        transcendentals=0,
    )

    scaled = pl.pallas_call(
        scale_kernel,
        out_shape=shape((chips, node_dev, feature_count), bf16),
        in_specs=[VMEM] * 2,
        out_specs=VMEM,
        compiler_params=PARAMS,
    )(features, degree_tiles)
    own_panel = across_chips(scaled).reshape(half, feature_count)
    other_panel = lax.ppermute(own_panel, "row", swap)
    row_part = pl.pallas_call(
        forward_kernel,
        out_shape=shape((col_devices * node_dev, feature_count), bf16),
        in_specs=[SMEM] * 2 + [VMEM] + [ANY] * 2,
        out_specs=VMEM,
        scratch_shapes=[
            pltpu.VMEM((2 * half, feature_count), bf16),
            pltpu.VMEM((col_devices * node_dev, feature_count), f32),
            pltpu.SemaphoreType.DMA((2,)),
        ],
        compiler_params=PARAMS,
        cost_estimate=tile_cost,
    )(tile_count, slots, patterns, own_panel, other_panel)
    parts = across_cols(row_part.reshape(col_devices, node_dev, feature_count))
    activations, spread = pl.pallas_call(
        middle_kernel,
        out_shape=(
            shape((node_dev, hidden), bf16),
            shape((col_devices, node_dev + extra, edge), bf16),
        ),
        in_specs=[VMEM] * 5,
        out_specs=(VMEM,) * 2,
        compiler_params=PARAMS,
    )(parts, degree_tiles, cotangent, weight, layer_bias[None, :])
    spread_all = across_cols(spread)
    keep, send = pl.pallas_call(
        backward_kernel,
        out_shape=(shape((half + extra, edge), f32), shape((half + extra, edge), bf16)),
        in_specs=[SMEM] * 2 + [VMEM] * 2,
        out_specs=(VMEM,) * 2,
        scratch_shapes=[pltpu.VMEM((2 * half, edge), f32)],
        compiler_params=PARAMS,
        cost_estimate=tile_cost,
    )(tile_count, slots, patterns, spread_all)
    got = lax.ppermute(send, "row", swap)
    joined = pl.pallas_call(
        join_kernel,
        out_shape=shape((chips, node_dev + extra, edge), bf16),
        in_specs=[VMEM] * 2,
        out_specs=VMEM,
        compiler_params=PARAMS,
    )(keep, got)
    back_parts = across_chips(joined)
    scale_factor = 1.0 / math.sqrt(node_dev * row_devices * col_devices)
    grad_features, finished, grad_bias = pl.pallas_call(
        functools.partial(last_kernel, scale_factor),
        out_shape=(
            shape((node_dev, feature_count), bf16),
            shape((col_devices, segment, edge), f32),
            shape((1, hidden), f32),
        ),
        in_specs=[VMEM] * 2,
        out_specs=(VMEM,) * 3,
        compiler_params=PARAMS,
    )(back_parts, degree_tiles)
    grad_weight = pl.pallas_call(
        lay_out_kernel,
        out_shape=shape((feature_count, hidden), f32),
        in_specs=[VMEM],
        out_specs=VMEM,
        compiler_params=PARAMS,
    )(across_cols(finished))
    return (activations, grad_features, grad_weight, grad_bias[0])


def solution(mesh):
    in_specs = (
        P(("row", "col"), None),
        P(("row", "col")),
        P(("row", "col"), None),
        P(),
        P(),
        P(),
        P("row", "col", None),
        P("row", "col", None),
        P("row", "col", None),
        P("row", "col", None),
        P("row", "col"),
    )
    out_specs = (P(("row", "col"), None), P(("row", "col"), None), P(), P())
    return jax.shard_map(
        per_device, mesh=mesh, in_specs=in_specs, out_specs=out_specs, check_vma=False
    )
```

```python
import functools
import math

import jax
import jax.numpy as jnp
from jax import lax
from jax.experimental import pallas as pl
from jax.experimental.pallas import tpu as pltpu
from jax.sharding import PartitionSpec as P

GROUP = 64
VMEM_LIMIT = 20 * 1024 * 1024
ROOT_2_PI = math.sqrt(2.0 / math.pi)
CUBIC = 0.044715
BIAS_ROWS = 16
ANY = pl.BlockSpec(memory_space=pl.ANY)
VMEM = pl.BlockSpec(memory_space=pltpu.VMEM)
SMEM = pl.BlockSpec(memory_space=pltpu.SMEM)
PARAMS = pltpu.CompilerParams(vmem_limit_bytes=VMEM_LIMIT)


def pack_slots(tile_row, tile_col, tile_pattern, tile_weight, live, per_shard, core):
    shard = tile_col // per_shard
    half = (shard % 2) ^ core
    place = (half * 8 + shard // 2) * per_shard + tile_col % per_shard
    slots = tile_col.shape[0]
    factor = jnp.where(jnp.arange(slots, dtype=jnp.int32) < live, tile_weight, 0)
    return place | (tile_row << 6) | (tile_pattern << 11) | (factor << 17)


def unpack_slot(word):
    return word & 63, (word >> 6) & 31, (word >> 11) & 63, (word >> 17).astype(jnp.float32)


def root_columns(degree):
    rows = lax.rsqrt(degree.astype(jnp.float32))
    rows = jnp.concatenate([rows, jnp.ones((8 - rows.shape[0], rows.shape[1]), jnp.float32)], 0)
    return rows.T


def scale_kernel(features_hbm, degree_hbm, out_ref, features_ref, degree_ref, sems):
    copies = (
        pltpu.make_async_copy(degree_hbm, degree_ref, sems.at[0]),
        pltpu.make_async_copy(features_hbm, features_ref, sems.at[1]),
    )
    for copy in copies:
        copy.start()
    copies[0].wait()
    roots = root_columns(degree_ref[...])
    copies[1].wait()
    edge = degree_ref.shape[1]
    for tile in range(degree_ref.shape[0]):
        rows = pl.ds(tile * edge, edge)
        scaled = features_ref[rows, :].astype(jnp.float32) * roots[:, tile : tile + 1]
        scaled = scaled.astype(jnp.bfloat16)
        for copy in range(out_ref.shape[0]):
            out_ref[copy, rows, :] = scaled


def forward_kernel(live_ref, slots_ref, patterns_ref, own_ref, other_ref, out_ref, panel, sums, sems):
    edge = patterns_ref.shape[1]
    half = own_ref.shape[0]
    copies = (
        pltpu.make_async_copy(own_ref, panel.at[pl.ds(0, half)], sems.at[0]),
        pltpu.make_async_copy(other_ref, panel.at[pl.ds(half, half)], sems.at[1]),
    )
    for copy in copies:
        copy.start()
    sums[...] = jnp.zeros_like(sums)
    for copy in copies:
        copy.wait()

    def one_group(group, carry):
        terms = []
        for member in range(GROUP):
            place, row, pattern, factor = unpack_slot(slots_ref[group * GROUP + member])
            block = panel[pl.ds(pl.multiple_of(place * edge, edge), edge), :]
            product = jnp.dot(patterns_ref[pattern], block, preferred_element_type=jnp.float32)
            terms.append((row, factor, product))
        for row, factor, product in terms:
            rows = pl.ds(pl.multiple_of(row * edge, edge), edge)
            sums[rows, :] += factor * product
        return carry

    lax.fori_loop(0, (live_ref[0, 0] + GROUP - 1) // GROUP, one_group, 0)
    out_ref[...] = sums[...].astype(jnp.bfloat16)


def backward_kernel(
    live_ref, slots_ref, patterns_ref, spread_ref, keep_ref, send_ref, grads_ref, sums
):
    edge = patterns_ref.shape[1]
    shards, rows_in_shard, _ = spread_ref.shape
    half = sums.shape[0] // 2
    own = rows_in_shard - grads_ref.shape[0]
    per_shard = own // edge
    sums[...] = jnp.zeros_like(sums)

    def one_group(group, carry):
        terms = []
        for member in range(GROUP):
            place, row, pattern, factor = unpack_slot(slots_ref[group * GROUP + member])
            start = pl.multiple_of((row % per_shard) * edge, edge)
            block = spread_ref[row // per_shard, pl.ds(start, edge), :]
            product = jnp.dot(block, patterns_ref[pattern], preferred_element_type=jnp.float32)
            terms.append((place, factor, product))
        for place, factor, product in terms:
            rows = pl.ds(pl.multiple_of(place * edge, edge), edge)
            sums[rows, :] += factor * product
        return carry

    lax.fori_loop(0, (live_ref[0, 0] + GROUP - 1) // GROUP, one_group, 0)
    keep_ref[...] = sums[:half, :]
    send_ref[...] = sums[half:, :].astype(jnp.bfloat16)
    grads = spread_ref[0, own:, :].astype(jnp.float32)
    for shard in range(1, shards):
        grads += spread_ref[shard, own:, :].astype(jnp.float32)
    grads_ref[...] = grads.astype(jnp.bfloat16)


def split_product(left, right, dims):
    high = left.astype(jnp.bfloat16)
    low = (left - high.astype(jnp.float32)).astype(jnp.bfloat16)
    return lax.dot_general(
        high, right, (dims, ((), ())), preferred_element_type=jnp.float32
    ) + lax.dot_general(low, right, (dims, ((), ())), preferred_element_type=jnp.float32)


def activate(pre_act):
    square = pre_act * pre_act
    bent = jnp.tanh(ROOT_2_PI * (pre_act + CUBIC * (pre_act * square)))
    return square, bent, 0.5 * (1.0 + bent)


def middle_kernel(
    core_ref,
    parts_ref,
    degree_ref,
    cotangent_ref,
    weight_ref,
    bias_ref,
    pre_ref,
    upstream_ref,
    keep_ref,
    send_ref,
):
    tiles, edge = degree_ref.shape
    shards = parts_ref.shape[0]
    weight = weight_ref[...]
    height = weight.shape[0]
    roots = root_columns(degree_ref[...])
    grads = jnp.zeros(weight.shape, jnp.float32)
    bias_row = jnp.zeros(bias_ref.shape, jnp.float32)
    for tile in range(tiles):
        rows = pl.ds(tile * edge, edge)
        sums = parts_ref[0, rows, :].astype(jnp.float32)
        for shard in range(1, shards):
            sums += parts_ref[shard, rows, :].astype(jnp.float32)
        inv_root = roots[:, tile : tile + 1]
        pre_act = inv_root * split_product(sums, weight, ((1,), (0,))) + bias_ref[...]
        pre_ref[rows, :] = pre_act
        square, bent, half = activate(pre_act)
        rise = 0.5 * pre_act * (1.0 - bent * bent) * (ROOT_2_PI * (1.0 + 3.0 * CUBIC * square))
        slope = cotangent_ref[rows, :].astype(jnp.float32) * (half + rise)
        upstream = (inv_root * slope).astype(jnp.bfloat16)
        upstream_ref[rows, :] = upstream
        grads += split_product(sums, upstream, ((0,), (0,)))
        bias_row += jnp.sum(slope, axis=0, keepdims=True)
    width = keep_ref.shape[1]
    bias_high = bias_row.astype(jnp.bfloat16).astype(jnp.float32)
    bias_low = bias_row - bias_high
    first = core_ref[0] == 0

    def put(target, left):
        pick = lambda whole: jnp.where(left, whole[:, :width], whole[:, width:])
        target[:height, :] = pick(grads).astype(target.dtype)
        row_ids = lax.broadcasted_iota(jnp.int32, (BIAS_ROWS, width), 0)
        block = jnp.where(row_ids == 0, pick(bias_high), 0.0)
        block = jnp.where(row_ids == 1, pick(bias_low), block)
        target[height:, :] = block.astype(target.dtype)

    put(keep_ref, first)
    put(send_ref, jnp.logical_not(first))


def activation_kernel(pre_ref, act_ref):
    pre_act = pre_ref[...]
    act_ref[...] = (pre_act * activate(pre_act)[2]).astype(jnp.bfloat16)


def spread_kernel(upstream_ref, weight_ref, out_ref):
    edge = out_ref.shape[2]
    for tile in range(upstream_ref.shape[0] // edge):
        rows = pl.ds(tile * edge, edge)
        spread = lax.dot_general(
            weight_ref[...],
            upstream_ref[rows, :],
            (((1,), (1,)), ((), ())),
            preferred_element_type=jnp.float32,
        ).astype(jnp.bfloat16)
        for shard in range(out_ref.shape[0]):
            out_ref[shard, rows, :] = spread


def append_kernel(keep_ref, got_ref, spread_ref, out_ref):
    terms = (keep_ref[...] + got_ref[...].astype(jnp.float32)).astype(jnp.bfloat16)
    rows = pl.ds(out_ref.shape[1] - terms.shape[0], terms.shape[0])
    for shard in range(out_ref.shape[0]):
        out_ref[shard, rows, :] = terms


def join_kernel(keep_ref, got_ref, grads_ref, out_ref):
    shards = out_ref.shape[0]
    own = keep_ref.shape[0] // shards
    for shard in range(shards):
        rows = pl.ds(shard * own, own)
        total = keep_ref[rows, :] + got_ref[rows, :].astype(jnp.float32)
        out_ref[shard, pl.ds(0, own), :] = total.astype(jnp.bfloat16)
        out_ref[shard, pl.ds(own, grads_ref.shape[0]), :] = grads_ref[...]


def total_kernel(scale_factor, parts_ref, half_ref):
    shards = parts_ref.shape[0]
    own = parts_ref.shape[1] - (half_ref.shape[0] - 8 + BIAS_ROWS)
    tail = parts_ref[0, own:, :].astype(jnp.float32)
    for shard in range(1, shards):
        tail += parts_ref[shard, own:, :].astype(jnp.float32)
    tail = tail * scale_factor
    height = half_ref.shape[0] - 8
    half_ref[:height, :] = tail[:height, :]
    bias_row = tail[height : height + 1, :] + tail[height + 1 : height + 2, :]
    half_ref[height:, :] = jnp.broadcast_to(bias_row, (8, bias_row.shape[1]))


def features_kernel(parts_ref, degree_ref, features_ref):
    tiles, edge = degree_ref.shape
    roots = lax.rsqrt(degree_ref[...].astype(jnp.float32))
    for tile in range(tiles):
        rows = pl.ds(tile * edge, edge)
        total = parts_ref[0, rows, :].astype(jnp.float32)
        for shard in range(1, parts_ref.shape[0]):
            total += parts_ref[shard, rows, :].astype(jnp.float32)
        features_ref[rows, :] = (total * roots[tile : tile + 1, :]).T.astype(jnp.bfloat16)


def lay_out_kernel(core_ref, mine_ref, other_ref, grads_ref, bias_ref):
    first = core_ref[0] == 0
    height = grads_ref.shape[0]
    width = mine_ref.shape[1]
    mine, other = mine_ref[...], other_ref[...]
    halves = (jnp.where(first, mine, other), jnp.where(first, other, mine))
    for index, half in enumerate(halves):
        lanes = pl.ds(index * width, width)
        grads_ref[:, lanes] = half[:height, :]
        bias_ref[:, lanes] = half[height : height + 1, :]


def per_device(
    features,
    degree,
    cotangent,
    weight,
    layer_bias,
    patterns,
    tile_row,
    tile_col,
    tile_pattern,
    tile_weight,
    tile_count,
):
    node_dev, feature_count = features.shape
    hidden = weight.shape[1]
    row_devices = lax.axis_size("row")
    col_devices = lax.axis_size("col")
    chips = row_devices // 2
    edge = patterns.shape[1]
    per_shard = node_dev // edge
    core = lax.axis_index("row") % 2
    same_core = [list(range(first, row_devices, 2)) for first in range(2)]
    swap = [(index, index ^ 1) for index in range(row_devices)]
    across_chips = functools.partial(
        lax.all_to_all,
        axis_name="row",
        split_axis=0,
        concat_axis=0,
        axis_index_groups=same_core,
    )
    across_cols = functools.partial(lax.all_to_all, axis_name="col", split_axis=0, concat_axis=0)
    extra = feature_count + BIAS_ROWS
    half = chips * node_dev
    bf16, f32 = jnp.bfloat16, jnp.float32
    shape = jax.ShapeDtypeStruct
    degree_tiles = degree.reshape(per_shard, edge)
    slots = pack_slots(
        tile_row[0, 0],
        tile_col[0, 0],
        tile_pattern[0, 0],
        tile_weight[0, 0],
        tile_count[0, 0],
        per_shard,
        core,
    )
    tile_cost = pl.CostEstimate(
        flops=2 * slots.shape[0] * edge * edge * feature_count,
        bytes_accessed=patterns.size * 2 + 4 * half * feature_count * 2,
        transcendentals=0,
    )

    scaled = pl.pallas_call(
        scale_kernel,
        out_shape=shape((chips, node_dev, feature_count), bf16),
        in_specs=[ANY] * 2,
        out_specs=VMEM,
        scratch_shapes=[
            pltpu.VMEM(features.shape, bf16),
            pltpu.VMEM(degree_tiles.shape, jnp.int32),
            pltpu.SemaphoreType.DMA((2,)),
        ],
        compiler_params=PARAMS,
    )(features, degree_tiles)
    own_panel = across_chips(scaled).reshape(half, feature_count)
    other_panel = lax.ppermute(own_panel, "row", swap)
    row_part = pl.pallas_call(
        forward_kernel,
        out_shape=shape((col_devices * node_dev, feature_count), bf16),
        in_specs=[SMEM] * 2 + [VMEM] + [ANY] * 2,
        out_specs=VMEM,
        scratch_shapes=[
            pltpu.VMEM((2 * half, feature_count), bf16),
            pltpu.VMEM((col_devices * node_dev, feature_count), f32),
            pltpu.SemaphoreType.DMA((2,)),
        ],
        compiler_params=PARAMS,
        cost_estimate=tile_cost,
    )(tile_count, slots, patterns, own_panel, other_panel)
    parts = across_cols(row_part.reshape(col_devices, node_dev, feature_count))
    core_word = core.astype(jnp.int32).reshape(1)
    pre_act, upstream, keep_terms, send_terms = pl.pallas_call(
        middle_kernel,
        out_shape=(
            shape((node_dev, hidden), f32),
            shape((node_dev, hidden), bf16),
            shape((extra, edge), f32),
            shape((extra, edge), bf16),
        ),
        in_specs=[SMEM] + [VMEM] * 5,
        out_specs=(VMEM,) * 4,
        compiler_params=PARAMS,
    )(core_word, parts, degree_tiles, cotangent, weight, layer_bias[None, :])
    got_terms = lax.ppermute(send_terms, "row", swap)
    spread = pl.pallas_call(
        spread_kernel,
        out_shape=shape((col_devices, node_dev + extra, edge), bf16),
        in_specs=[VMEM] * 2,
        out_specs=VMEM,
        compiler_params=PARAMS,
    )(upstream, weight)
    spread = pl.pallas_call(
        append_kernel,
        out_shape=shape(spread.shape, bf16),
        in_specs=[VMEM] * 3,
        out_specs=VMEM,
        input_output_aliases={2: 0},
        compiler_params=PARAMS,
    )(keep_terms, got_terms, spread)
    spread_all = across_cols(spread)
    keep, send, grads = pl.pallas_call(
        backward_kernel,
        out_shape=(
            shape((half, edge), f32),
            shape((half, edge), bf16),
            shape((extra, edge), bf16),
        ),
        in_specs=[SMEM] * 2 + [VMEM] * 2,
        out_specs=(VMEM,) * 3,
        scratch_shapes=[pltpu.VMEM((2 * half, edge), f32)],
        compiler_params=PARAMS,
        cost_estimate=tile_cost,
    )(tile_count, slots, patterns, spread_all)
    got = lax.ppermute(send, "row", swap)
    pre_act, keep = lax.optimization_barrier((pre_act, keep))
    activations = pl.pallas_call(
        activation_kernel,
        out_shape=shape((node_dev, hidden), bf16),
        in_specs=[VMEM],
        out_specs=VMEM,
        compiler_params=PARAMS,
    )(pre_act)
    got, activations = lax.optimization_barrier((got, activations))
    joined = pl.pallas_call(
        join_kernel,
        out_shape=shape((chips, node_dev + extra, edge), bf16),
        in_specs=[VMEM] * 3,
        out_specs=VMEM,
        compiler_params=PARAMS,
    )(keep, got, grads)
    back_parts = across_chips(joined)
    scale_factor = 1.0 / math.sqrt(node_dev * row_devices * col_devices)
    mine = pl.pallas_call(
        functools.partial(total_kernel, scale_factor),
        out_shape=shape((feature_count + 8, edge), f32),
        in_specs=[VMEM],
        out_specs=VMEM,
        compiler_params=PARAMS,
    )(back_parts)
    other = lax.ppermute(mine, "row", swap)
    grad_features = pl.pallas_call(
        features_kernel,
        out_shape=shape((node_dev, feature_count), bf16),
        in_specs=[VMEM] * 2,
        out_specs=VMEM,
        compiler_params=PARAMS,
    )(back_parts, degree_tiles)
    grad_weight, grad_bias = pl.pallas_call(
        lay_out_kernel,
        out_shape=(shape((feature_count, hidden), f32), shape((1, hidden), f32)),
        in_specs=[SMEM] + [VMEM] * 2,
        out_specs=(VMEM,) * 2,
        compiler_params=PARAMS,
    )(core_word, mine, other)
    return (activations, grad_features, grad_weight, grad_bias[0])


def solution(mesh):
    in_specs = (
        P(("row", "col"), None),
        P(("row", "col")),
        P(("row", "col"), None),
        P(),
        P(),
        P(),
        P("row", "col", None),
        P("row", "col", None),
        P("row", "col", None),
        P("row", "col", None),
        P("row", "col"),
    )
    out_specs = (P(("row", "col"), None), P(("row", "col"), None), P(), P())
    return jax.shard_map(
        per_device, mesh=mesh, in_specs=in_specs, out_specs=out_specs, check_vma=False
    )
```

```python
import functools
import math

import jax
import jax.numpy as jnp
from jax import lax
from jax.experimental import pallas as pl
from jax.experimental.pallas import tpu as pltpu
from jax.sharding import PartitionSpec as P

GROUP = 64
VMEM_LIMIT = 20 * 1024 * 1024
ROOT_2_PI = math.sqrt(2.0 / math.pi)
CUBIC = 0.044715
BIAS_ROWS = 16
PAIRS = (((0, 1), (2, 3)), ((0, 3), (1, 2)))
ANY = pl.BlockSpec(memory_space=pl.ANY)
VMEM = pl.BlockSpec(memory_space=pltpu.VMEM)
SMEM = pl.BlockSpec(memory_space=pltpu.SMEM)
PARAMS = pltpu.CompilerParams(vmem_limit_bytes=VMEM_LIMIT)


def pair_of(place, core):
    return jnp.where(core == 0, place >> 1, (place ^ (place >> 1)) & 1)


def pair_index(place, core):
    return jnp.where(core == 0, place & 1, place >> 1)


def far_neighbour(place, core):
    return place ^ 3 if core == 0 else place ^ 1


def pack_slots(tile_row, tile_col, tile_pattern, tile_weight, live, per_shard, row, col):
    core = row % 2
    shard = tile_col // per_shard
    parity = shard % 2
    chip = shard // 2
    tile = tile_col % per_shard
    half = parity ^ core
    forward = (half * 8 + chip) * per_shard + tile
    ring = chip % 4
    far = (pair_of(ring, parity) != pair_of((row // 2) % 4, parity)).astype(jnp.int32)
    rank = pair_index(ring, parity) * 2 + chip // 4
    target = ((half * 2 + far) * 4 + rank) * per_shard + tile
    peer = tile_row // per_shard
    far = (pair_of(peer // 2, core) != pair_of(col // 2, core)).astype(jnp.int32)
    rank = pair_index(peer // 2, core) * 2 + peer % 2
    source = (far * 4 + rank) * per_shard + tile_row % per_shard
    slots = tile_col.shape[0]
    factor = jnp.where(jnp.arange(slots, dtype=jnp.int32) < live, tile_weight, 0)
    return (
        forward
        | (tile_row << 6)
        | (tile_pattern << 11)
        | (factor << 17)
        | (target << 20)
        | (source << 26)
    )


def root_columns(degree):
    rows = lax.rsqrt(degree.astype(jnp.float32))
    rows = jnp.concatenate([rows, jnp.ones((8 - rows.shape[0], rows.shape[1]), jnp.float32)], 0)
    return rows.T


def scale_kernel(features_hbm, degree_hbm, out_ref, features_ref, degree_ref, sems):
    copies = (
        pltpu.make_async_copy(degree_hbm, degree_ref, sems.at[0]),
        pltpu.make_async_copy(features_hbm, features_ref, sems.at[1]),
    )
    for copy in copies:
        copy.start()
    copies[0].wait()
    roots = root_columns(degree_ref[...])
    copies[1].wait()
    edge = degree_ref.shape[1]
    for tile in range(degree_ref.shape[0]):
        rows = pl.ds(tile * edge, edge)
        scaled = features_ref[rows, :].astype(jnp.float32) * roots[:, tile : tile + 1]
        scaled = scaled.astype(jnp.bfloat16)
        for copy in range(out_ref.shape[0]):
            out_ref[copy, rows, :] = scaled


def forward_kernel(live_ref, slots_ref, patterns_ref, own_ref, other_ref, out_ref, panel, sums):
    edge = patterns_ref.shape[1]
    half = own_ref.shape[0]
    panel[:half, :] = own_ref[...]
    panel[half:, :] = other_ref[...]
    sums[...] = jnp.zeros_like(sums)

    def one_group(group, carry):
        terms = []
        for member in range(GROUP):
            word = slots_ref[group * GROUP + member]
            place, row, pattern = word & 63, (word >> 6) & 31, (word >> 11) & 63
            factor = ((word >> 17) & 7).astype(jnp.float32)
            block = panel[pl.ds(pl.multiple_of(place * edge, edge), edge), :]
            product = jnp.dot(patterns_ref[pattern], block, preferred_element_type=jnp.float32)
            terms.append((row, factor, product))
        for row, factor, product in terms:
            rows = pl.ds(pl.multiple_of(row * edge, edge), edge)
            sums[rows, :] += factor * product
        return carry

    lax.fori_loop(0, (live_ref[0, 0] + GROUP - 1) // GROUP, one_group, 0)
    out_ref[...] = sums[...].astype(jnp.bfloat16)


def backward_kernel(
    live_ref,
    slots_ref,
    patterns_ref,
    near_ref,
    far_ref,
    keep_ref,
    send_ref,
    grads_ref,
    panel,
    sums,
):
    edge = patterns_ref.shape[1]
    half = keep_ref.shape[0]
    part = panel.shape[0] // 2
    panel[:part, :] = near_ref[:part, :]
    panel[part:, :] = far_ref[:part, :]
    sums[...] = jnp.zeros_like(sums)

    def one_group(group, carry):
        terms = []
        for member in range(GROUP):
            word = slots_ref[group * GROUP + member]
            pattern, target, source = (word >> 11) & 63, (word >> 20) & 63, (word >> 26) & 31
            factor = ((word >> 17) & 7).astype(jnp.float32)
            block = panel[pl.ds(pl.multiple_of(source * edge, edge), edge), :]
            product = jnp.dot(block, patterns_ref[pattern], preferred_element_type=jnp.float32)
            terms.append((target, factor, product))
        for target, factor, product in terms:
            rows = pl.ds(pl.multiple_of(target * edge, edge), edge)
            sums[rows, :] += factor * product
        return carry

    lax.fori_loop(0, (live_ref[0, 0] + GROUP - 1) // GROUP, one_group, 0)
    keep_ref[...] = sums[:half, :]
    send_ref[...] = sums[half:, :].astype(jnp.bfloat16)
    grads = near_ref[part:, :].astype(jnp.float32) + far_ref[part:, :].astype(jnp.float32)
    grads_ref[...] = grads.astype(jnp.bfloat16)


def split_product(left, right, dims):
    high = left.astype(jnp.bfloat16)
    low = (left - high.astype(jnp.float32)).astype(jnp.bfloat16)
    return lax.dot_general(
        high, right, (dims, ((), ())), preferred_element_type=jnp.float32
    ) + lax.dot_general(low, right, (dims, ((), ())), preferred_element_type=jnp.float32)


def activate(pre_act):
    square = pre_act * pre_act
    bent = jnp.tanh(ROOT_2_PI * (pre_act + CUBIC * (pre_act * square)))
    return square, bent, 0.5 * (1.0 + bent)


def middle_kernel(
    core_ref,
    parts_ref,
    degree_ref,
    cotangent_ref,
    weight_ref,
    bias_ref,
    pre_ref,
    upstream_ref,
    keep_ref,
    send_ref,
):
    tiles, edge = degree_ref.shape
    shards = parts_ref.shape[0]
    weight = weight_ref[...]
    height = weight.shape[0]
    roots = root_columns(degree_ref[...])
    grads = jnp.zeros(weight.shape, jnp.float32)
    bias_row = jnp.zeros(bias_ref.shape, jnp.float32)
    for tile in range(tiles):
        rows = pl.ds(tile * edge, edge)
        sums = parts_ref[0, rows, :].astype(jnp.float32)
        for shard in range(1, shards):
            sums += parts_ref[shard, rows, :].astype(jnp.float32)
        inv_root = roots[:, tile : tile + 1]
        pre_act = inv_root * split_product(sums, weight, ((1,), (0,))) + bias_ref[...]
        pre_ref[rows, :] = pre_act
        square, bent, half = activate(pre_act)
        rise = 0.5 * pre_act * (1.0 - bent * bent) * (ROOT_2_PI * (1.0 + 3.0 * CUBIC * square))
        slope = cotangent_ref[rows, :].astype(jnp.float32) * (half + rise)
        upstream = (inv_root * slope).astype(jnp.bfloat16)
        upstream_ref[rows, :] = upstream
        grads += split_product(sums, upstream, ((0,), (0,)))
        bias_row += jnp.sum(slope, axis=0, keepdims=True)
    width = keep_ref.shape[1]
    bias_high = bias_row.astype(jnp.bfloat16).astype(jnp.float32)
    bias_low = bias_row - bias_high
    first = core_ref[0] == 0

    def put(target, left):
        pick = lambda whole: jnp.where(left, whole[:, :width], whole[:, width:])
        target[:height, :] = pick(grads).astype(target.dtype)
        row_ids = lax.broadcasted_iota(jnp.int32, (BIAS_ROWS, width), 0)
        block = jnp.where(row_ids == 0, pick(bias_high), 0.0)
        block = jnp.where(row_ids == 1, pick(bias_low), block)
        target[height:, :] = block.astype(target.dtype)

    put(keep_ref, first)
    put(send_ref, jnp.logical_not(first))


def activation_kernel(pre_ref, act_ref):
    pre_act = pre_ref[...]
    act_ref[...] = (pre_act * activate(pre_act)[2]).astype(jnp.bfloat16)


def spread_kernel(upstream_ref, weight_ref, out_ref):
    edge = out_ref.shape[2]
    for tile in range(upstream_ref.shape[0] // edge):
        rows = pl.ds(tile * edge, edge)
        spread = lax.dot_general(
            weight_ref[...],
            upstream_ref[rows, :],
            (((1,), (1,)), ((), ())),
            preferred_element_type=jnp.float32,
        ).astype(jnp.bfloat16)
        for shard in range(out_ref.shape[0]):
            out_ref[shard, rows, :] = spread


def append_kernel(keep_ref, got_ref, spread_ref, out_ref):
    terms = (keep_ref[...] + got_ref[...].astype(jnp.float32)).astype(jnp.bfloat16)
    rows = pl.ds(out_ref.shape[1] - terms.shape[0], terms.shape[0])
    for shard in range(out_ref.shape[0]):
        out_ref[shard, rows, :] = terms


def sum_of_four(parts_ref, rows):
    part = lambda index: parts_ref[index, rows, :].astype(jnp.float32)
    return (part(0) + part(2)) + (part(1) + part(3))


def gather_kernel(parts_ref, out_ref):
    shards, rows_in_shard, _ = parts_ref.shape
    extra = (shards * rows_in_shard - out_ref.shape[0]) // (shards - 1)
    own = rows_in_shard - extra
    for shard in range(shards):
        out_ref[pl.ds(shard * own, own), :] = parts_ref[shard, :own, :]
    out_ref[shards * own :, :] = sum_of_four(parts_ref, pl.ds(own, extra)).astype(jnp.bfloat16)


def split_kernel(keep_ref, got_ref, grads_ref, near_ref, far_ref):
    half = near_ref.shape[0]
    near_ref[...] = keep_ref[:half, :] + got_ref[:half, :].astype(jnp.float32)
    far = keep_ref[half:, :] + got_ref[half:, :].astype(jnp.float32)
    far_ref[:half, :] = far.astype(jnp.bfloat16)
    far_ref[half:, :] = grads_ref[...]


def join_kernel(near_ref, got_ref, grads_ref, out_ref):
    shards = out_ref.shape[0]
    half = near_ref.shape[0]
    own = half // shards
    grads = grads_ref[...].astype(jnp.float32) + got_ref[half:, :].astype(jnp.float32)
    grads = grads.astype(jnp.bfloat16)
    for shard in range(shards):
        rows = pl.ds(shard * own, own)
        total = near_ref[rows, :] + got_ref[rows, :].astype(jnp.float32)
        out_ref[shard, pl.ds(0, own), :] = total.astype(jnp.bfloat16)
        out_ref[shard, pl.ds(own, grads.shape[0]), :] = grads


def total_kernel(scale_factor, parts_ref, half_ref):
    extra = half_ref.shape[0] - 8 + BIAS_ROWS
    tail = sum_of_four(parts_ref, pl.ds(parts_ref.shape[1] - extra, extra))
    tail = tail * scale_factor
    height = half_ref.shape[0] - 8
    half_ref[:height, :] = tail[:height, :]
    bias_row = tail[height : height + 1, :] + tail[height + 1 : height + 2, :]
    half_ref[height:, :] = jnp.broadcast_to(bias_row, (8, bias_row.shape[1]))


def features_kernel(parts_ref, degree_ref, features_ref):
    tiles, edge = degree_ref.shape
    roots = lax.rsqrt(degree_ref[...].astype(jnp.float32))
    for tile in range(tiles):
        rows = pl.ds(tile * edge, edge)
        total = sum_of_four(parts_ref, rows)
        features_ref[rows, :] = (total * roots[tile : tile + 1, :]).T.astype(jnp.bfloat16)


def lay_out_kernel(core_ref, mine_ref, other_ref, grads_ref, bias_ref):
    first = core_ref[0] == 0
    height = grads_ref.shape[0]
    width = mine_ref.shape[1]
    mine, other = mine_ref[...], other_ref[...]
    halves = (jnp.where(first, mine, other), jnp.where(first, other, mine))
    for index, half in enumerate(halves):
        lanes = pl.ds(index * width, width)
        grads_ref[:, lanes] = half[:height, :]
        bias_ref[:, lanes] = half[height : height + 1, :]


def per_device(
    features,
    degree,
    cotangent,
    weight,
    layer_bias,
    patterns,
    tile_row,
    tile_col,
    tile_pattern,
    tile_weight,
    tile_count,
):
    node_dev, feature_count = features.shape
    hidden = weight.shape[1]
    row_devices = lax.axis_size("row")
    col_devices = lax.axis_size("col")
    chips = row_devices // 2
    edge = patterns.shape[1]
    per_shard = node_dev // edge
    row, col = lax.axis_index("row"), lax.axis_index("col")
    core = row % 2
    same_core = [list(range(first, row_devices, 2)) for first in range(2)]
    swap = [(index, index ^ 1) for index in range(row_devices)]
    row_near = [
        [(low * 4 + ring) * 2 + core_index for ring in pair for low in range(2)]
        for core_index in range(2)
        for pair in PAIRS[core_index]
    ]
    row_far = [
        (index, (index // 8 * 4 + far_neighbour(index // 2 % 4, index % 2)) * 2 + index % 2)
        for index in range(row_devices)
    ]
    col_near = [
        [index * col_devices + ring * 2 + high for ring in pair for high in range(2)]
        for index in range(row_devices)
        for pair in PAIRS[index % 2]
    ]
    col_far = [
        (
            index * col_devices + place,
            index * col_devices + far_neighbour(place // 2, index % 2) * 2 + place % 2,
        )
        for index in range(row_devices)
        for place in range(col_devices)
    ]
    exchange = functools.partial(lax.all_to_all, split_axis=0, concat_axis=0)
    both = ("row", "col")
    extra = feature_count + BIAS_ROWS
    half = chips * node_dev
    bf16, f32 = jnp.bfloat16, jnp.float32
    shape = jax.ShapeDtypeStruct
    degree_tiles = degree.reshape(per_shard, edge)
    slots = pack_slots(
        tile_row[0, 0],
        tile_col[0, 0],
        tile_pattern[0, 0],
        tile_weight[0, 0],
        tile_count[0, 0],
        per_shard,
        row,
        col,
    )
    tile_cost = pl.CostEstimate(
        flops=2 * slots.shape[0] * edge * edge * feature_count,
        bytes_accessed=patterns.size * 2 + 4 * half * feature_count * 2,
        transcendentals=0,
    )

    scaled = pl.pallas_call(
        scale_kernel,
        out_shape=shape((chips, node_dev, feature_count), bf16),
        in_specs=[ANY] * 2,
        out_specs=VMEM,
        scratch_shapes=[
            pltpu.VMEM(features.shape, bf16),
            pltpu.VMEM(degree_tiles.shape, jnp.int32),
            pltpu.SemaphoreType.DMA((2,)),
        ],
        compiler_params=PARAMS,
    )(features, degree_tiles)
    own_panel = exchange(scaled, "row", axis_index_groups=same_core).reshape(half, feature_count)
    other_panel = lax.ppermute(own_panel, "row", swap)
    row_part = pl.pallas_call(
        forward_kernel,
        out_shape=shape((col_devices * node_dev, feature_count), bf16),
        in_specs=[SMEM] * 2 + [VMEM] * 3,
        out_specs=VMEM,
        scratch_shapes=[
            pltpu.VMEM((2 * half, feature_count), bf16),
            pltpu.VMEM((col_devices * node_dev, feature_count), f32),
        ],
        compiler_params=PARAMS,
        cost_estimate=tile_cost,
    )(tile_count, slots, patterns, own_panel, other_panel)
    parts = exchange(row_part.reshape(col_devices, node_dev, feature_count), "col")
    core_word = core.astype(jnp.int32).reshape(1)
    pre_act, upstream, keep_terms, send_terms = pl.pallas_call(
        middle_kernel,
        out_shape=(
            shape((node_dev, hidden), f32),
            shape((node_dev, hidden), bf16),
            shape((extra, edge), f32),
            shape((extra, edge), bf16),
        ),
        in_specs=[SMEM] + [VMEM] * 5,
        out_specs=(VMEM,) * 4,
        compiler_params=PARAMS,
    )(core_word, parts, degree_tiles, cotangent, weight, layer_bias[None, :])
    got_terms = lax.ppermute(send_terms, "row", swap)
    spread = pl.pallas_call(
        spread_kernel,
        out_shape=shape((4, node_dev + extra, edge), bf16),
        in_specs=[VMEM] * 2,
        out_specs=VMEM,
        compiler_params=PARAMS,
    )(upstream, weight)
    spread = pl.pallas_call(
        append_kernel,
        out_shape=shape(spread.shape, bf16),
        in_specs=[VMEM] * 3,
        out_specs=VMEM,
        input_output_aliases={2: 0},
        compiler_params=PARAMS,
    )(keep_terms, got_terms, spread)
    near = pl.pallas_call(
        gather_kernel,
        out_shape=shape((4 * node_dev + extra, edge), bf16),
        in_specs=[VMEM],
        out_specs=VMEM,
        compiler_params=PARAMS,
    )(exchange(spread, both, axis_index_groups=col_near))
    pre_act, near = lax.optimization_barrier((pre_act, near))
    far = lax.ppermute(near, both, col_far)
    activations = pl.pallas_call(
        activation_kernel,
        out_shape=shape((node_dev, hidden), bf16),
        in_specs=[VMEM],
        out_specs=VMEM,
        compiler_params=PARAMS,
    )(pre_act)
    far, activations = lax.optimization_barrier((far, activations))
    keep, send, grads = pl.pallas_call(
        backward_kernel,
        out_shape=(
            shape((half, edge), f32),
            shape((half, edge), bf16),
            shape((extra, edge), bf16),
        ),
        in_specs=[SMEM] * 2 + [VMEM] * 3,
        out_specs=(VMEM,) * 3,
        scratch_shapes=[
            pltpu.VMEM((col_devices * node_dev, edge), bf16),
            pltpu.VMEM((2 * half, edge), f32),
        ],
        compiler_params=PARAMS,
        cost_estimate=tile_cost,
    )(tile_count, slots, patterns, near, far)
    got = lax.ppermute(send, "row", swap)
    near_sums, far_sums = pl.pallas_call(
        split_kernel,
        out_shape=(shape((half // 2, edge), f32), shape((half // 2 + extra, edge), bf16)),
        in_specs=[VMEM] * 3,
        out_specs=(VMEM,) * 2,
        compiler_params=PARAMS,
    )(keep, got, grads)
    joined = pl.pallas_call(
        join_kernel,
        out_shape=shape((4, node_dev + extra, edge), bf16),
        in_specs=[VMEM] * 3,
        out_specs=VMEM,
        compiler_params=PARAMS,
    )(near_sums, lax.ppermute(far_sums, "row", row_far), grads)
    back_parts = exchange(joined, "row", axis_index_groups=row_near)
    scale_factor = 1.0 / math.sqrt(node_dev * row_devices * col_devices)
    mine = pl.pallas_call(
        functools.partial(total_kernel, scale_factor),
        out_shape=shape((feature_count + 8, edge), f32),
        in_specs=[VMEM],
        out_specs=VMEM,
        compiler_params=PARAMS,
    )(back_parts)
    other = lax.ppermute(mine, "row", swap)
    grad_features = pl.pallas_call(
        features_kernel,
        out_shape=shape((node_dev, feature_count), bf16),
        in_specs=[VMEM] * 2,
        out_specs=VMEM,
        compiler_params=PARAMS,
    )(back_parts, degree_tiles)
    grad_weight, grad_bias = pl.pallas_call(
        lay_out_kernel,
        out_shape=(shape((feature_count, hidden), f32), shape((1, hidden), f32)),
        in_specs=[SMEM] + [VMEM] * 2,
        out_specs=(VMEM,) * 2,
        compiler_params=PARAMS,
    )(core_word, mine, other)
    return (activations, grad_features, grad_weight, grad_bias[0])


def solution(mesh):
    in_specs = (
        P(("row", "col"), None),
        P(("row", "col")),
        P(("row", "col"), None),
        P(),
        P(),
        P(),
        P("row", "col", None),
        P("row", "col", None),
        P("row", "col", None),
        P("row", "col", None),
        P("row", "col"),
    )
    out_specs = (P(("row", "col"), None), P(("row", "col"), None), P(), P())
    return jax.shard_map(
        per_device, mesh=mesh, in_specs=in_specs, out_specs=out_specs, check_vma=False
    )
```

```python
import functools
import math

import jax
import jax.numpy as jnp
from jax import lax
from jax.experimental import pallas as pl
from jax.experimental.pallas import tpu as pltpu
from jax.sharding import PartitionSpec as P

GROUP = 64
VMEM_LIMIT = 20 * 1024 * 1024
ROOT_2_PI = math.sqrt(2.0 / math.pi)
CUBIC = 0.044715
BIAS_ROWS = 16
PER_SHARD = 4
ORDERED = 640
BOUNDS = 600
PAIRS = (((0, 1), (2, 3)), ((0, 3), (1, 2)))
ANY = pl.BlockSpec(memory_space=pl.ANY)
VMEM = pl.BlockSpec(memory_space=pltpu.VMEM)
SMEM = pl.BlockSpec(memory_space=pltpu.SMEM)
PARAMS = pltpu.CompilerParams(vmem_limit_bytes=VMEM_LIMIT)


def pair_of(place, core):
    return jnp.where(core == 0, place >> 1, (place ^ (place >> 1)) & 1)


def pair_index(place, core):
    return jnp.where(core == 0, place & 1, place >> 1)


def far_neighbour(place, core):
    return place ^ 3 if core == 0 else place ^ 1


def order_kernel(place_ref, live_ref, row_ref, col_ref, pattern_ref, weight_ref, out_ref):
    row, col = place_ref[0], place_ref[1]
    core = row % 2
    per_shard = PER_SHARD
    rows, edge = row_ref.shape
    tile_col, tile_row = col_ref[...], row_ref[...]
    shard = tile_col // per_shard
    parity = shard % 2
    chip = shard // 2
    ring = chip % 4
    column_far = (pair_of(ring, parity) != pair_of((row // 2) % 4, parity)).astype(jnp.int32)
    rank = pair_index(ring, parity) * 2 + chip // 4
    column = (((parity ^ core) * 2 + column_far) * 4 + rank) * per_shard + tile_col % per_shard
    peer = tile_row // per_shard
    row_far = (pair_of(peer // 2, core) != pair_of(col // 2, core)).astype(jnp.int32)
    rank = pair_index(peer // 2, core) * 2 + peer % 2
    source = (row_far * 4 + rank) * per_shard + tile_row % per_shard
    word = tile_row | (pattern_ref[...] << 5) | (weight_ref[...] << 11) | (column << 14) | (source << 20)
    slot = lax.broadcasted_iota(jnp.int32, (rows, edge), 0) * edge
    slot += lax.broadcasted_iota(jnp.int32, (rows, edge), 1)
    alive = slot < live_ref[0, 0]
    word = jnp.where(alive, word, 0)
    kind = jnp.where(alive, column_far * 2 + row_far, 4)

    flags = [(kind == index).astype(jnp.float32) for index in range(5)]
    stacked = jnp.concatenate(flags + [jnp.zeros((4, edge), jnp.float32)], 0)
    before = lax.broadcasted_iota(jnp.int32, (edge, edge), 0) < lax.broadcasted_iota(
        jnp.int32, (edge, edge), 1
    )
    earlier = jnp.dot(
        stacked.astype(jnp.bfloat16),
        before.astype(jnp.float32).astype(jnp.bfloat16),
        preferred_element_type=jnp.float32,
    )
    counts = jnp.sum(stacked, axis=1, keepdims=True)
    start = jnp.zeros((1, 1), jnp.float32)
    ends = []
    position = [jnp.zeros((1, edge), jnp.float32) for _ in range(rows)]
    for index in range(5):
        for line in range(rows):
            at = index * rows + line
            position[line] += flags[index][line : line + 1] * (start + earlier[at : at + 1])
            start = start + counts[at : at + 1]
        ends.append(start)
    turned = jnp.concatenate(position + [jnp.zeros((8 - rows, edge), jnp.float32)], 0).T
    slots = rows * edge
    lanes = lax.broadcasted_iota(jnp.int32, (edge, slots), 1).astype(jnp.float32)
    pieces = jnp.zeros((8, slots), jnp.float32)
    for line in range(rows):
        chosen = (turned[:, line : line + 1] == lanes).astype(jnp.float32).astype(jnp.bfloat16)
        parts = [(word[line : line + 1] >> shift) & 127 for shift in (0, 7, 14, 21)]
        parts = jnp.concatenate(parts + [jnp.zeros((4, edge), jnp.int32)], 0)
        parts = parts.astype(jnp.float32).astype(jnp.bfloat16)
        pieces += jnp.dot(parts, chosen, preferred_element_type=jnp.float32)
    pieces = pieces.astype(jnp.int32)
    out_ref[:, :slots] = (
        pieces[0:1] | (pieces[1:2] << 7) | (pieces[2:3] << 14) | (pieces[3:4] << 21)
    )
    lane = lax.broadcasted_iota(jnp.int32, (1, out_ref.shape[1] - slots), 1) + slots
    tail = jnp.zeros(lane.shape, jnp.int32)
    for index in range(4):
        tail = jnp.where(lane == BOUNDS + index, ends[index].astype(jnp.int32), tail)
    out_ref[:, slots:] = tail


def add_products(slots_ref, runs, product_of, place_of, sums):
    edge = sums.shape[1]
    (first, end), (first_b, end_b) = runs
    turns = (end - first + GROUP - 1) // GROUP
    turns_b = (end_b - first_b + GROUP - 1) // GROUP

    def one_group(turn, carry):
        is_a = turn < turns
        start = jnp.where(is_a, first + turn * GROUP, first_b + (turn - turns) * GROUP)
        stop = jnp.where(is_a, end, end_b)
        terms = []
        for member in range(GROUP):
            slot = start + member
            word = slots_ref[0, slot]
            factor = jnp.where(slot < stop, (word >> 11) & 7, 0).astype(jnp.float32)
            terms.append((place_of(word), factor, product_of(word)))
        for place, factor, product in terms:
            rows = pl.ds(pl.multiple_of(place * edge, edge), edge)
            sums[rows, :] += factor * product
        return carry

    lax.fori_loop(0, turns + turns_b, one_group, 0)


def tile_of(ref, place, edge):
    return ref[pl.ds(pl.multiple_of(place * edge, edge), edge), :]


def class_bounds(slots_ref):
    return [0] + [slots_ref[0, BOUNDS + index] for index in range(4)]


def root_columns(degree):
    rows = lax.rsqrt(degree.astype(jnp.float32))
    rows = jnp.concatenate([rows, jnp.ones((8 - rows.shape[0], rows.shape[1]), jnp.float32)], 0)
    return rows.T


def scale_kernel(features_hbm, degree_hbm, out_ref, features_ref, degree_ref, sems):
    copies = (
        pltpu.make_async_copy(degree_hbm, degree_ref, sems.at[0]),
        pltpu.make_async_copy(features_hbm, features_ref, sems.at[1]),
    )
    for copy in copies:
        copy.start()
    copies[0].wait()
    roots = root_columns(degree_ref[...])
    copies[1].wait()
    edge = degree_ref.shape[1]
    for tile in range(degree_ref.shape[0]):
        rows = pl.ds(tile * edge, edge)
        scaled = features_ref[rows, :].astype(jnp.float32) * roots[:, tile : tile + 1]
        scaled = scaled.astype(jnp.bfloat16)
        for copy in range(out_ref.shape[0]):
            out_ref[copy, rows, :] = scaled


def forward_sums(slots_ref, patterns_ref, own_ref, other_ref, panel, sums, far):
    edge = patterns_ref.shape[1]
    half = own_ref.shape[0]
    panel[:half, :] = own_ref[...]
    panel[half:, :] = other_ref[...]
    bounds = class_bounds(slots_ref)

    def product_of(word):
        place = ((word >> 15) & 16) | ((word >> 14) & 15)
        return jnp.dot(
            patterns_ref[(word >> 5) & 63],
            tile_of(panel, place, edge),
            preferred_element_type=jnp.float32,
        )

    run = (bounds[2], bounds[4]) if far else (bounds[0], bounds[2])
    add_products(slots_ref, (run, (0, 0)), product_of, lambda word: word & 31, sums)


def forward_near_kernel(slots_ref, patterns_ref, own_ref, other_ref, out_ref, panel):
    out_ref[...] = jnp.zeros_like(out_ref)
    forward_sums(slots_ref, patterns_ref, own_ref, other_ref, panel, out_ref, False)


def forward_far_kernel(slots_ref, patterns_ref, own_ref, other_ref, so_far_ref, out_ref, panel, sums):
    sums[...] = so_far_ref[...]
    forward_sums(slots_ref, patterns_ref, own_ref, other_ref, panel, sums, True)
    out_ref[...] = sums[...].astype(jnp.bfloat16)


def backward_sums(slots_ref, patterns_ref, panel_ref, sums, far):
    edge = patterns_ref.shape[1]
    bounds = class_bounds(slots_ref)

    def product_of(word):
        return jnp.dot(
            tile_of(panel_ref, (word >> 20) & 15, edge),
            patterns_ref[(word >> 5) & 63],
            preferred_element_type=jnp.float32,
        )

    runs = [(bounds[index], bounds[index + 1]) for index in ((1, 3) if far else (0, 2))]
    add_products(slots_ref, runs, product_of, lambda word: (word >> 14) & 63, sums)


def backward_near_kernel(slots_ref, patterns_ref, near_ref, out_ref):
    out_ref[...] = jnp.zeros_like(out_ref)
    backward_sums(slots_ref, patterns_ref, near_ref, out_ref, False)


def backward_far_kernel(
    slots_ref, patterns_ref, near_ref, far_ref, so_far_ref, keep_ref, send_ref, grads_ref, sums
):
    half = keep_ref.shape[0]
    part = near_ref.shape[0] - grads_ref.shape[0]
    sums[...] = so_far_ref[...]
    backward_sums(slots_ref, patterns_ref, far_ref, sums, True)
    keep_ref[...] = sums[:half, :]
    send_ref[...] = sums[half:, :].astype(jnp.bfloat16)
    grads = near_ref[part:, :].astype(jnp.float32) + far_ref[part:, :].astype(jnp.float32)
    grads_ref[...] = grads.astype(jnp.bfloat16)


def split_product(left, right, dims):
    high = left.astype(jnp.bfloat16)
    low = (left - high.astype(jnp.float32)).astype(jnp.bfloat16)
    return lax.dot_general(
        high, right, (dims, ((), ())), preferred_element_type=jnp.float32
    ) + lax.dot_general(low, right, (dims, ((), ())), preferred_element_type=jnp.float32)


def activate(pre_act):
    square = pre_act * pre_act
    bent = jnp.tanh(ROOT_2_PI * (pre_act + CUBIC * (pre_act * square)))
    return square, bent, 0.5 * (1.0 + bent)


def middle_kernel(
    core_ref,
    parts_ref,
    degree_ref,
    cotangent_ref,
    weight_ref,
    bias_ref,
    pre_ref,
    upstream_ref,
    keep_ref,
    send_ref,
):
    tiles, edge = degree_ref.shape
    shards = parts_ref.shape[0]
    weight = weight_ref[...]
    height = weight.shape[0]
    roots = root_columns(degree_ref[...])
    grads = jnp.zeros(weight.shape, jnp.float32)
    bias_row = jnp.zeros(bias_ref.shape, jnp.float32)
    for tile in range(tiles):
        rows = pl.ds(tile * edge, edge)
        sums = parts_ref[0, rows, :].astype(jnp.float32)
        for shard in range(1, shards):
            sums += parts_ref[shard, rows, :].astype(jnp.float32)
        inv_root = roots[:, tile : tile + 1]
        pre_act = inv_root * split_product(sums, weight, ((1,), (0,))) + bias_ref[...]
        pre_ref[rows, :] = pre_act
        square, bent, half = activate(pre_act)
        rise = 0.5 * pre_act * (1.0 - bent * bent) * (ROOT_2_PI * (1.0 + 3.0 * CUBIC * square))
        slope = cotangent_ref[rows, :].astype(jnp.float32) * (half + rise)
        upstream = inv_root * slope
        upstream_ref[rows, :] = upstream
        grads += split_product(sums, upstream.astype(jnp.bfloat16), ((0,), (0,)))
        bias_row += jnp.sum(slope, axis=0, keepdims=True)
    width = keep_ref.shape[1]
    bias_high = bias_row.astype(jnp.bfloat16).astype(jnp.float32)
    bias_low = bias_row - bias_high
    first = core_ref[0] == 0

    def put(target, left):
        pick = lambda whole: jnp.where(left, whole[:, :width], whole[:, width:])
        target[:height, :] = pick(grads).astype(target.dtype)
        row_ids = lax.broadcasted_iota(jnp.int32, (BIAS_ROWS, width), 0)
        block = jnp.where(row_ids == 0, pick(bias_high), 0.0)
        block = jnp.where(row_ids == 1, pick(bias_low), block)
        target[height:, :] = block.astype(target.dtype)

    put(keep_ref, first)
    put(send_ref, jnp.logical_not(first))


def activation_kernel(pre_ref, act_ref):
    pre_act = pre_ref[...]
    act_ref[...] = (pre_act * activate(pre_act)[2]).astype(jnp.bfloat16)


def spread_kernel(upstream_ref, weight_ref, out_ref):
    edge = out_ref.shape[2]
    for tile in range(upstream_ref.shape[0] // edge):
        rows = pl.ds(tile * edge, edge)
        upstream = upstream_ref[rows, :]
        high = upstream.astype(jnp.bfloat16)
        low = (upstream - high.astype(jnp.float32)).astype(jnp.bfloat16)
        spread = sum(
            lax.dot_general(
                weight_ref[...], part, (((1,), (1,)), ((), ())), preferred_element_type=jnp.float32
            )
            for part in (high, low)
        ).astype(jnp.bfloat16)
        for shard in range(out_ref.shape[0]):
            out_ref[shard, rows, :] = spread


def append_kernel(keep_ref, got_ref, spread_ref, out_ref):
    terms = (keep_ref[...] + got_ref[...].astype(jnp.float32)).astype(jnp.bfloat16)
    rows = pl.ds(out_ref.shape[1] - terms.shape[0], terms.shape[0])
    for shard in range(out_ref.shape[0]):
        out_ref[shard, rows, :] = terms


def sum_of_four(parts_ref, rows):
    part = lambda index: parts_ref[index, rows, :].astype(jnp.float32)
    return (part(0) + part(2)) + (part(1) + part(3))


def gather_kernel(parts_ref, out_ref):
    shards, rows_in_shard, _ = parts_ref.shape
    extra = (shards * rows_in_shard - out_ref.shape[0]) // (shards - 1)
    own = rows_in_shard - extra
    for shard in range(shards):
        out_ref[pl.ds(shard * own, own), :] = parts_ref[shard, :own, :]
    out_ref[shards * own :, :] = sum_of_four(parts_ref, pl.ds(own, extra)).astype(jnp.bfloat16)


def split_kernel(keep_ref, got_ref, grads_ref, near_ref, far_ref):
    half = near_ref.shape[0]
    near_ref[...] = keep_ref[:half, :] + got_ref[:half, :].astype(jnp.float32)
    far = keep_ref[half:, :] + got_ref[half:, :].astype(jnp.float32)
    far_ref[:half, :] = far.astype(jnp.bfloat16)
    far_ref[half:, :] = grads_ref[...]


def join_kernel(near_ref, got_ref, grads_ref, out_ref):
    shards = out_ref.shape[0]
    half = near_ref.shape[0]
    own = half // shards
    grads = grads_ref[...].astype(jnp.float32) + got_ref[half:, :].astype(jnp.float32)
    grads = grads.astype(jnp.bfloat16)
    for shard in range(shards):
        rows = pl.ds(shard * own, own)
        total = near_ref[rows, :] + got_ref[rows, :].astype(jnp.float32)
        out_ref[shard, pl.ds(0, own), :] = total.astype(jnp.bfloat16)
        out_ref[shard, pl.ds(own, grads.shape[0]), :] = grads


def total_kernel(scale_factor, parts_ref, half_ref):
    extra = half_ref.shape[0] - 8 + BIAS_ROWS
    tail = sum_of_four(parts_ref, pl.ds(parts_ref.shape[1] - extra, extra))
    tail = tail * scale_factor
    height = half_ref.shape[0] - 8
    half_ref[:height, :] = tail[:height, :]
    bias_row = tail[height : height + 1, :] + tail[height + 1 : height + 2, :]
    half_ref[height:, :] = jnp.broadcast_to(bias_row, (8, bias_row.shape[1]))


def features_kernel(parts_ref, degree_ref, features_ref):
    tiles, edge = degree_ref.shape
    roots = lax.rsqrt(degree_ref[...].astype(jnp.float32))
    for tile in range(tiles):
        rows = pl.ds(tile * edge, edge)
        total = sum_of_four(parts_ref, rows)
        features_ref[rows, :] = (total * roots[tile : tile + 1, :]).T.astype(jnp.bfloat16)


def lay_out_kernel(core_ref, mine_ref, other_ref, grads_ref, bias_ref):
    first = core_ref[0] == 0
    height = grads_ref.shape[0]
    width = mine_ref.shape[1]
    mine, other = mine_ref[...], other_ref[...]
    halves = (jnp.where(first, mine, other), jnp.where(first, other, mine))
    for index, half in enumerate(halves):
        lanes = pl.ds(index * width, width)
        grads_ref[:, lanes] = half[:height, :]
        bias_ref[:, lanes] = half[height : height + 1, :]


def per_device(
    features,
    degree,
    cotangent,
    weight,
    layer_bias,
    patterns,
    tile_row,
    tile_col,
    tile_pattern,
    tile_weight,
    tile_count,
):
    node_dev, feature_count = features.shape
    hidden = weight.shape[1]
    row_devices = lax.axis_size("row")
    col_devices = lax.axis_size("col")
    chips = row_devices // 2
    edge = patterns.shape[1]
    per_shard = node_dev // edge
    row, col = lax.axis_index("row"), lax.axis_index("col")
    core = row % 2
    swap = [(index, index ^ 1) for index in range(row_devices)]
    row_near = [
        [(low * 4 + ring) * 2 + core_index for ring in pair for low in range(2)]
        for core_index in range(2)
        for pair in PAIRS[core_index]
    ]
    row_far = [
        (index, (index // 8 * 4 + far_neighbour(index // 2 % 4, index % 2)) * 2 + index % 2)
        for index in range(row_devices)
    ]
    col_near = [
        [index * col_devices + ring * 2 + high for ring in pair for high in range(2)]
        for index in range(row_devices)
        for pair in PAIRS[index % 2]
    ]
    col_far = [
        (
            index * col_devices + place,
            index * col_devices + far_neighbour(place // 2, index % 2) * 2 + place % 2,
        )
        for index in range(row_devices)
        for place in range(col_devices)
    ]
    exchange = functools.partial(lax.all_to_all, split_axis=0, concat_axis=0)
    both = ("row", "col")
    extra = feature_count + BIAS_ROWS
    half = chips * node_dev
    bf16, f32 = jnp.bfloat16, jnp.float32
    shape = jax.ShapeDtypeStruct
    degree_tiles = degree.reshape(per_shard, edge)
    tile_cost = pl.CostEstimate(
        flops=tile_row.size // (row_devices * col_devices) * edge * edge * feature_count,
        bytes_accessed=patterns.size * 2 + 4 * half * feature_count * 2,
        transcendentals=0,
    )

    scaled = pl.pallas_call(
        scale_kernel,
        out_shape=shape((4, node_dev, feature_count), bf16),
        in_specs=[ANY] * 2,
        out_specs=VMEM,
        scratch_shapes=[
            pltpu.VMEM(features.shape, bf16),
            pltpu.VMEM(degree_tiles.shape, jnp.int32),
            pltpu.SemaphoreType.DMA((2,)),
        ],
        compiler_params=PARAMS,
    )(features, degree_tiles)
    near_own = exchange(scaled, "row", axis_index_groups=row_near).reshape(half // 2, feature_count)
    near_other = lax.ppermute(near_own, "row", swap)
    far_own = lax.ppermute(near_own, "row", row_far)
    row_tiles, near_own = lax.optimization_barrier((tile_row.reshape(per_shard, edge), near_own))
    place = jnp.stack([row, col]).astype(jnp.int32)
    slots = pl.pallas_call(
        order_kernel,
        out_shape=shape((1, ORDERED), jnp.int32),
        in_specs=[SMEM] * 2 + [VMEM] * 4,
        out_specs=VMEM,
        compiler_params=PARAMS,
    )(
        place,
        tile_count,
        row_tiles,
        tile_col.reshape(per_shard, edge),
        tile_pattern.reshape(per_shard, edge),
        tile_weight.reshape(per_shard, edge),
    )
    forward_panel = pltpu.VMEM((half, feature_count), bf16)
    row_sums = shape((col_devices * node_dev, feature_count), f32)
    near_sums = pl.pallas_call(
        forward_near_kernel,
        out_shape=row_sums,
        in_specs=[SMEM] + [VMEM] * 3,
        out_specs=VMEM,
        scratch_shapes=[forward_panel],
        compiler_params=PARAMS,
        cost_estimate=tile_cost,
    )(slots, patterns, near_own, near_other)
    far_own, near_sums = lax.optimization_barrier((far_own, near_sums))
    far_other = lax.ppermute(far_own, "row", swap)
    row_part = pl.pallas_call(
        forward_far_kernel,
        out_shape=shape(row_sums.shape, bf16),
        in_specs=[SMEM] + [VMEM] * 4,
        out_specs=VMEM,
        scratch_shapes=[forward_panel, pltpu.VMEM(row_sums.shape, f32)],
        compiler_params=PARAMS,
        cost_estimate=tile_cost,
    )(slots, patterns, far_own, far_other, near_sums)
    parts = exchange(row_part.reshape(col_devices, node_dev, feature_count), "col")
    core_word = core.astype(jnp.int32).reshape(1)
    pre_act, upstream, keep_terms, send_terms = pl.pallas_call(
        middle_kernel,
        out_shape=(
            shape((node_dev, hidden), f32),
            shape((node_dev, hidden), f32),
            shape((extra, edge), f32),
            shape((extra, edge), bf16),
        ),
        in_specs=[SMEM] + [VMEM] * 5,
        out_specs=(VMEM,) * 4,
        compiler_params=PARAMS,
    )(core_word, parts, degree_tiles, cotangent, weight, layer_bias[None, :])
    got_terms = lax.ppermute(send_terms, "row", swap)
    spread = pl.pallas_call(
        spread_kernel,
        out_shape=shape((4, node_dev + extra, edge), bf16),
        in_specs=[VMEM] * 2,
        out_specs=VMEM,
        compiler_params=PARAMS,
    )(upstream, weight)
    spread = pl.pallas_call(
        append_kernel,
        out_shape=shape(spread.shape, bf16),
        in_specs=[VMEM] * 3,
        out_specs=VMEM,
        input_output_aliases={2: 0},
        compiler_params=PARAMS,
    )(keep_terms, got_terms, spread)
    near = pl.pallas_call(
        gather_kernel,
        out_shape=shape((4 * node_dev + extra, edge), bf16),
        in_specs=[VMEM],
        out_specs=VMEM,
        compiler_params=PARAMS,
    )(exchange(spread, both, axis_index_groups=col_near))
    pre_act, near = lax.optimization_barrier((pre_act, near))
    far = lax.ppermute(near, both, col_far)
    activations = pl.pallas_call(
        activation_kernel,
        out_shape=shape((node_dev, hidden), bf16),
        in_specs=[VMEM],
        out_specs=VMEM,
        compiler_params=PARAMS,
    )(pre_act)
    back_sums = shape((2 * half, edge), f32)
    back_near = pl.pallas_call(
        backward_near_kernel,
        out_shape=back_sums,
        in_specs=[SMEM] + [VMEM] * 2,
        out_specs=VMEM,
        compiler_params=PARAMS,
        cost_estimate=tile_cost,
    )(slots, patterns, near)
    far, activations, back_near = lax.optimization_barrier((far, activations, back_near))
    keep, send, grads = pl.pallas_call(
        backward_far_kernel,
        out_shape=(
            shape((half, edge), f32),
            shape((half, edge), bf16),
            shape((extra, edge), bf16),
        ),
        in_specs=[SMEM] + [VMEM] * 4,
        out_specs=(VMEM,) * 3,
        scratch_shapes=[pltpu.VMEM(back_sums.shape, f32)],
        compiler_params=PARAMS,
        cost_estimate=tile_cost,
    )(slots, patterns, near, far, back_near)
    got = lax.ppermute(send, "row", swap)
    near_sums, far_sums = pl.pallas_call(
        split_kernel,
        out_shape=(shape((half // 2, edge), f32), shape((half // 2 + extra, edge), bf16)),
        in_specs=[VMEM] * 3,
        out_specs=(VMEM,) * 2,
        compiler_params=PARAMS,
    )(keep, got, grads)
    joined = pl.pallas_call(
        join_kernel,
        out_shape=shape((4, node_dev + extra, edge), bf16),
        in_specs=[VMEM] * 3,
        out_specs=VMEM,
        compiler_params=PARAMS,
    )(near_sums, lax.ppermute(far_sums, "row", row_far), grads)
    back_parts = exchange(joined, "row", axis_index_groups=row_near)
    scale_factor = 1.0 / math.sqrt(node_dev * row_devices * col_devices)
    mine = pl.pallas_call(
        functools.partial(total_kernel, scale_factor),
        out_shape=shape((feature_count + 8, edge), f32),
        in_specs=[VMEM],
        out_specs=VMEM,
        compiler_params=PARAMS,
    )(back_parts)
    other = lax.ppermute(mine, "row", swap)
    grad_features = pl.pallas_call(
        features_kernel,
        out_shape=shape((node_dev, feature_count), bf16),
        in_specs=[VMEM] * 2,
        out_specs=VMEM,
        compiler_params=PARAMS,
    )(back_parts, degree_tiles)
    grad_weight, grad_bias = pl.pallas_call(
        lay_out_kernel,
        out_shape=(shape((feature_count, hidden), f32), shape((1, hidden), f32)),
        in_specs=[SMEM] + [VMEM] * 2,
        out_specs=(VMEM,) * 2,
        compiler_params=PARAMS,
    )(core_word, mine, other)
    return (activations, grad_features, grad_weight, grad_bias[0])


def solution(mesh):
    in_specs = (
        P(("row", "col"), None),
        P(("row", "col")),
        P(("row", "col"), None),
        P(),
        P(),
        P(),
        P("row", "col", None),
        P("row", "col", None),
        P("row", "col", None),
        P("row", "col", None),
        P("row", "col"),
    )
    out_specs = (P(("row", "col"), None), P(("row", "col"), None), P(), P())
    return jax.shard_map(
        per_device, mesh=mesh, in_specs=in_specs, out_specs=out_specs, check_vma=False
    )
```

```python
import functools
import math

import jax
import jax.numpy as jnp
from jax import lax
from jax.experimental import pallas as pl
from jax.experimental.pallas import tpu as pltpu
from jax.sharding import PartitionSpec as P

GROUP = 64
SMALL_GROUP = 32
CLASSES = 8
VMEM_LIMIT = 20 * 1024 * 1024
ROOT_2_PI = math.sqrt(2.0 / math.pi)
CUBIC = 0.044715
BIAS_ROWS = 16
PER_SHARD = 4
ORDERED = 640
BOUNDS = 600
ANY = pl.BlockSpec(memory_space=pl.ANY)
VMEM = pl.BlockSpec(memory_space=pltpu.VMEM)
SMEM = pl.BlockSpec(memory_space=pltpu.SMEM)
PARAMS = pltpu.CompilerParams(vmem_limit_bytes=VMEM_LIMIT)


def order_kernel(core_ref, live_ref, row_ref, col_ref, pattern_ref, weight_ref, out_ref):
    rows, edge = row_ref.shape
    tile_col, tile_row = col_ref[...], row_ref[...]
    shard = tile_col // PER_SHARD
    other = (shard % 2) ^ core_ref[0]
    column = (other * 8 + shard // 2) * PER_SHARD + tile_col % PER_SHARD
    word = tile_row | (pattern_ref[...] << 5) | (weight_ref[...] << 11) | (column << 14)
    slot = lax.broadcasted_iota(jnp.int32, (rows, edge), 0) * edge
    slot += lax.broadcasted_iota(jnp.int32, (rows, edge), 1)
    alive = slot < live_ref[0, 0]
    word = jnp.where(alive, word, 0)
    second = PER_SHARD // 2
    kind = ((column % PER_SHARD) // second) * 4 + ((tile_row % PER_SHARD) // second) * 2 + other
    kind = jnp.where(alive, kind, CLASSES)

    flags = [(kind == index).astype(jnp.float32) for index in range(CLASSES + 1)]
    stacked = jnp.concatenate(flags + [jnp.zeros((4, edge), jnp.float32)], 0)
    before = lax.broadcasted_iota(jnp.int32, (edge, edge), 0) < lax.broadcasted_iota(
        jnp.int32, (edge, edge), 1
    )
    earlier = jnp.dot(
        stacked.astype(jnp.bfloat16),
        before.astype(jnp.float32).astype(jnp.bfloat16),
        preferred_element_type=jnp.float32,
    )
    counts = jnp.sum(stacked, axis=1, keepdims=True)
    start = jnp.zeros((1, 1), jnp.float32)
    ends = []
    position = [jnp.zeros((1, edge), jnp.float32) for _ in range(rows)]
    for index in range(CLASSES + 1):
        for line in range(rows):
            at = index * rows + line
            position[line] += flags[index][line : line + 1] * (start + earlier[at : at + 1])
            start = start + counts[at : at + 1]
        ends.append(start)
    turned = jnp.concatenate(position + [jnp.zeros((8 - rows, edge), jnp.float32)], 0).T
    slots = rows * edge
    lanes = lax.broadcasted_iota(jnp.int32, (edge, slots), 1).astype(jnp.float32)
    pieces = jnp.zeros((8, slots), jnp.float32)
    for line in range(rows):
        chosen = (turned[:, line : line + 1] == lanes).astype(jnp.float32).astype(jnp.bfloat16)
        parts = [(word[line : line + 1] >> shift) & 127 for shift in (0, 7, 14)]
        parts = jnp.concatenate(parts + [jnp.zeros((5, edge), jnp.int32)], 0)
        parts = parts.astype(jnp.float32).astype(jnp.bfloat16)
        pieces += jnp.dot(parts, chosen, preferred_element_type=jnp.float32)
    pieces = pieces.astype(jnp.int32)
    out_ref[:, :slots] = pieces[0:1] | (pieces[1:2] << 7) | (pieces[2:3] << 14)
    lane = lax.broadcasted_iota(jnp.int32, (1, out_ref.shape[1] - slots), 1) + slots
    tail = jnp.zeros(lane.shape, jnp.int32)
    for index in range(CLASSES):
        tail = jnp.where(lane == BOUNDS + index, ends[index].astype(jnp.int32), tail)
    out_ref[:, slots:] = tail


def add_products(slots_ref, runs, product_of, place_of, sums, size):
    edge = sums.shape[1]
    (first, end), (first_b, end_b) = runs
    turns = (end - first + size - 1) // size
    turns_b = (end_b - first_b + size - 1) // size

    def one_group(turn, carry):
        is_a = turn < turns
        start = jnp.where(is_a, first + turn * size, first_b + (turn - turns) * size)
        stop = jnp.where(is_a, end, end_b)
        terms = []
        for member in range(size):
            slot = start + member
            word = slots_ref[0, slot]
            factor = jnp.where(slot < stop, (word >> 11) & 7, 0).astype(jnp.float32)
            terms.append((place_of(word), factor, product_of(word)))
        for place, factor, product in terms:
            rows = pl.ds(pl.multiple_of(place * edge, edge), edge)
            sums[rows, :] += factor * product
        return carry

    lax.fori_loop(0, turns + turns_b, one_group, 0)


def tile_of(ref, place, edge):
    return ref[pl.ds(pl.multiple_of(place * edge, edge), edge), :]


def class_bounds(slots_ref):
    return [0] + [slots_ref[0, BOUNDS + index] for index in range(CLASSES)]


def root_columns(degree):
    rows = lax.rsqrt(degree.astype(jnp.float32))
    rows = jnp.concatenate([rows, jnp.ones((8 - rows.shape[0], rows.shape[1]), jnp.float32)], 0)
    return rows.T


def scale_kernel(
    features_hbm, degree_hbm, first_ref, second_ref, features_ref, degree_ref, sems
):
    copies = (
        pltpu.make_async_copy(degree_hbm, degree_ref, sems.at[0]),
        pltpu.make_async_copy(features_hbm, features_ref, sems.at[1]),
    )
    for copy in copies:
        copy.start()
    copies[0].wait()
    roots = root_columns(degree_ref[...])
    copies[1].wait()
    tiles, edge = degree_ref.shape
    for tile in range(tiles):
        scaled = features_ref[pl.ds(tile * edge, edge), :].astype(jnp.float32)
        scaled = (scaled * roots[:, tile : tile + 1]).astype(jnp.bfloat16)
        out_ref, at = (first_ref, tile) if 2 * tile < tiles else (second_ref, tile - tiles // 2)
        for copy in range(out_ref.shape[0]):
            out_ref[copy, pl.ds(at * edge, edge), :] = scaled


def forward_sums(slots_ref, patterns_ref, own_ref, other_ref, panel, sums, second):
    edge = patterns_ref.shape[1]
    half = own_ref.shape[0]
    panel[:half, :] = own_ref[...]
    panel[half:, :] = other_ref[...]
    bounds = class_bounds(slots_ref)

    def product_of(word):
        place = ((word >> 16) << 1) | ((word >> 14) & 1)
        return jnp.dot(
            patterns_ref[(word >> 5) & 63],
            tile_of(panel, place, edge),
            preferred_element_type=jnp.float32,
        )

    run = (bounds[4], bounds[8]) if second else (bounds[0], bounds[4])
    add_products(slots_ref, (run, (0, 0)), product_of, lambda word: word & 31, sums, GROUP)


def forward_first_kernel(slots_ref, patterns_ref, own_ref, other_ref, out_ref, panel):
    out_ref[...] = jnp.zeros_like(out_ref)
    forward_sums(slots_ref, patterns_ref, own_ref, other_ref, panel, out_ref, False)


def forward_second_kernel(
    slots_ref, patterns_ref, own_ref, other_ref, so_far_ref, out_ref, panel, sums
):
    sums[...] = so_far_ref[...]
    forward_sums(slots_ref, patterns_ref, own_ref, other_ref, panel, sums, True)
    out_ref[...] = sums[...].astype(jnp.bfloat16)


def backward_sums(slots_ref, patterns_ref, spread_ref, sums, runs, size):
    edge = patterns_ref.shape[1]
    mask = sums.shape[0] // edge - 1

    def product_of(word):
        start = pl.multiple_of((word & 1) * edge, edge)
        return jnp.dot(
            spread_ref[(word >> 2) & 7, pl.ds(start, edge), :],
            patterns_ref[(word >> 5) & 63],
            preferred_element_type=jnp.float32,
        )

    add_products(slots_ref, runs, product_of, lambda word: (word >> 14) & mask, sums, size)


def backward_first_kernel(slots_ref, patterns_ref, spread_ref, out_ref):
    out_ref[...] = jnp.zeros_like(out_ref)
    bounds = class_bounds(slots_ref)
    runs = ((bounds[0], bounds[2]), (bounds[4], bounds[6]))
    backward_sums(slots_ref, patterns_ref, spread_ref, out_ref, runs, GROUP)


def backward_send_kernel(slots_ref, patterns_ref, spread_ref, so_far_ref, send_ref, sums):
    half = sums.shape[0]
    sums[...] = so_far_ref[half:, :]
    bounds = class_bounds(slots_ref)
    runs = ((bounds[3], bounds[4]), (bounds[7], bounds[8]))
    backward_sums(slots_ref, patterns_ref, spread_ref, sums, runs, SMALL_GROUP)
    send_ref[...] = sums[...].astype(jnp.bfloat16)


def backward_keep_kernel(slots_ref, patterns_ref, spread_ref, so_far_ref, keep_ref, grads_ref):
    keep_ref[...] = so_far_ref[: keep_ref.shape[0], :]
    bounds = class_bounds(slots_ref)
    runs = ((bounds[2], bounds[3]), (bounds[6], bounds[7]))
    backward_sums(slots_ref, patterns_ref, spread_ref, keep_ref, runs, SMALL_GROUP)
    shards, rows_in_shard, _ = spread_ref.shape
    own = rows_in_shard - grads_ref.shape[0]
    grads = spread_ref[0, own:, :].astype(jnp.float32)
    for shard in range(1, shards):
        grads += spread_ref[shard, own:, :].astype(jnp.float32)
    grads_ref[...] = grads.astype(jnp.bfloat16)


def split_product(left, right, dims):
    high = left.astype(jnp.bfloat16)
    low = (left - high.astype(jnp.float32)).astype(jnp.bfloat16)
    return lax.dot_general(
        high, right, (dims, ((), ())), preferred_element_type=jnp.float32
    ) + lax.dot_general(low, right, (dims, ((), ())), preferred_element_type=jnp.float32)


def activate(pre_act):
    square = pre_act * pre_act
    bent = jnp.tanh(ROOT_2_PI * (pre_act + CUBIC * (pre_act * square)))
    return square, bent, 0.5 * (1.0 + bent)


def middle_tiles(
    tiles, parts_ref, degree_ref, cotangent_ref, weight_ref, bias_ref, pre_ref, out_ref
):
    edge = degree_ref.shape[1]
    shards = parts_ref.shape[0]
    weight = weight_ref[...]
    roots = root_columns(degree_ref[...])
    grads = jnp.zeros(weight.shape, jnp.float32)
    bias_row = jnp.zeros(bias_ref.shape, jnp.float32)
    for index, tile in enumerate(tiles):
        rows = pl.ds(tile * edge, edge)
        own_rows = pl.ds(index * edge, edge)
        sums = parts_ref[0, rows, :].astype(jnp.float32)
        for shard in range(1, shards):
            sums += parts_ref[shard, rows, :].astype(jnp.float32)
        inv_root = roots[:, tile : tile + 1]
        pre_act = inv_root * split_product(sums, weight, ((1,), (0,))) + bias_ref[...]
        pre_ref[own_rows, :] = pre_act
        square, bent, half = activate(pre_act)
        rise = 0.5 * pre_act * (1.0 - bent * bent) * (ROOT_2_PI * (1.0 + 3.0 * CUBIC * square))
        slope = cotangent_ref[rows, :].astype(jnp.float32) * (half + rise)
        upstream = inv_root * slope
        high = upstream.astype(jnp.bfloat16)
        low = (upstream - high.astype(jnp.float32)).astype(jnp.bfloat16)
        spread = sum(
            lax.dot_general(
                weight, part, (((1,), (1,)), ((), ())), preferred_element_type=jnp.float32
            )
            for part in (high, low)
        ).astype(jnp.bfloat16)
        for shard in range(shards):
            out_ref[shard, own_rows, :] = spread
        grads += split_product(sums, high, ((0,), (0,)))
        bias_row += jnp.sum(slope, axis=0, keepdims=True)
    return grads, bias_row


def middle_first_kernel(
    parts_ref,
    degree_ref,
    cotangent_ref,
    weight_ref,
    bias_ref,
    pre_ref,
    out_ref,
    grads_ref,
    bias_out_ref,
):
    tiles = range(degree_ref.shape[0] // 2)
    grads_ref[...], bias_out_ref[...] = middle_tiles(
        tiles, parts_ref, degree_ref, cotangent_ref, weight_ref, bias_ref, pre_ref, out_ref
    )


def middle_second_kernel(
    core_ref,
    parts_ref,
    degree_ref,
    cotangent_ref,
    weight_ref,
    bias_ref,
    grads_ref,
    bias_so_far_ref,
    pre_ref,
    out_ref,
    keep_ref,
    send_ref,
):
    tiles = range(degree_ref.shape[0] // 2, degree_ref.shape[0])
    grads, bias_row = middle_tiles(
        tiles, parts_ref, degree_ref, cotangent_ref, weight_ref, bias_ref, pre_ref, out_ref
    )
    grads += grads_ref[...]
    bias_row += bias_so_far_ref[...]
    height, width = weight_ref.shape[0], keep_ref.shape[1]
    bias_high = bias_row.astype(jnp.bfloat16).astype(jnp.float32)
    bias_low = bias_row - bias_high
    first = core_ref[0] == 0

    def put(target, left):
        pick = lambda whole: jnp.where(left, whole[:, :width], whole[:, width:])
        target[:height, :] = pick(grads).astype(target.dtype)
        row_ids = lax.broadcasted_iota(jnp.int32, (BIAS_ROWS, width), 0)
        block = jnp.where(row_ids == 0, pick(bias_high), 0.0)
        block = jnp.where(row_ids == 1, pick(bias_low), block)
        target[height:, :] = block.astype(target.dtype)

    put(keep_ref, first)
    put(send_ref, jnp.logical_not(first))


def activation_kernel(first_ref, second_ref, act_ref):
    half = first_ref.shape[0]
    for ref, rows in ((first_ref, pl.ds(0, half)), (second_ref, pl.ds(half, half))):
        pre_act = ref[...]
        act_ref[rows, :] = (pre_act * activate(pre_act)[2]).astype(jnp.bfloat16)


def append_kernel(keep_ref, got_ref, spread_ref, out_ref):
    terms = (keep_ref[...] + got_ref[...].astype(jnp.float32)).astype(jnp.bfloat16)
    rows = pl.ds(out_ref.shape[1] - terms.shape[0], terms.shape[0])
    for shard in range(out_ref.shape[0]):
        out_ref[shard, rows, :] = terms


def sum_of_parts(parts_ref, rows):
    total = parts_ref[0, rows, :].astype(jnp.float32)
    for shard in range(1, parts_ref.shape[0]):
        total += parts_ref[shard, rows, :].astype(jnp.float32)
    return total


def join_kernel(keep_ref, got_ref, grads_ref, out_ref):
    shards = out_ref.shape[0]
    own = keep_ref.shape[0] // shards
    for shard in range(shards):
        rows = pl.ds(shard * own, own)
        total = keep_ref[rows, :] + got_ref[rows, :].astype(jnp.float32)
        out_ref[shard, pl.ds(0, own), :] = total.astype(jnp.bfloat16)
        out_ref[shard, pl.ds(own, grads_ref.shape[0]), :] = grads_ref[...]


def total_kernel(scale_factor, parts_ref, half_ref):
    extra = half_ref.shape[0] - 8 + BIAS_ROWS
    tail = sum_of_parts(parts_ref, pl.ds(parts_ref.shape[1] - extra, extra))
    tail = tail * scale_factor
    height = half_ref.shape[0] - 8
    half_ref[:height, :] = tail[:height, :]
    bias_row = tail[height : height + 1, :] + tail[height + 1 : height + 2, :]
    half_ref[height:, :] = jnp.broadcast_to(bias_row, (8, bias_row.shape[1]))


def features_kernel(parts_ref, degree_ref, features_ref):
    tiles, edge = degree_ref.shape
    roots = lax.rsqrt(degree_ref[...].astype(jnp.float32))
    for tile in range(tiles):
        rows = pl.ds(tile * edge, edge)
        total = sum_of_parts(parts_ref, rows)
        features_ref[rows, :] = (total * roots[tile : tile + 1, :]).T.astype(jnp.bfloat16)


def lay_out_kernel(core_ref, mine_ref, other_ref, grads_ref, bias_ref):
    first = core_ref[0] == 0
    height = grads_ref.shape[0]
    width = mine_ref.shape[1]
    mine, other = mine_ref[...], other_ref[...]
    halves = (jnp.where(first, mine, other), jnp.where(first, other, mine))
    for index, half in enumerate(halves):
        lanes = pl.ds(index * width, width)
        grads_ref[:, lanes] = half[:height, :]
        bias_ref[:, lanes] = half[height : height + 1, :]


def per_device(
    features,
    degree,
    cotangent,
    weight,
    layer_bias,
    patterns,
    tile_row,
    tile_col,
    tile_pattern,
    tile_weight,
    tile_count,
):
    node_dev, feature_count = features.shape
    hidden = weight.shape[1]
    row_devices = lax.axis_size("row")
    col_devices = lax.axis_size("col")
    chips = row_devices // 2
    edge = patterns.shape[1]
    per_shard = node_dev // edge
    core = lax.axis_index("row") % 2
    same_core = [list(range(first, row_devices, 2)) for first in range(2)]
    swap = [(index, index ^ 1) for index in range(row_devices)]
    exchange = functools.partial(lax.all_to_all, split_axis=0, concat_axis=0)
    across_chips = functools.partial(exchange, axis_name="row", axis_index_groups=same_core)
    across_cols = functools.partial(exchange, axis_name="col")
    extra = feature_count + BIAS_ROWS
    half = chips * node_dev
    bf16, f32 = jnp.bfloat16, jnp.float32
    shape = jax.ShapeDtypeStruct
    degree_tiles = degree.reshape(per_shard, edge)
    tile_cost = pl.CostEstimate(
        flops=tile_row.size // (row_devices * col_devices) * edge * edge * feature_count,
        bytes_accessed=patterns.size * 2 + 4 * half * feature_count * 2,
        transcendentals=0,
    )

    core_word = core.astype(jnp.int32).reshape(1)
    half_shard = node_dev // 2
    copies = shape((chips, half_shard, feature_count), bf16)
    first, second = pl.pallas_call(
        scale_kernel,
        out_shape=(copies, copies),
        in_specs=[ANY] * 2,
        out_specs=(VMEM,) * 2,
        scratch_shapes=[
            pltpu.VMEM(features.shape, bf16),
            pltpu.VMEM(degree_tiles.shape, jnp.int32),
            pltpu.SemaphoreType.DMA((2,)),
        ],
        compiler_params=PARAMS,
    )(features, degree_tiles)
    first_own = across_chips(first).reshape(half // 2, feature_count)
    second_own = across_chips(second).reshape(half // 2, feature_count)
    slots = pl.pallas_call(
        order_kernel,
        out_shape=shape((1, ORDERED), jnp.int32),
        in_specs=[SMEM] * 2 + [VMEM] * 4,
        out_specs=VMEM,
        compiler_params=PARAMS,
    )(
        core_word,
        tile_count,
        tile_row.reshape(per_shard, edge),
        tile_col.reshape(per_shard, edge),
        tile_pattern.reshape(per_shard, edge),
        tile_weight.reshape(per_shard, edge),
    )
    first_own, slots = lax.optimization_barrier((first_own, slots))
    first_other = lax.ppermute(first_own, "row", swap)
    forward_panel = pltpu.VMEM((half, feature_count), bf16)
    row_sums = shape((col_devices * node_dev, feature_count), f32)
    so_far = pl.pallas_call(
        forward_first_kernel,
        out_shape=row_sums,
        in_specs=[SMEM] + [VMEM] * 3,
        out_specs=VMEM,
        scratch_shapes=[forward_panel],
        compiler_params=PARAMS,
        cost_estimate=tile_cost,
    )(slots, patterns, first_own, first_other)
    second_own, so_far = lax.optimization_barrier((second_own, so_far))
    second_other = lax.ppermute(second_own, "row", swap)
    row_part = pl.pallas_call(
        forward_second_kernel,
        out_shape=shape(row_sums.shape, bf16),
        in_specs=[SMEM] + [VMEM] * 4,
        out_specs=VMEM,
        scratch_shapes=[forward_panel, pltpu.VMEM(row_sums.shape, f32)],
        compiler_params=PARAMS,
        cost_estimate=tile_cost,
    )(slots, patterns, second_own, second_other, so_far)
    parts = across_cols(row_part.reshape(col_devices, node_dev, feature_count))

    middle_inputs = (parts, degree_tiles, cotangent, weight, layer_bias[None, :])
    pre_shape = shape((half_shard, hidden), f32)
    pre_first, spread, grads, bias_row = pl.pallas_call(
        middle_first_kernel,
        out_shape=(
            pre_shape,
            shape((col_devices, half_shard, edge), bf16),
            shape((feature_count, hidden), f32),
            shape((1, hidden), f32),
        ),
        in_specs=[VMEM] * 5,
        out_specs=(VMEM,) * 4,
        compiler_params=PARAMS,
    )(*middle_inputs)
    spread_first = across_cols(spread)
    pre_second, spread, keep_terms, send_terms = pl.pallas_call(
        middle_second_kernel,
        out_shape=(
            pre_shape,
            shape((col_devices, half_shard + extra, edge), bf16),
            shape((extra, edge), f32),
            shape((extra, edge), bf16),
        ),
        in_specs=[SMEM] + [VMEM] * 7,
        out_specs=(VMEM,) * 4,
        compiler_params=PARAMS,
    )(core_word, *middle_inputs, grads, bias_row)
    got_terms = lax.ppermute(send_terms, "row", swap)
    spread = pl.pallas_call(
        append_kernel,
        out_shape=shape(spread.shape, bf16),
        in_specs=[VMEM] * 3,
        out_specs=VMEM,
        input_output_aliases={2: 0},
        compiler_params=PARAMS,
    )(keep_terms, got_terms, spread)
    spread_first, spread = lax.optimization_barrier((spread_first, spread))
    spread_second = across_cols(spread)
    back_sums = pl.pallas_call(
        backward_first_kernel,
        out_shape=shape((2 * half, edge), f32),
        in_specs=[SMEM] + [VMEM] * 2,
        out_specs=VMEM,
        compiler_params=PARAMS,
        cost_estimate=tile_cost,
    )(slots, patterns, spread_first)
    spread_second, back_sums = lax.optimization_barrier((spread_second, back_sums))
    send = pl.pallas_call(
        backward_send_kernel,
        out_shape=shape((half, edge), bf16),
        in_specs=[SMEM] + [VMEM] * 3,
        out_specs=VMEM,
        scratch_shapes=[pltpu.VMEM((half, edge), f32)],
        compiler_params=PARAMS,
        cost_estimate=tile_cost,
    )(slots, patterns, spread_second, back_sums)
    back_sums, send = lax.optimization_barrier((back_sums, send))
    got = lax.ppermute(send, "row", swap)
    keep, grads = pl.pallas_call(
        backward_keep_kernel,
        out_shape=(shape((half, edge), f32), shape((extra, edge), bf16)),
        in_specs=[SMEM] + [VMEM] * 3,
        out_specs=(VMEM,) * 2,
        compiler_params=PARAMS,
        cost_estimate=tile_cost,
    )(slots, patterns, spread_second, back_sums)
    got, keep = lax.optimization_barrier((got, keep))
    joined = pl.pallas_call(
        join_kernel,
        out_shape=shape((chips, node_dev + extra, edge), bf16),
        in_specs=[VMEM] * 3,
        out_specs=VMEM,
        compiler_params=PARAMS,
    )(keep, got, grads)
    joined, pre_first, pre_second = lax.optimization_barrier((joined, pre_first, pre_second))
    back_parts = across_chips(joined)
    activations = pl.pallas_call(
        activation_kernel,
        out_shape=shape((node_dev, hidden), bf16),
        in_specs=[VMEM] * 2,
        out_specs=VMEM,
        compiler_params=PARAMS,
    )(pre_first, pre_second)
    back_parts, activations = lax.optimization_barrier((back_parts, activations))
    scale_factor = 1.0 / math.sqrt(node_dev * row_devices * col_devices)
    mine = pl.pallas_call(
        functools.partial(total_kernel, scale_factor),
        out_shape=shape((feature_count + 8, edge), f32),
        in_specs=[VMEM],
        out_specs=VMEM,
        compiler_params=PARAMS,
    )(back_parts)
    other = lax.ppermute(mine, "row", swap)
    grad_features = pl.pallas_call(
        features_kernel,
        out_shape=shape((node_dev, feature_count), bf16),
        in_specs=[VMEM] * 2,
        out_specs=VMEM,
        compiler_params=PARAMS,
    )(back_parts, degree_tiles)
    grad_weight, grad_bias = pl.pallas_call(
        lay_out_kernel,
        out_shape=(shape((feature_count, hidden), f32), shape((1, hidden), f32)),
        in_specs=[SMEM] + [VMEM] * 2,
        out_specs=(VMEM,) * 2,
        compiler_params=PARAMS,
    )(core_word, mine, other)
    return (activations, grad_features, grad_weight, grad_bias[0])


def solution(mesh):
    in_specs = (
        P(("row", "col"), None),
        P(("row", "col")),
        P(("row", "col"), None),
        P(),
        P(),
        P(),
        P("row", "col", None),
        P("row", "col", None),
        P("row", "col", None),
        P("row", "col", None),
        P("row", "col"),
    )
    out_specs = (P(("row", "col"), None), P(("row", "col"), None), P(), P())
    return jax.shard_map(
        per_device, mesh=mesh, in_specs=in_specs, out_specs=out_specs, check_vma=False
    )
```

```python
import functools
import math

import jax
import jax.numpy as jnp
from jax import lax
from jax.experimental import pallas as pl
from jax.experimental.pallas import tpu as pltpu
from jax.sharding import PartitionSpec as P

GROUP = 64
VMEM_LIMIT = 20 * 1024 * 1024
ROOT_2_PI = math.sqrt(2.0 / math.pi)
CUBIC = 0.044715
BIAS_ROWS = 16
PER_SHARD = 4
CLASSES = 2
ORDERED = 640
BOUNDS = 600
PAIRS = (((0, 1), (2, 3)), ((0, 3), (1, 2)))
HBM = pl.BlockSpec(memory_space=pltpu.HBM)
VMEM = pl.BlockSpec(memory_space=pltpu.VMEM)
SMEM = pl.BlockSpec(memory_space=pltpu.SMEM)
PARAMS = pltpu.CompilerParams(vmem_limit_bytes=VMEM_LIMIT)


def pair_of(place, core):
    return jnp.where(core == 0, place >> 1, (place ^ (place >> 1)) & 1)


def pair_index(place, core):
    return jnp.where(core == 0, place & 1, place >> 1)


def far_neighbour(place, core):
    return place ^ 3 if core == 0 else place ^ 1


def order_kernel(
    place_ref, live_ref, row_hbm, col_hbm, pattern_hbm, weight_hbm, out_ref, fields, sems
):
    sources = (row_hbm, col_hbm, pattern_hbm, weight_hbm)
    copies = [
        pltpu.make_async_copy(source, fields.at[index], sems.at[index])
        for index, source in enumerate(sources)
    ]
    for copy in copies:
        copy.start()
    for copy in copies:
        copy.wait()
    row = place_ref[0]
    _, rows, edge = fields.shape
    tile_row, tile_col = fields[0], fields[1]
    shard = tile_col // PER_SHARD
    parity = shard % 2
    chip = shard // 2
    ring = chip % 4
    tile = tile_col % PER_SHARD
    half = parity ^ (row % 2)
    far = (pair_of(ring, parity) != pair_of((row // 2) % 4, parity)).astype(jnp.int32)
    rank = pair_index(ring, parity) * 2 + chip // 4
    place = (half * 4 + rank) * PER_SHARD + tile
    target = (half * 8 + chip) * PER_SHARD + tile
    word = tile_row | (fields[2] << 5) | (fields[3] << 11) | (place << 14) | (target << 19)
    slot = lax.broadcasted_iota(jnp.int32, (rows, edge), 0) * edge
    slot += lax.broadcasted_iota(jnp.int32, (rows, edge), 1)
    alive = slot < live_ref[0, 0]
    word = jnp.where(alive, word, 0)
    kind = jnp.where(alive, far, CLASSES)

    flags = [(kind == index).astype(jnp.float32) for index in range(CLASSES + 1)]
    stacked = jnp.concatenate(flags + [jnp.zeros((4, edge), jnp.float32)], 0)
    before = lax.broadcasted_iota(jnp.int32, (edge, edge), 0) < lax.broadcasted_iota(
        jnp.int32, (edge, edge), 1
    )
    earlier = jnp.dot(
        stacked.astype(jnp.bfloat16),
        before.astype(jnp.float32).astype(jnp.bfloat16),
        preferred_element_type=jnp.float32,
    )
    counts = jnp.sum(stacked, axis=1, keepdims=True)
    start = jnp.zeros((1, 1), jnp.float32)
    ends = []
    position = [jnp.zeros((1, edge), jnp.float32) for _ in range(rows)]
    for index in range(CLASSES + 1):
        for line in range(rows):
            at = index * rows + line
            position[line] += flags[index][line : line + 1] * (start + earlier[at : at + 1])
            start = start + counts[at : at + 1]
        ends.append(start)
    turned = jnp.concatenate(position + [jnp.zeros((8 - rows, edge), jnp.float32)], 0).T
    slots = rows * edge
    lanes = lax.broadcasted_iota(jnp.int32, (edge, slots), 1).astype(jnp.float32)
    pieces = jnp.zeros((8, slots), jnp.float32)
    for line in range(rows):
        chosen = (turned[:, line : line + 1] == lanes).astype(jnp.float32).astype(jnp.bfloat16)
        parts = [(word[line : line + 1] >> shift) & 127 for shift in (0, 7, 14, 21)]
        parts = jnp.concatenate(parts + [jnp.zeros((4, edge), jnp.int32)], 0)
        parts = parts.astype(jnp.float32).astype(jnp.bfloat16)
        pieces += jnp.dot(parts, chosen, preferred_element_type=jnp.float32)
    pieces = pieces.astype(jnp.int32)
    out_ref[:, :slots] = (
        pieces[0:1] | (pieces[1:2] << 7) | (pieces[2:3] << 14) | (pieces[3:4] << 21)
    )
    lane = lax.broadcasted_iota(jnp.int32, (1, out_ref.shape[1] - slots), 1) + slots
    tail = jnp.zeros(lane.shape, jnp.int32)
    for index in range(CLASSES):
        tail = jnp.where(lane == BOUNDS + index, ends[index].astype(jnp.int32), tail)
    out_ref[:, slots:] = tail


def root_columns(degree):
    rows = lax.rsqrt(degree.astype(jnp.float32))
    rows = jnp.concatenate([rows, jnp.ones((8 - rows.shape[0], rows.shape[1]), jnp.float32)], 0)
    return rows.T


def scale_kernel(features_hbm, degree_hbm, out_ref, features_ref, degree_ref, sems):
    copies = (
        pltpu.make_async_copy(degree_hbm, degree_ref, sems.at[0]),
        pltpu.make_async_copy(features_hbm, features_ref, sems.at[1]),
    )
    for copy in copies:
        copy.start()
    copies[0].wait()
    roots = root_columns(degree_ref[...])
    copies[1].wait()
    edge = degree_ref.shape[1]
    for tile in range(degree_ref.shape[0]):
        rows = pl.ds(tile * edge, edge)
        scaled = features_ref[rows, :].astype(jnp.float32) * roots[:, tile : tile + 1]
        scaled = scaled.astype(jnp.bfloat16)
        for copy in range(out_ref.shape[0]):
            out_ref[copy, rows, :] = scaled


def add_products(slots_ref, first, end, product_of, place_of, sums):
    edge = sums.shape[1]

    def one_group(turn, carry):
        terms = []
        for member in range(GROUP):
            slot = first + turn * GROUP + member
            word = slots_ref[0, slot]
            factor = jnp.where(slot < end, (word >> 11) & 7, 0).astype(jnp.float32)
            terms.append((place_of(word), factor, product_of(word)))
        for place, factor, product in terms:
            rows = pl.ds(pl.multiple_of(place * edge, edge), edge)
            sums[rows, :] += factor * product
        return carry

    lax.fori_loop(0, (end - first + GROUP - 1) // GROUP, one_group, 0)


def tile_of(ref, place, edge):
    return ref[pl.ds(pl.multiple_of(place * edge, edge), edge), :]


def forward_sums(slots_ref, patterns_ref, own_ref, other_ref, panel, sums, far):
    edge = patterns_ref.shape[1]
    half = own_ref.shape[0]
    panel[:half, :] = own_ref[...]
    panel[half:, :] = other_ref[...]
    middle, end = slots_ref[0, BOUNDS], slots_ref[0, BOUNDS + 1]

    def product_of(word):
        return jnp.dot(
            patterns_ref[(word >> 5) & 63],
            tile_of(panel, (word >> 14) & 31, edge),
            preferred_element_type=jnp.float32,
        )

    first, end = (middle, end) if far else (0, middle)
    add_products(slots_ref, first, end, product_of, lambda word: word & 31, sums)


def forward_near_kernel(slots_ref, patterns_ref, own_ref, other_ref, out_ref, panel):
    out_ref[...] = jnp.zeros_like(out_ref)
    forward_sums(slots_ref, patterns_ref, own_ref, other_ref, panel, out_ref, False)


def forward_far_kernel(slots_ref, patterns_ref, own_ref, other_ref, so_far_ref, out_ref, panel, sums):
    sums[...] = so_far_ref[...]
    forward_sums(slots_ref, patterns_ref, own_ref, other_ref, panel, sums, True)
    out_ref[...] = sums[...].astype(jnp.bfloat16)


def backward_kernel(slots_ref, patterns_ref, spread_ref, keep_ref, send_ref, grads_ref, sums):
    edge = patterns_ref.shape[1]
    shards, rows_in_shard, _ = spread_ref.shape
    half = sums.shape[0] // 2
    own = rows_in_shard - grads_ref.shape[0]
    sums[...] = jnp.zeros_like(sums)

    def product_of(word):
        start = pl.multiple_of((word & 3) * edge, edge)
        return jnp.dot(
            spread_ref[(word >> 2) & 7, pl.ds(start, edge), :],
            patterns_ref[(word >> 5) & 63],
            preferred_element_type=jnp.float32,
        )

    end = slots_ref[0, BOUNDS + CLASSES - 1]
    add_products(slots_ref, 0, end, product_of, lambda word: (word >> 19) & 63, sums)
    keep_ref[...] = sums[:half, :]
    send_ref[...] = sums[half:, :].astype(jnp.bfloat16)
    grads = spread_ref[0, own:, :].astype(jnp.float32)
    for shard in range(1, shards):
        grads += spread_ref[shard, own:, :].astype(jnp.float32)
    grads_ref[...] = grads.astype(jnp.bfloat16)


def split_product(left, right, dims):
    high = left.astype(jnp.bfloat16)
    low = (left - high.astype(jnp.float32)).astype(jnp.bfloat16)
    return lax.dot_general(
        high, right, (dims, ((), ())), preferred_element_type=jnp.float32
    ) + lax.dot_general(low, right, (dims, ((), ())), preferred_element_type=jnp.float32)


def activate(pre_act):
    square = pre_act * pre_act
    bent = jnp.tanh(ROOT_2_PI * (pre_act + CUBIC * (pre_act * square)))
    return square, bent, 0.5 * (1.0 + bent)


def middle_kernel(
    place_ref,
    parts_ref,
    degree_ref,
    cotangent_ref,
    weight_ref,
    bias_ref,
    pre_ref,
    upstream_ref,
    keep_ref,
    send_ref,
):
    tiles, edge = degree_ref.shape
    shards = parts_ref.shape[0]
    weight = weight_ref[...]
    height = weight.shape[0]
    roots = root_columns(degree_ref[...])
    grads = jnp.zeros(weight.shape, jnp.float32)
    bias_row = jnp.zeros(bias_ref.shape, jnp.float32)
    for tile in range(tiles):
        rows = pl.ds(tile * edge, edge)
        sums = parts_ref[0, rows, :].astype(jnp.float32)
        for shard in range(1, shards):
            sums += parts_ref[shard, rows, :].astype(jnp.float32)
        inv_root = roots[:, tile : tile + 1]
        pre_act = inv_root * split_product(sums, weight, ((1,), (0,))) + bias_ref[...]
        pre_ref[rows, :] = pre_act
        square, bent, half = activate(pre_act)
        rise = 0.5 * pre_act * (1.0 - bent * bent) * (ROOT_2_PI * (1.0 + 3.0 * CUBIC * square))
        slope = cotangent_ref[rows, :].astype(jnp.float32) * (half + rise)
        upstream = inv_root * slope
        upstream_ref[rows, :] = upstream
        grads += split_product(sums, upstream.astype(jnp.bfloat16), ((0,), (0,)))
        bias_row += jnp.sum(slope, axis=0, keepdims=True)
    width = keep_ref.shape[1]
    bias_high = bias_row.astype(jnp.bfloat16).astype(jnp.float32)
    bias_low = bias_row - bias_high
    first = place_ref[0] % 2 == 0

    def put(target, left):
        pick = lambda whole: jnp.where(left, whole[:, :width], whole[:, width:])
        target[:height, :] = pick(grads).astype(target.dtype)
        row_ids = lax.broadcasted_iota(jnp.int32, (BIAS_ROWS, width), 0)
        block = jnp.where(row_ids == 0, pick(bias_high), 0.0)
        block = jnp.where(row_ids == 1, pick(bias_low), block)
        target[height:, :] = block.astype(target.dtype)

    put(keep_ref, first)
    put(send_ref, jnp.logical_not(first))


def activation_kernel(pre_ref, act_ref):
    pre_act = pre_ref[...]
    act_ref[...] = (pre_act * activate(pre_act)[2]).astype(jnp.bfloat16)


def spread_kernel(upstream_ref, weight_ref, out_ref):
    edge = out_ref.shape[2]
    for tile in range(upstream_ref.shape[0] // edge):
        rows = pl.ds(tile * edge, edge)
        upstream = upstream_ref[rows, :]
        high = upstream.astype(jnp.bfloat16)
        low = (upstream - high.astype(jnp.float32)).astype(jnp.bfloat16)
        spread = sum(
            lax.dot_general(
                weight_ref[...], part, (((1,), (1,)), ((), ())), preferred_element_type=jnp.float32
            )
            for part in (high, low)
        ).astype(jnp.bfloat16)
        for shard in range(out_ref.shape[0]):
            out_ref[shard, rows, :] = spread


def append_kernel(keep_ref, got_ref, spread_ref, out_ref):
    terms = (keep_ref[...] + got_ref[...].astype(jnp.float32)).astype(jnp.bfloat16)
    rows = pl.ds(out_ref.shape[1] - terms.shape[0], terms.shape[0])
    for shard in range(out_ref.shape[0]):
        out_ref[shard, rows, :] = terms


def join_kernel(keep_ref, got_ref, grads_ref, out_ref):
    shards = out_ref.shape[0]
    own = keep_ref.shape[0] // shards
    for shard in range(shards):
        rows = pl.ds(shard * own, own)
        total = keep_ref[rows, :] + got_ref[rows, :].astype(jnp.float32)
        out_ref[shard, pl.ds(0, own), :] = total.astype(jnp.bfloat16)
        out_ref[shard, pl.ds(own, grads_ref.shape[0]), :] = grads_ref[...]


def total_kernel(scale_factor, parts_ref, half_ref):
    shards = parts_ref.shape[0]
    own = parts_ref.shape[1] - (half_ref.shape[0] - 8 + BIAS_ROWS)
    tail = parts_ref[0, own:, :].astype(jnp.float32)
    for shard in range(1, shards):
        tail += parts_ref[shard, own:, :].astype(jnp.float32)
    tail = tail * scale_factor
    height = half_ref.shape[0] - 8
    half_ref[:height, :] = tail[:height, :]
    bias_row = tail[height : height + 1, :] + tail[height + 1 : height + 2, :]
    half_ref[height:, :] = jnp.broadcast_to(bias_row, (8, bias_row.shape[1]))


def features_kernel(parts_ref, degree_ref, features_ref):
    tiles, edge = degree_ref.shape
    roots = lax.rsqrt(degree_ref[...].astype(jnp.float32))
    for tile in range(tiles):
        rows = pl.ds(tile * edge, edge)
        total = parts_ref[0, rows, :].astype(jnp.float32)
        for shard in range(1, parts_ref.shape[0]):
            total += parts_ref[shard, rows, :].astype(jnp.float32)
        features_ref[rows, :] = (total * roots[tile : tile + 1, :]).T.astype(jnp.bfloat16)


def lay_out_kernel(place_ref, mine_ref, other_ref, grads_ref, bias_ref):
    first = place_ref[0] % 2 == 0
    height = grads_ref.shape[0]
    width = mine_ref.shape[1]
    mine, other = mine_ref[...], other_ref[...]
    halves = (jnp.where(first, mine, other), jnp.where(first, other, mine))
    for index, half in enumerate(halves):
        lanes = pl.ds(index * width, width)
        grads_ref[:, lanes] = half[:height, :]
        bias_ref[:, lanes] = half[height : height + 1, :]


def per_device(
    features,
    degree,
    cotangent,
    weight,
    layer_bias,
    patterns,
    tile_row,
    tile_col,
    tile_pattern,
    tile_weight,
    tile_count,
):
    node_dev, feature_count = features.shape
    hidden = weight.shape[1]
    row_devices = lax.axis_size("row")
    col_devices = lax.axis_size("col")
    chips = row_devices // 2
    edge = patterns.shape[1]
    per_shard = node_dev // edge
    row = lax.axis_index("row")
    swap = [(index, index ^ 1) for index in range(row_devices)]
    row_near = [
        [(low * 4 + ring) * 2 + core_index for ring in pair for low in range(2)]
        for core_index in range(2)
        for pair in PAIRS[core_index]
    ]
    row_far = [
        (index, (index // 8 * 4 + far_neighbour(index // 2 % 4, index % 2)) * 2 + index % 2)
        for index in range(row_devices)
    ]
    exchange = functools.partial(lax.all_to_all, split_axis=0, concat_axis=0)
    same_core = [list(range(first, row_devices, 2)) for first in range(2)]
    extra = feature_count + BIAS_ROWS
    half = chips * node_dev
    bf16, f32 = jnp.bfloat16, jnp.float32
    shape = jax.ShapeDtypeStruct
    degree_tiles = degree.reshape(per_shard, edge)
    tile_cost = pl.CostEstimate(
        flops=tile_row.size // (row_devices * col_devices) * edge * edge * feature_count,
        bytes_accessed=patterns.size * 2 + 4 * half * feature_count * 2,
        transcendentals=0,
    )

    scaled = pl.pallas_call(
        scale_kernel,
        out_shape=shape((4, node_dev, feature_count), bf16),
        in_specs=[HBM] * 2,
        out_specs=VMEM,
        scratch_shapes=[
            pltpu.VMEM(features.shape, bf16),
            pltpu.VMEM(degree_tiles.shape, jnp.int32),
            pltpu.SemaphoreType.DMA((2,)),
        ],
        compiler_params=PARAMS,
    )(features, degree_tiles)
    near_own = exchange(scaled, "row", axis_index_groups=row_near).reshape(half // 2, feature_count)
    near_other = lax.ppermute(near_own, "row", swap)
    far_own = lax.ppermute(near_own, "row", row_far)
    row_tiles, near_own = lax.optimization_barrier((tile_row.reshape(per_shard, edge), near_own))
    place = row.astype(jnp.int32).reshape(1)
    slots = pl.pallas_call(
        order_kernel,
        out_shape=shape((1, ORDERED), jnp.int32),
        in_specs=[SMEM] * 2 + [HBM] * 4,
        out_specs=VMEM,
        scratch_shapes=[
            pltpu.VMEM((4, per_shard, edge), jnp.int32),
            pltpu.SemaphoreType.DMA((4,)),
        ],
        compiler_params=PARAMS,
    )(
        place,
        tile_count,
        row_tiles,
        tile_col.reshape(per_shard, edge),
        tile_pattern.reshape(per_shard, edge),
        tile_weight.reshape(per_shard, edge),
    )
    forward_panel = pltpu.VMEM((half, feature_count), bf16)
    row_sums = shape((col_devices * node_dev, feature_count), f32)
    near_sums = pl.pallas_call(
        forward_near_kernel,
        out_shape=row_sums,
        in_specs=[SMEM] + [VMEM] * 3,
        out_specs=VMEM,
        scratch_shapes=[forward_panel],
        compiler_params=PARAMS,
        cost_estimate=tile_cost,
    )(slots, patterns, near_own, near_other)
    far_own, near_sums = lax.optimization_barrier((far_own, near_sums))
    far_other = lax.ppermute(far_own, "row", swap)
    row_part = pl.pallas_call(
        forward_far_kernel,
        out_shape=shape(row_sums.shape, bf16),
        in_specs=[SMEM] + [VMEM] * 4,
        out_specs=VMEM,
        scratch_shapes=[forward_panel, pltpu.VMEM(row_sums.shape, f32)],
        compiler_params=PARAMS,
        cost_estimate=tile_cost,
    )(slots, patterns, far_own, far_other, near_sums)
    parts = exchange(row_part.reshape(col_devices, node_dev, feature_count), "col")
    pre_act, upstream, keep_terms, send_terms = pl.pallas_call(
        middle_kernel,
        out_shape=(
            shape((node_dev, hidden), f32),
            shape((node_dev, hidden), f32),
            shape((extra, edge), f32),
            shape((extra, edge), bf16),
        ),
        in_specs=[SMEM] + [VMEM] * 5,
        out_specs=(VMEM,) * 4,
        compiler_params=PARAMS,
    )(place, parts, degree_tiles, cotangent, weight, layer_bias[None, :])
    got_terms = lax.ppermute(send_terms, "row", swap)
    spread = pl.pallas_call(
        spread_kernel,
        out_shape=shape((col_devices, node_dev + extra, edge), bf16),
        in_specs=[VMEM] * 2,
        out_specs=VMEM,
        compiler_params=PARAMS,
    )(upstream, weight)
    spread = pl.pallas_call(
        append_kernel,
        out_shape=shape(spread.shape, bf16),
        in_specs=[VMEM] * 3,
        out_specs=VMEM,
        input_output_aliases={2: 0},
        compiler_params=PARAMS,
    )(keep_terms, got_terms, spread)
    spread_all = exchange(spread, "col")
    keep, send, grads = pl.pallas_call(
        backward_kernel,
        out_shape=(
            shape((half, edge), f32),
            shape((half, edge), bf16),
            shape((extra, edge), bf16),
        ),
        in_specs=[SMEM] + [VMEM] * 2,
        out_specs=(VMEM,) * 3,
        scratch_shapes=[pltpu.VMEM((2 * half, edge), f32)],
        compiler_params=PARAMS,
        cost_estimate=tile_cost,
    )(slots, patterns, spread_all)
    got = lax.ppermute(send, "row", swap)
    pre_act, keep = lax.optimization_barrier((pre_act, keep))
    activations = pl.pallas_call(
        activation_kernel,
        out_shape=shape((node_dev, hidden), bf16),
        in_specs=[VMEM],
        out_specs=VMEM,
        compiler_params=PARAMS,
    )(pre_act)
    got, activations = lax.optimization_barrier((got, activations))
    joined = pl.pallas_call(
        join_kernel,
        out_shape=shape((chips, node_dev + extra, edge), bf16),
        in_specs=[VMEM] * 3,
        out_specs=VMEM,
        compiler_params=PARAMS,
    )(keep, got, grads)
    back_parts = exchange(joined, "row", axis_index_groups=same_core)
    scale_factor = 1.0 / math.sqrt(node_dev * row_devices * col_devices)
    mine = pl.pallas_call(
        functools.partial(total_kernel, scale_factor),
        out_shape=shape((feature_count + 8, edge), f32),
        in_specs=[VMEM],
        out_specs=VMEM,
        compiler_params=PARAMS,
    )(back_parts)
    other = lax.ppermute(mine, "row", swap)
    grad_features = pl.pallas_call(
        features_kernel,
        out_shape=shape((node_dev, feature_count), bf16),
        in_specs=[VMEM] * 2,
        out_specs=VMEM,
        compiler_params=PARAMS,
    )(back_parts, degree_tiles)
    grad_weight, grad_bias = pl.pallas_call(
        lay_out_kernel,
        out_shape=(shape((feature_count, hidden), f32), shape((1, hidden), f32)),
        in_specs=[SMEM] + [VMEM] * 2,
        out_specs=(VMEM,) * 2,
        compiler_params=PARAMS,
    )(place, mine, other)
    return (activations, grad_features, grad_weight, grad_bias[0])


def solution(mesh):
    in_specs = (
        P(("row", "col"), None),
        P(("row", "col")),
        P(("row", "col"), None),
        P(),
        P(),
        P(),
        P("row", "col", None),
        P("row", "col", None),
        P("row", "col", None),
        P("row", "col", None),
        P("row", "col"),
    )
    out_specs = (P(("row", "col"), None), P(("row", "col"), None), P(), P())
    return jax.shard_map(
        per_device, mesh=mesh, in_specs=in_specs, out_specs=out_specs, check_vma=False
    )
```

```python
import functools
import math

import jax
import jax.numpy as jnp
from jax import lax
from jax.experimental import pallas as pl
from jax.experimental.pallas import tpu as pltpu
from jax.sharding import PartitionSpec as P

GROUP = 64
VMEM_LIMIT = 20 * 1024 * 1024
ROOT_2_PI = math.sqrt(2.0 / math.pi)
CUBIC = 0.044715
BIAS_ROWS = 16
PER_SHARD = 4
CLASSES = 2
ORDERED = 640
BOUNDS = 600
PAIRS = (((0, 1), (2, 3)), ((0, 3), (1, 2)))
HBM = pl.BlockSpec(memory_space=pltpu.HBM)
VMEM = pl.BlockSpec(memory_space=pltpu.VMEM)
SMEM = pl.BlockSpec(memory_space=pltpu.SMEM)
PARAMS = pltpu.CompilerParams(vmem_limit_bytes=VMEM_LIMIT)


def pair_of(place, core):
    return jnp.where(core == 0, place >> 1, (place ^ (place >> 1)) & 1)


def pair_index(place, core):
    return jnp.where(core == 0, place & 1, place >> 1)


def far_neighbour(place, core):
    return place ^ 3 if core == 0 else place ^ 1


def order_kernel(
    place_ref, live_ref, row_hbm, col_hbm, pattern_hbm, weight_hbm, out_ref, fields, sems
):
    sources = (row_hbm, col_hbm, pattern_hbm, weight_hbm)
    copies = [
        pltpu.make_async_copy(source, fields.at[index], sems.at[index])
        for index, source in enumerate(sources)
    ]
    for copy in copies:
        copy.start()
    for copy in copies:
        copy.wait()
    row = place_ref[0]
    _, rows, edge = fields.shape
    tile_row, tile_col = fields[0], fields[1]
    shard = tile_col // PER_SHARD
    parity = shard % 2
    chip = shard // 2
    ring = chip % 4
    tile = tile_col % PER_SHARD
    half = parity ^ (row % 2)
    far = (pair_of(ring, parity) != pair_of((row // 2) % 4, parity)).astype(jnp.int32)
    rank = pair_index(ring, parity) * 2 + chip // 4
    place = (half * 4 + rank) * PER_SHARD + tile
    word = tile_row | (fields[2] << 5) | (fields[3] << 11) | (place << 14)
    slot = lax.broadcasted_iota(jnp.int32, (rows, edge), 0) * edge
    slot += lax.broadcasted_iota(jnp.int32, (rows, edge), 1)
    alive = slot < live_ref[0, 0]
    word = jnp.where(alive, word, 0)
    kind = jnp.where(alive, far, CLASSES)

    flags = [(kind == index).astype(jnp.float32) for index in range(CLASSES + 1)]
    stacked = jnp.concatenate(flags + [jnp.zeros((4, edge), jnp.float32)], 0)
    before = lax.broadcasted_iota(jnp.int32, (edge, edge), 0) < lax.broadcasted_iota(
        jnp.int32, (edge, edge), 1
    )
    earlier = jnp.dot(
        stacked.astype(jnp.bfloat16),
        before.astype(jnp.float32).astype(jnp.bfloat16),
        preferred_element_type=jnp.float32,
    )
    counts = jnp.sum(stacked, axis=1, keepdims=True)
    start = jnp.zeros((1, 1), jnp.float32)
    ends = []
    position = [jnp.zeros((1, edge), jnp.float32) for _ in range(rows)]
    for index in range(CLASSES + 1):
        for line in range(rows):
            at = index * rows + line
            position[line] += flags[index][line : line + 1] * (start + earlier[at : at + 1])
            start = start + counts[at : at + 1]
        ends.append(start)
    turned = jnp.concatenate(position + [jnp.zeros((8 - rows, edge), jnp.float32)], 0).T
    slots = rows * edge
    lanes = lax.broadcasted_iota(jnp.int32, (edge, slots), 1).astype(jnp.float32)
    pieces = jnp.zeros((8, slots), jnp.float32)
    for line in range(rows):
        chosen = (turned[:, line : line + 1] == lanes).astype(jnp.float32).astype(jnp.bfloat16)
        parts = [(word[line : line + 1] >> shift) & 127 for shift in (0, 7, 14)]
        parts = jnp.concatenate(parts + [jnp.zeros((5, edge), jnp.int32)], 0)
        parts = parts.astype(jnp.float32).astype(jnp.bfloat16)
        pieces += jnp.dot(parts, chosen, preferred_element_type=jnp.float32)
    pieces = pieces.astype(jnp.int32)
    out_ref[:, :slots] = pieces[0:1] | (pieces[1:2] << 7) | (pieces[2:3] << 14)
    lane = lax.broadcasted_iota(jnp.int32, (1, out_ref.shape[1] - slots), 1) + slots
    tail = jnp.zeros(lane.shape, jnp.int32)
    for index in range(CLASSES):
        tail = jnp.where(lane == BOUNDS + index, ends[index].astype(jnp.int32), tail)
    out_ref[:, slots:] = tail


def root_columns(degree):
    rows = lax.rsqrt(degree.astype(jnp.float32))
    rows = jnp.concatenate([rows, jnp.ones((8 - rows.shape[0], rows.shape[1]), jnp.float32)], 0)
    return rows.T


def scale_kernel(features_hbm, degree_hbm, out_ref, features_ref, degree_ref, sems):
    copies = (
        pltpu.make_async_copy(degree_hbm, degree_ref, sems.at[0]),
        pltpu.make_async_copy(features_hbm, features_ref, sems.at[1]),
    )
    for copy in copies:
        copy.start()
    copies[0].wait()
    roots = root_columns(degree_ref[...])
    copies[1].wait()
    edge = degree_ref.shape[1]
    for tile in range(degree_ref.shape[0]):
        rows = pl.ds(tile * edge, edge)
        scaled = features_ref[rows, :].astype(jnp.float32) * roots[:, tile : tile + 1]
        scaled = scaled.astype(jnp.bfloat16)
        for copy in range(out_ref.shape[0]):
            out_ref[copy, rows, :] = scaled


def add_products(slots_ref, first, end, product_of, place_of, sums):
    edge = sums.shape[1]

    def one_group(turn, carry):
        terms = []
        for member in range(GROUP):
            slot = first + turn * GROUP + member
            word = slots_ref[0, slot]
            factor = jnp.where(slot < end, (word >> 11) & 7, 0).astype(jnp.float32)
            terms.append((place_of(word), factor, product_of(word)))
        for place, factor, product in terms:
            rows = pl.ds(pl.multiple_of(place * edge, edge), edge)
            sums[rows, :] += factor * product
        return carry

    lax.fori_loop(0, (end - first + GROUP - 1) // GROUP, one_group, 0)


def tile_of(ref, place, edge):
    return ref[pl.ds(pl.multiple_of(place * edge, edge), edge), :]


def forward_sums(slots_ref, patterns_ref, own_ref, other_ref, panel, sums, far):
    edge = patterns_ref.shape[1]
    half = own_ref.shape[0]
    panel[:half, :] = own_ref[...]
    panel[half:, :] = other_ref[...]
    middle, end = slots_ref[0, BOUNDS], slots_ref[0, BOUNDS + 1]

    def product_of(word):
        return jnp.dot(
            patterns_ref[(word >> 5) & 63],
            tile_of(panel, (word >> 14) & 31, edge),
            preferred_element_type=jnp.float32,
        )

    first, end = (middle, end) if far else (0, middle)
    add_products(slots_ref, first, end, product_of, lambda word: word & 31, sums)


def forward_near_kernel(slots_ref, patterns_ref, own_ref, other_ref, out_ref, panel):
    out_ref[...] = jnp.zeros_like(out_ref)
    forward_sums(slots_ref, patterns_ref, own_ref, other_ref, panel, out_ref, False)


def forward_far_kernel(slots_ref, patterns_ref, own_ref, other_ref, so_far_ref, out_ref, panel, sums):
    sums[...] = so_far_ref[...]
    forward_sums(slots_ref, patterns_ref, own_ref, other_ref, panel, sums, True)
    out_ref[...] = sums[...].astype(jnp.bfloat16)


def backward_sums(slots_ref, patterns_ref, spread_ref, keep_ref, send_ref, sums, far):
    edge = patterns_ref.shape[1]
    half = sums.shape[0] // 2
    sums[...] = jnp.zeros_like(sums)
    middle, end = slots_ref[0, BOUNDS], slots_ref[0, BOUNDS + 1]

    def product_of(word):
        start = pl.multiple_of((word & 3) * edge, edge)
        return jnp.dot(
            spread_ref[(word >> 2) & 7, pl.ds(start, edge), :],
            patterns_ref[(word >> 5) & 63],
            preferred_element_type=jnp.float32,
        )

    first, end = (middle, end) if far else (0, middle)
    add_products(slots_ref, first, end, product_of, lambda word: (word >> 14) & 31, sums)
    keep_ref[...] = sums[:half, :]
    send_ref[...] = sums[half:, :].astype(jnp.bfloat16)


def backward_far_kernel(slots_ref, patterns_ref, spread_ref, keep_ref, send_ref, grads_ref, sums):
    backward_sums(slots_ref, patterns_ref, spread_ref, keep_ref, send_ref, sums, True)
    own = spread_ref.shape[1] - grads_ref.shape[0]
    grads = spread_ref[0, own:, :].astype(jnp.float32)
    for shard in range(1, spread_ref.shape[0]):
        grads += spread_ref[shard, own:, :].astype(jnp.float32)
    grads_ref[...] = grads.astype(jnp.bfloat16)


def backward_near_kernel(slots_ref, patterns_ref, spread_ref, keep_ref, send_ref, sums):
    backward_sums(slots_ref, patterns_ref, spread_ref, keep_ref, send_ref, sums, False)


def split_product(left, right, dims):
    high = left.astype(jnp.bfloat16)
    low = (left - high.astype(jnp.float32)).astype(jnp.bfloat16)
    return lax.dot_general(
        high, right, (dims, ((), ())), preferred_element_type=jnp.float32
    ) + lax.dot_general(low, right, (dims, ((), ())), preferred_element_type=jnp.float32)


def activate(pre_act):
    square = pre_act * pre_act
    bent = jnp.tanh(ROOT_2_PI * (pre_act + CUBIC * (pre_act * square)))
    return square, bent, 0.5 * (1.0 + bent)


def middle_kernel(
    place_ref,
    parts_ref,
    degree_ref,
    cotangent_ref,
    weight_ref,
    bias_ref,
    pre_ref,
    upstream_ref,
    keep_ref,
    send_ref,
):
    tiles, edge = degree_ref.shape
    shards = parts_ref.shape[0]
    weight = weight_ref[...]
    height = weight.shape[0]
    roots = root_columns(degree_ref[...])
    grads = jnp.zeros(weight.shape, jnp.float32)
    bias_row = jnp.zeros(bias_ref.shape, jnp.float32)
    for tile in range(tiles):
        rows = pl.ds(tile * edge, edge)
        sums = parts_ref[0, rows, :].astype(jnp.float32)
        for shard in range(1, shards):
            sums += parts_ref[shard, rows, :].astype(jnp.float32)
        inv_root = roots[:, tile : tile + 1]
        pre_act = inv_root * split_product(sums, weight, ((1,), (0,))) + bias_ref[...]
        pre_ref[rows, :] = pre_act
        square, bent, half = activate(pre_act)
        rise = 0.5 * pre_act * (1.0 - bent * bent) * (ROOT_2_PI * (1.0 + 3.0 * CUBIC * square))
        slope = cotangent_ref[rows, :].astype(jnp.float32) * (half + rise)
        upstream = inv_root * slope
        upstream_ref[rows, :] = upstream
        grads += split_product(sums, upstream.astype(jnp.bfloat16), ((0,), (0,)))
        bias_row += jnp.sum(slope, axis=0, keepdims=True)
    width = keep_ref.shape[1]
    bias_high = bias_row.astype(jnp.bfloat16).astype(jnp.float32)
    bias_low = bias_row - bias_high
    first = place_ref[0] % 2 == 0

    def put(target, left):
        pick = lambda whole: jnp.where(left, whole[:, :width], whole[:, width:])
        target[:height, :] = pick(grads).astype(target.dtype)
        row_ids = lax.broadcasted_iota(jnp.int32, (BIAS_ROWS, width), 0)
        block = jnp.where(row_ids == 0, pick(bias_high), 0.0)
        block = jnp.where(row_ids == 1, pick(bias_low), block)
        target[height:, :] = block.astype(target.dtype)

    put(keep_ref, first)
    put(send_ref, jnp.logical_not(first))


def activation_kernel(pre_ref, act_ref):
    pre_act = pre_ref[...]
    act_ref[...] = (pre_act * activate(pre_act)[2]).astype(jnp.bfloat16)


def spread_kernel(upstream_ref, weight_ref, out_ref):
    edge = out_ref.shape[2]
    for tile in range(upstream_ref.shape[0] // edge):
        rows = pl.ds(tile * edge, edge)
        upstream = upstream_ref[rows, :]
        high = upstream.astype(jnp.bfloat16)
        low = (upstream - high.astype(jnp.float32)).astype(jnp.bfloat16)
        spread = sum(
            lax.dot_general(
                weight_ref[...], part, (((1,), (1,)), ((), ())), preferred_element_type=jnp.float32
            )
            for part in (high, low)
        ).astype(jnp.bfloat16)
        for shard in range(out_ref.shape[0]):
            out_ref[shard, rows, :] = spread


def append_kernel(keep_ref, got_ref, spread_ref, out_ref):
    terms = (keep_ref[...] + got_ref[...].astype(jnp.float32)).astype(jnp.bfloat16)
    rows = pl.ds(out_ref.shape[1] - terms.shape[0], terms.shape[0])
    for shard in range(out_ref.shape[0]):
        out_ref[shard, rows, :] = terms


def sum_of_four(parts_ref, rows):
    part = lambda index: parts_ref[index, rows, :].astype(jnp.float32)
    return (part(0) + part(2)) + (part(1) + part(3))


def far_join_kernel(keep_ref, got_ref, grads_ref, out_ref):
    half = keep_ref.shape[0]
    out_ref[:half, :] = (keep_ref[...] + got_ref[...].astype(jnp.float32)).astype(jnp.bfloat16)
    out_ref[half:, :] = grads_ref[...]


def near_join_kernel(keep_ref, got_ref, far_ref, grads_ref, out_ref):
    shards = out_ref.shape[0]
    half = keep_ref.shape[0]
    own = half // shards
    grads = grads_ref[...].astype(jnp.float32) + far_ref[half:, :].astype(jnp.float32)
    grads = grads.astype(jnp.bfloat16)
    for shard in range(shards):
        rows = pl.ds(shard * own, own)
        total = keep_ref[rows, :] + got_ref[rows, :].astype(jnp.float32)
        total += far_ref[rows, :].astype(jnp.float32)
        out_ref[shard, pl.ds(0, own), :] = total.astype(jnp.bfloat16)
        out_ref[shard, pl.ds(own, grads.shape[0]), :] = grads


def total_kernel(scale_factor, parts_ref, half_ref):
    extra = half_ref.shape[0] - 8 + BIAS_ROWS
    tail = sum_of_four(parts_ref, pl.ds(parts_ref.shape[1] - extra, extra))
    tail = tail * scale_factor
    height = half_ref.shape[0] - 8
    half_ref[:height, :] = tail[:height, :]
    bias_row = tail[height : height + 1, :] + tail[height + 1 : height + 2, :]
    half_ref[height:, :] = jnp.broadcast_to(bias_row, (8, bias_row.shape[1]))


def features_kernel(parts_ref, degree_ref, features_ref):
    tiles, edge = degree_ref.shape
    roots = lax.rsqrt(degree_ref[...].astype(jnp.float32))
    for tile in range(tiles):
        rows = pl.ds(tile * edge, edge)
        total = sum_of_four(parts_ref, rows)
        features_ref[rows, :] = (total * roots[tile : tile + 1, :]).T.astype(jnp.bfloat16)


def lay_out_kernel(place_ref, mine_ref, other_ref, grads_ref, bias_ref):
    first = place_ref[0] % 2 == 0
    height = grads_ref.shape[0]
    width = mine_ref.shape[1]
    mine, other = mine_ref[...], other_ref[...]
    halves = (jnp.where(first, mine, other), jnp.where(first, other, mine))
    for index, half in enumerate(halves):
        lanes = pl.ds(index * width, width)
        grads_ref[:, lanes] = half[:height, :]
        bias_ref[:, lanes] = half[height : height + 1, :]


def per_device(
    features,
    degree,
    cotangent,
    weight,
    layer_bias,
    patterns,
    tile_row,
    tile_col,
    tile_pattern,
    tile_weight,
    tile_count,
):
    node_dev, feature_count = features.shape
    hidden = weight.shape[1]
    row_devices = lax.axis_size("row")
    col_devices = lax.axis_size("col")
    chips = row_devices // 2
    edge = patterns.shape[1]
    per_shard = node_dev // edge
    row = lax.axis_index("row")
    swap = [(index, index ^ 1) for index in range(row_devices)]
    row_near = [
        [(low * 4 + ring) * 2 + core_index for ring in pair for low in range(2)]
        for core_index in range(2)
        for pair in PAIRS[core_index]
    ]
    row_far = [
        (index, (index // 8 * 4 + far_neighbour(index // 2 % 4, index % 2)) * 2 + index % 2)
        for index in range(row_devices)
    ]
    exchange = functools.partial(lax.all_to_all, split_axis=0, concat_axis=0)
    extra = feature_count + BIAS_ROWS
    half = chips * node_dev
    bf16, f32 = jnp.bfloat16, jnp.float32
    shape = jax.ShapeDtypeStruct
    degree_tiles = degree.reshape(per_shard, edge)
    tile_cost = pl.CostEstimate(
        flops=tile_row.size // (row_devices * col_devices) * edge * edge * feature_count,
        bytes_accessed=patterns.size * 2 + 4 * half * feature_count * 2,
        transcendentals=0,
    )

    scaled = pl.pallas_call(
        scale_kernel,
        out_shape=shape((4, node_dev, feature_count), bf16),
        in_specs=[HBM] * 2,
        out_specs=VMEM,
        scratch_shapes=[
            pltpu.VMEM(features.shape, bf16),
            pltpu.VMEM(degree_tiles.shape, jnp.int32),
            pltpu.SemaphoreType.DMA((2,)),
        ],
        compiler_params=PARAMS,
    )(features, degree_tiles)
    near_own = exchange(scaled, "row", axis_index_groups=row_near).reshape(half // 2, feature_count)
    near_other = lax.ppermute(near_own, "row", swap)
    far_own = lax.ppermute(near_own, "row", row_far)
    row_tiles, near_own = lax.optimization_barrier((tile_row.reshape(per_shard, edge), near_own))
    place = row.astype(jnp.int32).reshape(1)
    slots = pl.pallas_call(
        order_kernel,
        out_shape=shape((1, ORDERED), jnp.int32),
        in_specs=[SMEM] * 2 + [HBM] * 4,
        out_specs=VMEM,
        scratch_shapes=[
            pltpu.VMEM((4, per_shard, edge), jnp.int32),
            pltpu.SemaphoreType.DMA((4,)),
        ],
        compiler_params=PARAMS,
    )(
        place,
        tile_count,
        row_tiles,
        tile_col.reshape(per_shard, edge),
        tile_pattern.reshape(per_shard, edge),
        tile_weight.reshape(per_shard, edge),
    )
    forward_panel = pltpu.VMEM((half, feature_count), bf16)
    row_sums = shape((col_devices * node_dev, feature_count), f32)
    near_sums = pl.pallas_call(
        forward_near_kernel,
        out_shape=row_sums,
        in_specs=[SMEM] + [VMEM] * 3,
        out_specs=VMEM,
        scratch_shapes=[forward_panel],
        compiler_params=PARAMS,
        cost_estimate=tile_cost,
    )(slots, patterns, near_own, near_other)
    far_own, near_sums = lax.optimization_barrier((far_own, near_sums))
    far_other = lax.ppermute(far_own, "row", swap)
    row_part = pl.pallas_call(
        forward_far_kernel,
        out_shape=shape(row_sums.shape, bf16),
        in_specs=[SMEM] + [VMEM] * 4,
        out_specs=VMEM,
        scratch_shapes=[forward_panel, pltpu.VMEM(row_sums.shape, f32)],
        compiler_params=PARAMS,
        cost_estimate=tile_cost,
    )(slots, patterns, far_own, far_other, near_sums)
    parts = exchange(row_part.reshape(col_devices, node_dev, feature_count), "col")
    pre_act, upstream, keep_terms, send_terms = pl.pallas_call(
        middle_kernel,
        out_shape=(
            shape((node_dev, hidden), f32),
            shape((node_dev, hidden), f32),
            shape((extra, edge), f32),
            shape((extra, edge), bf16),
        ),
        in_specs=[SMEM] + [VMEM] * 5,
        out_specs=(VMEM,) * 4,
        compiler_params=PARAMS,
    )(place, parts, degree_tiles, cotangent, weight, layer_bias[None, :])
    got_terms = lax.ppermute(send_terms, "row", swap)
    spread = pl.pallas_call(
        spread_kernel,
        out_shape=shape((col_devices, node_dev + extra, edge), bf16),
        in_specs=[VMEM] * 2,
        out_specs=VMEM,
        compiler_params=PARAMS,
    )(upstream, weight)
    spread = pl.pallas_call(
        append_kernel,
        out_shape=shape(spread.shape, bf16),
        in_specs=[VMEM] * 3,
        out_specs=VMEM,
        input_output_aliases={2: 0},
        compiler_params=PARAMS,
    )(keep_terms, got_terms, spread)
    spread_all = exchange(spread, "col")
    kept, sent = shape((half // 2, edge), f32), shape((half // 2, edge), bf16)
    keep, send, grads = pl.pallas_call(
        backward_far_kernel,
        out_shape=(kept, sent, shape((extra, edge), bf16)),
        in_specs=[SMEM] + [VMEM] * 2,
        out_specs=(VMEM,) * 3,
        scratch_shapes=[pltpu.VMEM((half, edge), f32)],
        compiler_params=PARAMS,
        cost_estimate=tile_cost,
    )(slots, patterns, spread_all)
    got = lax.ppermute(send, "row", swap)
    pre_act, keep = lax.optimization_barrier((pre_act, keep))
    activations = pl.pallas_call(
        activation_kernel,
        out_shape=shape((node_dev, hidden), bf16),
        in_specs=[VMEM],
        out_specs=VMEM,
        compiler_params=PARAMS,
    )(pre_act)
    got, activations = lax.optimization_barrier((got, activations))
    far_sums = pl.pallas_call(
        far_join_kernel,
        out_shape=shape((half // 2 + extra, edge), bf16),
        in_specs=[VMEM] * 3,
        out_specs=VMEM,
        compiler_params=PARAMS,
    )(keep, got, grads)
    far_sums, spread_all = lax.optimization_barrier((far_sums, spread_all))
    far_got = lax.ppermute(far_sums, "row", row_far)
    keep, send = pl.pallas_call(
        backward_near_kernel,
        out_shape=(kept, sent),
        in_specs=[SMEM] + [VMEM] * 2,
        out_specs=(VMEM,) * 2,
        scratch_shapes=[pltpu.VMEM((half, edge), f32)],
        compiler_params=PARAMS,
        cost_estimate=tile_cost,
    )(slots, patterns, spread_all)
    got = lax.ppermute(send, "row", swap)
    got, far_got = lax.optimization_barrier((got, far_got))
    joined = pl.pallas_call(
        near_join_kernel,
        out_shape=shape((4, node_dev + extra, edge), bf16),
        in_specs=[VMEM] * 4,
        out_specs=VMEM,
        compiler_params=PARAMS,
    )(keep, got, far_got, grads)
    back_parts = exchange(joined, "row", axis_index_groups=row_near)
    scale_factor = 1.0 / math.sqrt(node_dev * row_devices * col_devices)
    mine = pl.pallas_call(
        functools.partial(total_kernel, scale_factor),
        out_shape=shape((feature_count + 8, edge), f32),
        in_specs=[VMEM],
        out_specs=VMEM,
        compiler_params=PARAMS,
    )(back_parts)
    other = lax.ppermute(mine, "row", swap)
    grad_features = pl.pallas_call(
        features_kernel,
        out_shape=shape((node_dev, feature_count), bf16),
        in_specs=[VMEM] * 2,
        out_specs=VMEM,
        compiler_params=PARAMS,
    )(back_parts, degree_tiles)
    grad_weight, grad_bias = pl.pallas_call(
        lay_out_kernel,
        out_shape=(shape((feature_count, hidden), f32), shape((1, hidden), f32)),
        in_specs=[SMEM] + [VMEM] * 2,
        out_specs=(VMEM,) * 2,
        compiler_params=PARAMS,
    )(place, mine, other)
    return (activations, grad_features, grad_weight, grad_bias[0])


def solution(mesh):
    in_specs = (
        P(("row", "col"), None),
        P(("row", "col")),
        P(("row", "col"), None),
        P(),
        P(),
        P(),
        P("row", "col", None),
        P("row", "col", None),
        P("row", "col", None),
        P("row", "col", None),
        P("row", "col"),
    )
    out_specs = (P(("row", "col"), None), P(("row", "col"), None), P(), P())
    return jax.shard_map(
        per_device, mesh=mesh, in_specs=in_specs, out_specs=out_specs, check_vma=False
    )
```

```python
import functools
import math

import jax
import jax.numpy as jnp
from jax import lax
from jax.experimental import pallas as pl
from jax.experimental.pallas import tpu as pltpu
from jax.sharding import PartitionSpec as P

GROUP = 64
VMEM_LIMIT = 20 * 1024 * 1024
ROOT_2_PI = math.sqrt(2.0 / math.pi)
CUBIC = 0.044715
BIAS_ROWS = 16
PER_SHARD = 4
CLASSES = 4
ORDERED = 640
BOUNDS = 600
PAIRS = (((0, 1), (2, 3)), ((0, 3), (1, 2)))
HBM = pl.BlockSpec(memory_space=pltpu.HBM)
VMEM = pl.BlockSpec(memory_space=pltpu.VMEM)
SMEM = pl.BlockSpec(memory_space=pltpu.SMEM)
PARAMS = pltpu.CompilerParams(vmem_limit_bytes=VMEM_LIMIT)


def pair_of(place, core):
    return jnp.where(core == 0, place >> 1, (place ^ (place >> 1)) & 1)


def pair_index(place, core):
    return jnp.where(core == 0, place & 1, place >> 1)


def far_neighbour(place, core):
    return place ^ 3 if core == 0 else place ^ 1


def order_kernel(
    place_ref, live_ref, row_hbm, col_hbm, pattern_hbm, weight_hbm, out_ref, fields, sems
):
    sources = (row_hbm, col_hbm, pattern_hbm, weight_hbm)
    copies = [
        pltpu.make_async_copy(source, fields.at[index], sems.at[index])
        for index, source in enumerate(sources)
    ]
    for copy in copies:
        copy.start()
    for copy in copies:
        copy.wait()
    row, col = place_ref[0], place_ref[1]
    core = row % 2
    _, rows, edge = fields.shape
    tile_row, tile_col = fields[0], fields[1]
    shard = tile_col // PER_SHARD
    parity = shard % 2
    chip = shard // 2
    ring = chip % 4
    tile = tile_col % PER_SHARD
    half = parity ^ core
    far = (pair_of(ring, parity) != pair_of((row // 2) % 4, parity)).astype(jnp.int32)
    rank = pair_index(ring, parity) * 2 + chip // 4
    place = (half * 4 + rank) * PER_SHARD + tile
    peer = tile_row // PER_SHARD
    row_far = (pair_of(peer // 2, core) != pair_of(col // 2, core)).astype(jnp.int32)
    rank = pair_index(peer // 2, core) * 2 + peer % 2
    target = (row_far * 4 + rank) * PER_SHARD + tile_row % PER_SHARD
    word = tile_row | (fields[2] << 5) | (fields[3] << 11) | (place << 14) | (target << 19)
    slot = lax.broadcasted_iota(jnp.int32, (rows, edge), 0) * edge
    slot += lax.broadcasted_iota(jnp.int32, (rows, edge), 1)
    alive = slot < live_ref[0, 0]
    word = jnp.where(alive, word, 0)
    kind = jnp.where(alive, far * 2 + row_far, CLASSES)

    flags = [(kind == index).astype(jnp.float32) for index in range(CLASSES + 1)]
    stacked = jnp.concatenate(flags + [jnp.zeros((4, edge), jnp.float32)], 0)
    before = lax.broadcasted_iota(jnp.int32, (edge, edge), 0) < lax.broadcasted_iota(
        jnp.int32, (edge, edge), 1
    )
    earlier = jnp.dot(
        stacked.astype(jnp.bfloat16),
        before.astype(jnp.float32).astype(jnp.bfloat16),
        preferred_element_type=jnp.float32,
    )
    counts = jnp.sum(stacked, axis=1, keepdims=True)
    start = jnp.zeros((1, 1), jnp.float32)
    ends = []
    position = [jnp.zeros((1, edge), jnp.float32) for _ in range(rows)]
    for index in range(CLASSES + 1):
        for line in range(rows):
            at = index * rows + line
            position[line] += flags[index][line : line + 1] * (start + earlier[at : at + 1])
            start = start + counts[at : at + 1]
        ends.append(start)
    turned = jnp.concatenate(position + [jnp.zeros((8 - rows, edge), jnp.float32)], 0).T
    slots = rows * edge
    lanes = lax.broadcasted_iota(jnp.int32, (edge, slots), 1).astype(jnp.float32)
    pieces = jnp.zeros((8, slots), jnp.float32)
    for line in range(rows):
        chosen = (turned[:, line : line + 1] == lanes).astype(jnp.float32).astype(jnp.bfloat16)
        parts = [(word[line : line + 1] >> shift) & 127 for shift in (0, 7, 14, 21)]
        parts = jnp.concatenate(parts + [jnp.zeros((4, edge), jnp.int32)], 0)
        parts = parts.astype(jnp.float32).astype(jnp.bfloat16)
        pieces += jnp.dot(parts, chosen, preferred_element_type=jnp.float32)
    pieces = pieces.astype(jnp.int32)
    out_ref[:, :slots] = (
        pieces[0:1] | (pieces[1:2] << 7) | (pieces[2:3] << 14) | (pieces[3:4] << 21)
    )
    lane = lax.broadcasted_iota(jnp.int32, (1, out_ref.shape[1] - slots), 1) + slots
    tail = jnp.zeros(lane.shape, jnp.int32)
    for index in range(CLASSES):
        tail = jnp.where(lane == BOUNDS + index, ends[index].astype(jnp.int32), tail)
    out_ref[:, slots:] = tail


def root_columns(degree):
    rows = lax.rsqrt(degree.astype(jnp.float32))
    rows = jnp.concatenate([rows, jnp.ones((8 - rows.shape[0], rows.shape[1]), jnp.float32)], 0)
    return rows.T


def scale_kernel(features_hbm, degree_hbm, out_ref, features_ref, degree_ref, sems):
    copies = (
        pltpu.make_async_copy(degree_hbm, degree_ref, sems.at[0]),
        pltpu.make_async_copy(features_hbm, features_ref, sems.at[1]),
    )
    for copy in copies:
        copy.start()
    copies[0].wait()
    roots = root_columns(degree_ref[...])
    copies[1].wait()
    edge = degree_ref.shape[1]
    for tile in range(degree_ref.shape[0]):
        rows = pl.ds(tile * edge, edge)
        scaled = features_ref[rows, :].astype(jnp.float32) * roots[:, tile : tile + 1]
        scaled = scaled.astype(jnp.bfloat16)
        for copy in range(out_ref.shape[0]):
            out_ref[copy, rows, :] = scaled


def add_products(slots_ref, first, end, product_of, place_of, sums):
    edge = sums.shape[1]

    def one_group(turn, carry):
        terms = []
        for member in range(GROUP):
            slot = first + turn * GROUP + member
            word = slots_ref[0, slot]
            factor = jnp.where(slot < end, (word >> 11) & 7, 0).astype(jnp.float32)
            terms.append((place_of(word), factor, product_of(word)))
        for place, factor, product in terms:
            rows = pl.ds(pl.multiple_of(place * edge, edge), edge)
            sums[rows, :] += factor * product
        return carry

    lax.fori_loop(0, (end - first + GROUP - 1) // GROUP, one_group, 0)


def tile_of(ref, place, edge):
    return ref[pl.ds(pl.multiple_of(place * edge, edge), edge), :]


def class_end(slots_ref, index):
    return slots_ref[0, BOUNDS + index]


def forward_sums(slots_ref, patterns_ref, own_ref, other_ref, panel, sums, first, end):
    edge = patterns_ref.shape[1]
    half = own_ref.shape[0]
    panel[:half, :] = own_ref[...]
    panel[half:, :] = other_ref[...]
    mask = sums.shape[0] // edge - 1

    def product_of(word):
        return jnp.dot(
            patterns_ref[(word >> 5) & 63],
            tile_of(panel, (word >> 14) & 31, edge),
            preferred_element_type=jnp.float32,
        )

    add_products(slots_ref, first, end, product_of, lambda word: (word >> 19) & mask, sums)


def forward_near_kernel(slots_ref, patterns_ref, own_ref, other_ref, out_ref, panel):
    out_ref[...] = jnp.zeros_like(out_ref)
    end = class_end(slots_ref, 1)
    forward_sums(slots_ref, patterns_ref, own_ref, other_ref, panel, out_ref, 0, end)


def forward_send_kernel(
    slots_ref, patterns_ref, own_ref, other_ref, so_far_ref, out_ref, panel, sums
):
    sums[...] = so_far_ref[sums.shape[0] :, :]
    first, end = class_end(slots_ref, 2), class_end(slots_ref, 3)
    forward_sums(slots_ref, patterns_ref, own_ref, other_ref, panel, sums, first, end)
    out_ref[...] = sums[...].astype(jnp.bfloat16)


def forward_keep_kernel(slots_ref, patterns_ref, own_ref, other_ref, so_far_ref, out_ref, panel):
    out_ref[...] = so_far_ref[: out_ref.shape[0], :]
    first, end = class_end(slots_ref, 1), class_end(slots_ref, 2)
    forward_sums(slots_ref, patterns_ref, own_ref, other_ref, panel, out_ref, first, end)


def row_join_kernel(keep_ref, got_ref, out_ref):
    shards, own, _ = out_ref.shape
    for shard in range(shards):
        rows = pl.ds(shard * own, own)
        total = keep_ref[rows, :] + got_ref[rows, :].astype(jnp.float32)
        out_ref[shard] = total.astype(jnp.bfloat16)


def backward_sums(slots_ref, patterns_ref, spread_ref, keep_ref, send_ref, sums, far):
    edge = patterns_ref.shape[1]
    half = sums.shape[0] // 2
    sums[...] = jnp.zeros_like(sums)
    middle, end = class_end(slots_ref, 1), class_end(slots_ref, 3)

    def product_of(word):
        start = pl.multiple_of((word & 3) * edge, edge)
        return jnp.dot(
            spread_ref[(word >> 2) & 7, pl.ds(start, edge), :],
            patterns_ref[(word >> 5) & 63],
            preferred_element_type=jnp.float32,
        )

    first, end = (middle, end) if far else (0, middle)
    add_products(slots_ref, first, end, product_of, lambda word: (word >> 14) & 31, sums)
    keep_ref[...] = sums[:half, :]
    send_ref[...] = sums[half:, :].astype(jnp.bfloat16)


def backward_far_kernel(slots_ref, patterns_ref, spread_ref, keep_ref, send_ref, grads_ref, sums):
    backward_sums(slots_ref, patterns_ref, spread_ref, keep_ref, send_ref, sums, True)
    own = spread_ref.shape[1] - grads_ref.shape[0]
    grads = spread_ref[0, own:, :].astype(jnp.float32)
    for shard in range(1, spread_ref.shape[0]):
        grads += spread_ref[shard, own:, :].astype(jnp.float32)
    grads_ref[...] = grads.astype(jnp.bfloat16)


def backward_near_kernel(slots_ref, patterns_ref, spread_ref, keep_ref, send_ref, sums):
    backward_sums(slots_ref, patterns_ref, spread_ref, keep_ref, send_ref, sums, False)


def split_product(left, right, dims):
    high = left.astype(jnp.bfloat16)
    low = (left - high.astype(jnp.float32)).astype(jnp.bfloat16)
    return lax.dot_general(
        high, right, (dims, ((), ())), preferred_element_type=jnp.float32
    ) + lax.dot_general(low, right, (dims, ((), ())), preferred_element_type=jnp.float32)


def activate(pre_act):
    square = pre_act * pre_act
    bent = jnp.tanh(ROOT_2_PI * (pre_act + CUBIC * (pre_act * square)))
    return square, bent, 0.5 * (1.0 + bent)


def middle_kernel(
    place_ref,
    parts_ref,
    degree_ref,
    cotangent_ref,
    weight_ref,
    bias_ref,
    pre_ref,
    upstream_ref,
    keep_ref,
    send_ref,
):
    tiles, edge = degree_ref.shape
    shards = parts_ref.shape[0]
    weight = weight_ref[...]
    height = weight.shape[0]
    roots = root_columns(degree_ref[...])
    grads = jnp.zeros(weight.shape, jnp.float32)
    bias_row = jnp.zeros(bias_ref.shape, jnp.float32)
    for tile in range(tiles):
        rows = pl.ds(tile * edge, edge)
        sums = parts_ref[0, rows, :].astype(jnp.float32)
        for shard in range(1, shards):
            sums += parts_ref[shard, rows, :].astype(jnp.float32)
        inv_root = roots[:, tile : tile + 1]
        pre_act = inv_root * split_product(sums, weight, ((1,), (0,))) + bias_ref[...]
        pre_ref[rows, :] = pre_act
        square, bent, half = activate(pre_act)
        rise = 0.5 * pre_act * (1.0 - bent * bent) * (ROOT_2_PI * (1.0 + 3.0 * CUBIC * square))
        slope = cotangent_ref[rows, :].astype(jnp.float32) * (half + rise)
        upstream = inv_root * slope
        upstream_ref[rows, :] = upstream
        grads += split_product(sums, upstream.astype(jnp.bfloat16), ((0,), (0,)))
        bias_row += jnp.sum(slope, axis=0, keepdims=True)
    width = keep_ref.shape[1]
    bias_high = bias_row.astype(jnp.bfloat16).astype(jnp.float32)
    bias_low = bias_row - bias_high
    first = place_ref[0] % 2 == 0

    def put(target, left):
        pick = lambda whole: jnp.where(left, whole[:, :width], whole[:, width:])
        target[:height, :] = pick(grads).astype(target.dtype)
        row_ids = lax.broadcasted_iota(jnp.int32, (BIAS_ROWS, width), 0)
        block = jnp.where(row_ids == 0, pick(bias_high), 0.0)
        block = jnp.where(row_ids == 1, pick(bias_low), block)
        target[height:, :] = block.astype(target.dtype)

    put(keep_ref, first)
    put(send_ref, jnp.logical_not(first))


def activation_kernel(pre_ref, act_ref):
    pre_act = pre_ref[...]
    act_ref[...] = (pre_act * activate(pre_act)[2]).astype(jnp.bfloat16)


def spread_kernel(upstream_ref, weight_ref, out_ref):
    edge = out_ref.shape[2]
    for tile in range(upstream_ref.shape[0] // edge):
        rows = pl.ds(tile * edge, edge)
        upstream = upstream_ref[rows, :]
        high = upstream.astype(jnp.bfloat16)
        low = (upstream - high.astype(jnp.float32)).astype(jnp.bfloat16)
        spread = sum(
            lax.dot_general(
                weight_ref[...], part, (((1,), (1,)), ((), ())), preferred_element_type=jnp.float32
            )
            for part in (high, low)
        ).astype(jnp.bfloat16)
        for shard in range(out_ref.shape[0]):
            out_ref[shard, rows, :] = spread


def append_kernel(keep_ref, got_ref, spread_ref, out_ref):
    terms = (keep_ref[...] + got_ref[...].astype(jnp.float32)).astype(jnp.bfloat16)
    rows = pl.ds(out_ref.shape[1] - terms.shape[0], terms.shape[0])
    for shard in range(out_ref.shape[0]):
        out_ref[shard, rows, :] = terms


def sum_of_four(parts_ref, rows):
    part = lambda index: parts_ref[index, rows, :].astype(jnp.float32)
    return (part(0) + part(2)) + (part(1) + part(3))


def far_join_kernel(keep_ref, got_ref, grads_ref, out_ref):
    half = keep_ref.shape[0]
    out_ref[:half, :] = (keep_ref[...] + got_ref[...].astype(jnp.float32)).astype(jnp.bfloat16)
    out_ref[half:, :] = grads_ref[...]


def near_join_kernel(keep_ref, got_ref, far_ref, grads_ref, out_ref):
    shards = out_ref.shape[0]
    half = keep_ref.shape[0]
    own = half // shards
    grads = grads_ref[...].astype(jnp.float32) + far_ref[half:, :].astype(jnp.float32)
    grads = grads.astype(jnp.bfloat16)
    for shard in range(shards):
        rows = pl.ds(shard * own, own)
        total = keep_ref[rows, :] + got_ref[rows, :].astype(jnp.float32)
        total += far_ref[rows, :].astype(jnp.float32)
        out_ref[shard, pl.ds(0, own), :] = total.astype(jnp.bfloat16)
        out_ref[shard, pl.ds(own, grads.shape[0]), :] = grads


def total_kernel(scale_factor, parts_ref, half_ref):
    extra = half_ref.shape[0] - 8 + BIAS_ROWS
    tail = sum_of_four(parts_ref, pl.ds(parts_ref.shape[1] - extra, extra))
    tail = tail * scale_factor
    height = half_ref.shape[0] - 8
    half_ref[:height, :] = tail[:height, :]
    bias_row = tail[height : height + 1, :] + tail[height + 1 : height + 2, :]
    half_ref[height:, :] = jnp.broadcast_to(bias_row, (8, bias_row.shape[1]))


def features_kernel(parts_ref, degree_ref, features_ref):
    tiles, edge = degree_ref.shape
    roots = lax.rsqrt(degree_ref[...].astype(jnp.float32))
    for tile in range(tiles):
        rows = pl.ds(tile * edge, edge)
        total = sum_of_four(parts_ref, rows)
        features_ref[rows, :] = (total * roots[tile : tile + 1, :]).T.astype(jnp.bfloat16)


def lay_out_kernel(place_ref, mine_ref, other_ref, grads_ref, bias_ref):
    first = place_ref[0] % 2 == 0
    height = grads_ref.shape[0]
    width = mine_ref.shape[1]
    mine, other = mine_ref[...], other_ref[...]
    halves = (jnp.where(first, mine, other), jnp.where(first, other, mine))
    for index, half in enumerate(halves):
        lanes = pl.ds(index * width, width)
        grads_ref[:, lanes] = half[:height, :]
        bias_ref[:, lanes] = half[height : height + 1, :]


def per_device(
    features,
    degree,
    cotangent,
    weight,
    layer_bias,
    patterns,
    tile_row,
    tile_col,
    tile_pattern,
    tile_weight,
    tile_count,
):
    node_dev, feature_count = features.shape
    hidden = weight.shape[1]
    row_devices = lax.axis_size("row")
    col_devices = lax.axis_size("col")
    chips = row_devices // 2
    edge = patterns.shape[1]
    per_shard = node_dev // edge
    row, col = lax.axis_index("row"), lax.axis_index("col")
    swap = [(index, index ^ 1) for index in range(row_devices)]
    row_near = [
        [(low * 4 + ring) * 2 + core_index for ring in pair for low in range(2)]
        for core_index in range(2)
        for pair in PAIRS[core_index]
    ]
    row_far = [
        (index, (index // 8 * 4 + far_neighbour(index // 2 % 4, index % 2)) * 2 + index % 2)
        for index in range(row_devices)
    ]
    col_near = [
        [index * col_devices + ring * 2 + high for ring in pair for high in range(2)]
        for index in range(row_devices)
        for pair in PAIRS[index % 2]
    ]
    col_far = [
        (
            index * col_devices + place,
            index * col_devices + far_neighbour(place // 2, index % 2) * 2 + place % 2,
        )
        for index in range(row_devices)
        for place in range(col_devices)
    ]
    exchange = functools.partial(lax.all_to_all, split_axis=0, concat_axis=0)
    extra = feature_count + BIAS_ROWS
    half = chips * node_dev
    bf16, f32 = jnp.bfloat16, jnp.float32
    shape = jax.ShapeDtypeStruct
    degree_tiles = degree.reshape(per_shard, edge)
    tile_cost = pl.CostEstimate(
        flops=tile_row.size // (row_devices * col_devices) * edge * edge * feature_count,
        bytes_accessed=patterns.size * 2 + 4 * half * feature_count * 2,
        transcendentals=0,
    )

    scaled = pl.pallas_call(
        scale_kernel,
        out_shape=shape((4, node_dev, feature_count), bf16),
        in_specs=[HBM] * 2,
        out_specs=VMEM,
        scratch_shapes=[
            pltpu.VMEM(features.shape, bf16),
            pltpu.VMEM(degree_tiles.shape, jnp.int32),
            pltpu.SemaphoreType.DMA((2,)),
        ],
        compiler_params=PARAMS,
    )(features, degree_tiles)
    near_own = exchange(scaled, "row", axis_index_groups=row_near).reshape(half // 2, feature_count)
    near_other = lax.ppermute(near_own, "row", swap)
    far_own = lax.ppermute(near_own, "row", row_far)
    row_tiles, near_own = lax.optimization_barrier((tile_row.reshape(per_shard, edge), near_own))
    place = jnp.stack([row, col]).astype(jnp.int32)
    slots = pl.pallas_call(
        order_kernel,
        out_shape=shape((1, ORDERED), jnp.int32),
        in_specs=[SMEM] * 2 + [HBM] * 4,
        out_specs=VMEM,
        scratch_shapes=[
            pltpu.VMEM((4, per_shard, edge), jnp.int32),
            pltpu.SemaphoreType.DMA((4,)),
        ],
        compiler_params=PARAMS,
    )(
        place,
        tile_count,
        row_tiles,
        tile_col.reshape(per_shard, edge),
        tile_pattern.reshape(per_shard, edge),
        tile_weight.reshape(per_shard, edge),
    )
    forward_panel = pltpu.VMEM((half, feature_count), bf16)
    row_sums = shape((col_devices * node_dev, feature_count), f32)
    near_sums = pl.pallas_call(
        forward_near_kernel,
        out_shape=row_sums,
        in_specs=[SMEM] + [VMEM] * 3,
        out_specs=VMEM,
        scratch_shapes=[forward_panel],
        compiler_params=PARAMS,
        cost_estimate=tile_cost,
    )(slots, patterns, near_own, near_other)
    far_own, near_sums = lax.optimization_barrier((far_own, near_sums))
    far_other = lax.ppermute(far_own, "row", swap)
    row_half = shape((col_devices // 2 * node_dev, feature_count), f32)
    far_sums = pl.pallas_call(
        forward_send_kernel,
        out_shape=shape(row_half.shape, bf16),
        in_specs=[SMEM] + [VMEM] * 4,
        out_specs=VMEM,
        scratch_shapes=[forward_panel, pltpu.VMEM(row_half.shape, f32)],
        compiler_params=PARAMS,
        cost_estimate=tile_cost,
    )(slots, patterns, far_own, far_other, near_sums)
    far_sums, near_sums = lax.optimization_barrier((far_sums, near_sums))
    got = lax.ppermute(far_sums, ("row", "col"), col_far)
    keep = pl.pallas_call(
        forward_keep_kernel,
        out_shape=row_half,
        in_specs=[SMEM] + [VMEM] * 4,
        out_specs=VMEM,
        scratch_shapes=[forward_panel],
        compiler_params=PARAMS,
        cost_estimate=tile_cost,
    )(slots, patterns, far_own, far_other, near_sums)
    row_part = pl.pallas_call(
        row_join_kernel,
        out_shape=shape((4, node_dev, feature_count), bf16),
        in_specs=[VMEM] * 2,
        out_specs=VMEM,
        compiler_params=PARAMS,
    )(keep, got)
    parts = exchange(row_part, ("row", "col"), axis_index_groups=col_near)
    pre_act, upstream, keep_terms, send_terms = pl.pallas_call(
        middle_kernel,
        out_shape=(
            shape((node_dev, hidden), f32),
            shape((node_dev, hidden), f32),
            shape((extra, edge), f32),
            shape((extra, edge), bf16),
        ),
        in_specs=[SMEM] + [VMEM] * 5,
        out_specs=(VMEM,) * 4,
        compiler_params=PARAMS,
    )(place, parts, degree_tiles, cotangent, weight, layer_bias[None, :])
    got_terms = lax.ppermute(send_terms, "row", swap)
    spread = pl.pallas_call(
        spread_kernel,
        out_shape=shape((col_devices, node_dev + extra, edge), bf16),
        in_specs=[VMEM] * 2,
        out_specs=VMEM,
        compiler_params=PARAMS,
    )(upstream, weight)
    spread = pl.pallas_call(
        append_kernel,
        out_shape=shape(spread.shape, bf16),
        in_specs=[VMEM] * 3,
        out_specs=VMEM,
        input_output_aliases={2: 0},
        compiler_params=PARAMS,
    )(keep_terms, got_terms, spread)
    spread_all = exchange(spread, "col")
    kept, sent = shape((half // 2, edge), f32), shape((half // 2, edge), bf16)
    keep, send, grads = pl.pallas_call(
        backward_far_kernel,
        out_shape=(kept, sent, shape((extra, edge), bf16)),
        in_specs=[SMEM] + [VMEM] * 2,
        out_specs=(VMEM,) * 3,
        scratch_shapes=[pltpu.VMEM((half, edge), f32)],
        compiler_params=PARAMS,
        cost_estimate=tile_cost,
    )(slots, patterns, spread_all)
    got = lax.ppermute(send, "row", swap)
    pre_act, keep = lax.optimization_barrier((pre_act, keep))
    activations = pl.pallas_call(
        activation_kernel,
        out_shape=shape((node_dev, hidden), bf16),
        in_specs=[VMEM],
        out_specs=VMEM,
        compiler_params=PARAMS,
    )(pre_act)
    got, activations = lax.optimization_barrier((got, activations))
    far_sums = pl.pallas_call(
        far_join_kernel,
        out_shape=shape((half // 2 + extra, edge), bf16),
        in_specs=[VMEM] * 3,
        out_specs=VMEM,
        compiler_params=PARAMS,
    )(keep, got, grads)
    far_sums, spread_all = lax.optimization_barrier((far_sums, spread_all))
    far_got = lax.ppermute(far_sums, "row", row_far)
    keep, send = pl.pallas_call(
        backward_near_kernel,
        out_shape=(kept, sent),
        in_specs=[SMEM] + [VMEM] * 2,
        out_specs=(VMEM,) * 2,
        scratch_shapes=[pltpu.VMEM((half, edge), f32)],
        compiler_params=PARAMS,
        cost_estimate=tile_cost,
    )(slots, patterns, spread_all)
    got = lax.ppermute(send, "row", swap)
    got, far_got = lax.optimization_barrier((got, far_got))
    joined = pl.pallas_call(
        near_join_kernel,
        out_shape=shape((4, node_dev + extra, edge), bf16),
        in_specs=[VMEM] * 4,
        out_specs=VMEM,
        compiler_params=PARAMS,
    )(keep, got, far_got, grads)
    back_parts = exchange(joined, "row", axis_index_groups=row_near)
    scale_factor = 1.0 / math.sqrt(node_dev * row_devices * col_devices)
    mine = pl.pallas_call(
        functools.partial(total_kernel, scale_factor),
        out_shape=shape((feature_count + 8, edge), f32),
        in_specs=[VMEM],
        out_specs=VMEM,
        compiler_params=PARAMS,
    )(back_parts)
    other = lax.ppermute(mine, "row", swap)
    grad_features = pl.pallas_call(
        features_kernel,
        out_shape=shape((node_dev, feature_count), bf16),
        in_specs=[VMEM] * 2,
        out_specs=VMEM,
        compiler_params=PARAMS,
    )(back_parts, degree_tiles)
    grad_weight, grad_bias = pl.pallas_call(
        lay_out_kernel,
        out_shape=(shape((feature_count, hidden), f32), shape((1, hidden), f32)),
        in_specs=[SMEM] + [VMEM] * 2,
        out_specs=(VMEM,) * 2,
        compiler_params=PARAMS,
    )(place, mine, other)
    return (activations, grad_features, grad_weight, grad_bias[0])


def solution(mesh):
    in_specs = (
        P(("row", "col"), None),
        P(("row", "col")),
        P(("row", "col"), None),
        P(),
        P(),
        P(),
        P("row", "col", None),
        P("row", "col", None),
        P("row", "col", None),
        P("row", "col", None),
        P("row", "col"),
    )
    out_specs = (P(("row", "col"), None), P(("row", "col"), None), P(), P())
    return jax.shard_map(
        per_device, mesh=mesh, in_specs=in_specs, out_specs=out_specs, check_vma=False
    )
```

```python
import functools
import math

import jax
import jax.numpy as jnp
from jax import lax
from jax.experimental import pallas as pl
from jax.experimental.pallas import tpu as pltpu
from jax.sharding import PartitionSpec as P

GROUP = 64
VMEM_LIMIT = 20 * 1024 * 1024
ROOT_2_PI = math.sqrt(2.0 / math.pi)
CUBIC = 0.044715
BIAS_ROWS = 16
PER_SHARD = 4
CLASSES = 2
ORDERED = 640
BOUNDS = 600
PAIRS = (((0, 1), (2, 3)), ((0, 3), (1, 2)))
HBM = pl.BlockSpec(memory_space=pltpu.HBM)
VMEM = pl.BlockSpec(memory_space=pltpu.VMEM)
SMEM = pl.BlockSpec(memory_space=pltpu.SMEM)
PARAMS = pltpu.CompilerParams(vmem_limit_bytes=VMEM_LIMIT)


def pair_of(place, core):
    return jnp.where(core == 0, place >> 1, (place ^ (place >> 1)) & 1)


def pair_index(place, core):
    return jnp.where(core == 0, place & 1, place >> 1)


def far_neighbour(place, core):
    return place ^ 3 if core == 0 else place ^ 1


def order_kernel(
    place_ref, live_ref, row_hbm, col_hbm, pattern_hbm, weight_hbm, out_ref, fields, sems
):
    sources = (row_hbm, col_hbm, pattern_hbm, weight_hbm)
    copies = [
        pltpu.make_async_copy(source, fields.at[index], sems.at[index])
        for index, source in enumerate(sources)
    ]
    for copy in copies:
        copy.start()
    for copy in copies:
        copy.wait()
    row = place_ref[0]
    _, rows, edge = fields.shape
    tile_row, tile_col = fields[0], fields[1]
    shard = tile_col // PER_SHARD
    parity = shard % 2
    chip = shard // 2
    ring = chip % 4
    tile = tile_col % PER_SHARD
    half = parity ^ (row % 2)
    far = (pair_of(ring, parity) != pair_of((row // 2) % 4, parity)).astype(jnp.int32)
    rank = pair_index(ring, parity) * 2 + chip // 4
    place = (half * 4 + rank) * PER_SHARD + tile
    word = tile_row | (fields[2] << 5) | (fields[3] << 11) | (place << 14)
    slot = lax.broadcasted_iota(jnp.int32, (rows, edge), 0) * edge
    slot += lax.broadcasted_iota(jnp.int32, (rows, edge), 1)
    alive = slot < live_ref[0, 0]
    word = jnp.where(alive, word, 0)
    kind = jnp.where(alive, far, CLASSES)

    flags = [(kind == index).astype(jnp.float32) for index in range(CLASSES + 1)]
    stacked = jnp.concatenate(flags + [jnp.zeros((4, edge), jnp.float32)], 0)
    before = lax.broadcasted_iota(jnp.int32, (edge, edge), 0) < lax.broadcasted_iota(
        jnp.int32, (edge, edge), 1
    )
    earlier = jnp.dot(
        stacked.astype(jnp.bfloat16),
        before.astype(jnp.float32).astype(jnp.bfloat16),
        preferred_element_type=jnp.float32,
    )
    counts = jnp.sum(stacked, axis=1, keepdims=True)
    start = jnp.zeros((1, 1), jnp.float32)
    ends = []
    position = [jnp.zeros((1, edge), jnp.float32) for _ in range(rows)]
    for index in range(CLASSES + 1):
        for line in range(rows):
            at = index * rows + line
            position[line] += flags[index][line : line + 1] * (start + earlier[at : at + 1])
            start = start + counts[at : at + 1]
        ends.append(start)
    turned = jnp.concatenate(position + [jnp.zeros((8 - rows, edge), jnp.float32)], 0).T
    slots = rows * edge
    lanes = lax.broadcasted_iota(jnp.int32, (edge, slots), 1).astype(jnp.float32)
    pieces = jnp.zeros((8, slots), jnp.float32)
    for line in range(rows):
        chosen = (turned[:, line : line + 1] == lanes).astype(jnp.float32).astype(jnp.bfloat16)
        parts = [(word[line : line + 1] >> shift) & 127 for shift in (0, 7, 14)]
        parts = jnp.concatenate(parts + [jnp.zeros((5, edge), jnp.int32)], 0)
        parts = parts.astype(jnp.float32).astype(jnp.bfloat16)
        pieces += jnp.dot(parts, chosen, preferred_element_type=jnp.float32)
    pieces = pieces.astype(jnp.int32)
    out_ref[:, :slots] = pieces[0:1] | (pieces[1:2] << 7) | (pieces[2:3] << 14)
    lane = lax.broadcasted_iota(jnp.int32, (1, out_ref.shape[1] - slots), 1) + slots
    tail = jnp.zeros(lane.shape, jnp.int32)
    for index in range(CLASSES):
        tail = jnp.where(lane == BOUNDS + index, ends[index].astype(jnp.int32), tail)
    out_ref[:, slots:] = tail


def root_columns(degree):
    rows = lax.rsqrt(degree.astype(jnp.float32))
    rows = jnp.concatenate([rows, jnp.ones((8 - rows.shape[0], rows.shape[1]), jnp.float32)], 0)
    return rows.T


def scale_kernel(features_hbm, degree_hbm, out_ref, features_ref, degree_ref, sems):
    copies = (
        pltpu.make_async_copy(degree_hbm, degree_ref, sems.at[0]),
        pltpu.make_async_copy(features_hbm, features_ref, sems.at[1]),
    )
    for copy in copies:
        copy.start()
    copies[0].wait()
    roots = root_columns(degree_ref[...])
    copies[1].wait()
    edge = degree_ref.shape[1]
    for tile in range(degree_ref.shape[0]):
        rows = pl.ds(tile * edge, edge)
        scaled = features_ref[rows, :].astype(jnp.float32) * roots[:, tile : tile + 1]
        scaled = scaled.astype(jnp.bfloat16)
        for copy in range(out_ref.shape[0]):
            out_ref[copy, rows, :] = scaled


def add_products(slots_ref, first, end, product_of, place_of, sums):
    edge = sums.shape[1]

    def one_group(turn, carry):
        terms = []
        for member in range(GROUP):
            slot = first + turn * GROUP + member
            word = slots_ref[0, slot]
            factor = jnp.where(slot < end, (word >> 11) & 7, 0).astype(jnp.float32)
            terms.append((place_of(word), factor, product_of(word)))
        for place, factor, product in terms:
            rows = pl.ds(pl.multiple_of(place * edge, edge), edge)
            sums[rows, :] += factor * product
        return carry

    lax.fori_loop(0, (end - first + GROUP - 1) // GROUP, one_group, 0)


def tile_of(ref, place, edge):
    return ref[pl.ds(pl.multiple_of(place * edge, edge), edge), :]


def forward_sums(slots_ref, patterns_ref, own_ref, other_ref, panel, sums, far):
    edge = patterns_ref.shape[1]
    half = own_ref.shape[0]
    panel[:half, :] = own_ref[...]
    panel[half:, :] = other_ref[...]
    middle, end = slots_ref[0, BOUNDS], slots_ref[0, BOUNDS + 1]

    def product_of(word):
        return jnp.dot(
            patterns_ref[(word >> 5) & 63],
            tile_of(panel, (word >> 14) & 31, edge),
            preferred_element_type=jnp.float32,
        )

    first, end = (middle, end) if far else (0, middle)
    add_products(slots_ref, first, end, product_of, lambda word: word & 31, sums)


def forward_near_kernel(slots_ref, patterns_ref, own_ref, other_ref, out_ref, panel):
    out_ref[...] = jnp.zeros_like(out_ref)
    forward_sums(slots_ref, patterns_ref, own_ref, other_ref, panel, out_ref, False)


def forward_far_kernel(slots_ref, patterns_ref, own_ref, other_ref, so_far_ref, out_ref, panel, sums):
    sums[...] = so_far_ref[...]
    forward_sums(slots_ref, patterns_ref, own_ref, other_ref, panel, sums, True)
    out_ref[...] = sums[...].astype(jnp.bfloat16)


def backward_sums(slots_ref, patterns_ref, spread_ref, keep_ref, send_ref, sums, far):
    edge = patterns_ref.shape[1]
    half = sums.shape[0] // 2
    sums[...] = jnp.zeros_like(sums)
    middle, end = slots_ref[0, BOUNDS], slots_ref[0, BOUNDS + 1]

    def product_of(word):
        start = pl.multiple_of((word & 3) * edge, edge)
        return jnp.dot(
            spread_ref[(word >> 2) & 7, pl.ds(start, edge), :],
            patterns_ref[(word >> 5) & 63],
            preferred_element_type=jnp.float32,
        )

    first, end = (middle, end) if far else (0, middle)
    add_products(slots_ref, first, end, product_of, lambda word: (word >> 14) & 31, sums)
    keep_ref[...] = sums[:half, :]
    send_ref[...] = sums[half:, :].astype(jnp.bfloat16)


def backward_far_kernel(slots_ref, patterns_ref, spread_ref, keep_ref, send_ref, sums):
    backward_sums(slots_ref, patterns_ref, spread_ref, keep_ref, send_ref, sums, True)


def backward_near_kernel(slots_ref, patterns_ref, spread_ref, keep_ref, send_ref, sums):
    backward_sums(slots_ref, patterns_ref, spread_ref, keep_ref, send_ref, sums, False)


def split_product(left, right, dims):
    high = left.astype(jnp.bfloat16)
    low = (left - high.astype(jnp.float32)).astype(jnp.bfloat16)
    return lax.dot_general(
        high, right, (dims, ((), ())), preferred_element_type=jnp.float32
    ) + lax.dot_general(low, right, (dims, ((), ())), preferred_element_type=jnp.float32)


def activate(pre_act):
    square = pre_act * pre_act
    bent = jnp.tanh(ROOT_2_PI * (pre_act + CUBIC * (pre_act * square)))
    return square, bent, 0.5 * (1.0 + bent)


def middle_tile(tile, roots, parts_ref, cotangent_ref, weight, bias_ref):
    edge = roots.shape[0]
    rows = pl.ds(tile * edge, edge)
    sums = parts_ref[0, rows, :].astype(jnp.float32)
    for shard in range(1, parts_ref.shape[0]):
        sums += parts_ref[shard, rows, :].astype(jnp.float32)
    inv_root = roots[:, tile : tile + 1]
    pre_act = inv_root * split_product(sums, weight, ((1,), (0,))) + bias_ref[...]
    square, bent, half = activate(pre_act)
    rise = 0.5 * pre_act * (1.0 - bent * bent) * (ROOT_2_PI * (1.0 + 3.0 * CUBIC * square))
    slope = cotangent_ref[rows, :].astype(jnp.float32) * (half + rise)
    return sums, pre_act * half, slope, inv_root


def spread_kernel(
    parts_ref, degree_ref, cotangent_ref, weight_ref, bias_ref, out_ref, done_ref
):
    tiles, edge = degree_ref.shape
    weight = weight_ref[...]
    roots = root_columns(degree_ref[...])
    for tile in range(tiles):
        _, _, slope, inv_root = middle_tile(
            tile, roots, parts_ref, cotangent_ref, weight, bias_ref
        )
        upstream = inv_root * slope
        high = upstream.astype(jnp.bfloat16)
        low = (upstream - high.astype(jnp.float32)).astype(jnp.bfloat16)
        spread = sum(
            lax.dot_general(
                weight, part, (((1,), (1,)), ((), ())), preferred_element_type=jnp.float32
            )
            for part in (high, low)
        ).astype(jnp.bfloat16)
        for shard in range(out_ref.shape[0]):
            out_ref[shard, pl.ds(tile * edge, edge), :] = spread
    done_ref[...] = jnp.zeros_like(done_ref)


def middle_kernel(
    place_ref,
    parts_ref,
    degree_ref,
    cotangent_ref,
    weight_ref,
    bias_ref,
    act_ref,
    keep_ref,
    send_ref,
):
    tiles, edge = degree_ref.shape
    weight = weight_ref[...]
    height = weight.shape[0]
    roots = root_columns(degree_ref[...])
    grads = jnp.zeros(weight.shape, jnp.float32)
    bias_row = jnp.zeros(bias_ref.shape, jnp.float32)
    for tile in range(tiles):
        sums, activations, slope, inv_root = middle_tile(
            tile, roots, parts_ref, cotangent_ref, weight, bias_ref
        )
        act_ref[pl.ds(tile * edge, edge), :] = activations.astype(jnp.bfloat16)
        upstream = (inv_root * slope).astype(jnp.bfloat16)
        grads += split_product(sums, upstream, ((0,), (0,)))
        bias_row += jnp.sum(slope, axis=0, keepdims=True)
    width = keep_ref.shape[1]
    first = place_ref[0] % 2 == 0

    def put(target, left):
        pick = lambda whole: jnp.where(left, whole[:, :width], whole[:, width:])
        target[:height, :] = pick(grads)
        row_ids = lax.broadcasted_iota(jnp.int32, (BIAS_ROWS, width), 0)
        target[height:, :] = jnp.where(row_ids == 0, pick(bias_row), 0.0)

    put(keep_ref, first)
    put(send_ref, jnp.logical_not(first))


def sum_of_four(parts_ref, rows):
    part = lambda index: parts_ref[index, rows, :].astype(jnp.float32)
    return (part(0) + part(2)) + (part(1) + part(3))


def terms_to_send(grads_ref):
    height = grads_ref.shape[0] - BIAS_ROWS
    bias = grads_ref[height:, :]
    high = bias.astype(jnp.bfloat16).astype(jnp.float32)
    row_ids = lax.broadcasted_iota(jnp.int32, bias.shape, 0)
    low = jnp.broadcast_to((bias - high)[0:1, :], bias.shape)
    bias = jnp.where(row_ids == 1, low, high)
    return jnp.concatenate([grads_ref[:height, :], bias], 0).astype(jnp.bfloat16)


def far_join_kernel(keep_ref, got_ref, grads_ref, out_ref, terms_ref):
    half = keep_ref.shape[0]
    out_ref[:half, :] = (keep_ref[...] + got_ref[...].astype(jnp.float32)).astype(jnp.bfloat16)
    terms = terms_to_send(grads_ref)
    out_ref[half:, :] = terms
    terms_ref[...] = terms


def near_join_kernel(keep_ref, got_ref, far_ref, grads_ref, out_ref):
    shards = out_ref.shape[0]
    half = keep_ref.shape[0]
    own = half // shards
    grads = grads_ref[...].astype(jnp.float32) + far_ref[half:, :].astype(jnp.float32)
    grads = grads.astype(jnp.bfloat16)
    for shard in range(shards):
        rows = pl.ds(shard * own, own)
        total = keep_ref[rows, :] + got_ref[rows, :].astype(jnp.float32)
        total += far_ref[rows, :].astype(jnp.float32)
        out_ref[shard, pl.ds(0, own), :] = total.astype(jnp.bfloat16)
        out_ref[shard, pl.ds(own, grads.shape[0]), :] = grads


def total_kernel(scale_factor, parts_ref, half_ref):
    extra = half_ref.shape[0] - 8 + BIAS_ROWS
    tail = sum_of_four(parts_ref, pl.ds(parts_ref.shape[1] - extra, extra))
    tail = tail * scale_factor
    height = half_ref.shape[0] - 8
    half_ref[:height, :] = tail[:height, :]
    bias_row = tail[height : height + 1, :] + tail[height + 1 : height + 2, :]
    half_ref[height:, :] = jnp.broadcast_to(bias_row, (8, bias_row.shape[1]))


def features_kernel(parts_ref, degree_ref, features_ref):
    tiles, edge = degree_ref.shape
    roots = lax.rsqrt(degree_ref[...].astype(jnp.float32))
    for tile in range(tiles):
        rows = pl.ds(tile * edge, edge)
        total = sum_of_four(parts_ref, rows)
        features_ref[rows, :] = (total * roots[tile : tile + 1, :]).T.astype(jnp.bfloat16)


def lay_out_kernel(place_ref, mine_ref, other_ref, grads_ref, bias_ref):
    first = place_ref[0] % 2 == 0
    height = grads_ref.shape[0]
    width = mine_ref.shape[1]
    mine, other = mine_ref[...], other_ref[...]
    halves = (jnp.where(first, mine, other), jnp.where(first, other, mine))
    for index, half in enumerate(halves):
        lanes = pl.ds(index * width, width)
        grads_ref[:, lanes] = half[:height, :]
        bias_ref[:, lanes] = half[height : height + 1, :]


def per_device(
    features,
    degree,
    cotangent,
    weight,
    layer_bias,
    patterns,
    tile_row,
    tile_col,
    tile_pattern,
    tile_weight,
    tile_count,
):
    node_dev, feature_count = features.shape
    hidden = weight.shape[1]
    row_devices = lax.axis_size("row")
    col_devices = lax.axis_size("col")
    chips = row_devices // 2
    edge = patterns.shape[1]
    per_shard = node_dev // edge
    row = lax.axis_index("row")
    swap = [(index, index ^ 1) for index in range(row_devices)]
    row_near = [
        [(low * 4 + ring) * 2 + core_index for ring in pair for low in range(2)]
        for core_index in range(2)
        for pair in PAIRS[core_index]
    ]
    row_far = [
        (index, (index // 8 * 4 + far_neighbour(index // 2 % 4, index % 2)) * 2 + index % 2)
        for index in range(row_devices)
    ]
    col_far, col_close, col_high = (
        [
            (index * col_devices + place, index * col_devices + peer(place, index % 2))
            for index in range(row_devices)
            for place in range(col_devices)
        ]
        for peer in (
            lambda place, core: far_neighbour(place // 2, core) * 2 + place % 2,
            lambda place, core: far_neighbour(place // 2, 1 - core) * 2 + place % 2,
            lambda place, core: place ^ 1,
        )
    )
    exchange = functools.partial(lax.all_to_all, split_axis=0, concat_axis=0)
    extra = feature_count + BIAS_ROWS
    half = chips * node_dev
    bf16, f32 = jnp.bfloat16, jnp.float32
    shape = jax.ShapeDtypeStruct
    degree_tiles = degree.reshape(per_shard, edge)
    tile_cost = pl.CostEstimate(
        flops=tile_row.size // (row_devices * col_devices) * edge * edge * feature_count,
        bytes_accessed=patterns.size * 2 + 4 * half * feature_count * 2,
        transcendentals=0,
    )

    scaled = pl.pallas_call(
        scale_kernel,
        out_shape=shape((4, node_dev, feature_count), bf16),
        in_specs=[HBM] * 2,
        out_specs=VMEM,
        scratch_shapes=[
            pltpu.VMEM(features.shape, bf16),
            pltpu.VMEM(degree_tiles.shape, jnp.int32),
            pltpu.SemaphoreType.DMA((2,)),
        ],
        compiler_params=PARAMS,
    )(features, degree_tiles)
    near_own = exchange(scaled, "row", axis_index_groups=row_near).reshape(half // 2, feature_count)
    near_other = lax.ppermute(near_own, "row", swap)
    far_own = lax.ppermute(near_own, "row", row_far)
    row_tiles, near_own = lax.optimization_barrier((tile_row.reshape(per_shard, edge), near_own))
    place = row.astype(jnp.int32).reshape(1)
    slots = pl.pallas_call(
        order_kernel,
        out_shape=shape((1, ORDERED), jnp.int32),
        in_specs=[SMEM] * 2 + [HBM] * 4,
        out_specs=VMEM,
        scratch_shapes=[
            pltpu.VMEM((4, per_shard, edge), jnp.int32),
            pltpu.SemaphoreType.DMA((4,)),
        ],
        compiler_params=PARAMS,
    )(
        place,
        tile_count,
        row_tiles,
        tile_col.reshape(per_shard, edge),
        tile_pattern.reshape(per_shard, edge),
        tile_weight.reshape(per_shard, edge),
    )
    forward_panel = pltpu.VMEM((half, feature_count), bf16)
    row_sums = shape((col_devices * node_dev, feature_count), f32)
    near_sums = pl.pallas_call(
        forward_near_kernel,
        out_shape=row_sums,
        in_specs=[SMEM] + [VMEM] * 3,
        out_specs=VMEM,
        scratch_shapes=[forward_panel],
        compiler_params=PARAMS,
        cost_estimate=tile_cost,
    )(slots, patterns, near_own, near_other)
    far_own, near_sums = lax.optimization_barrier((far_own, near_sums))
    far_other = lax.ppermute(far_own, "row", swap)
    row_part = pl.pallas_call(
        forward_far_kernel,
        out_shape=shape(row_sums.shape, bf16),
        in_specs=[SMEM] + [VMEM] * 4,
        out_specs=VMEM,
        scratch_shapes=[forward_panel, pltpu.VMEM(row_sums.shape, f32)],
        compiler_params=PARAMS,
        cost_estimate=tile_cost,
    )(slots, patterns, far_own, far_other, near_sums)
    parts = exchange(row_part.reshape(col_devices, node_dev, feature_count), "col")
    middle_inputs = (parts, degree_tiles, cotangent, weight, layer_bias[None, :])
    spread, done = pl.pallas_call(
        spread_kernel,
        out_shape=(shape((col_devices, node_dev, edge), bf16), shape((8, edge), f32)),
        in_specs=[VMEM] * 5,
        out_specs=(VMEM,) * 2,
        compiler_params=PARAMS,
    )(*middle_inputs)
    spread_all = exchange(spread, "col")
    middle_inputs, _ = lax.optimization_barrier((middle_inputs, done))
    terms = shape((extra, edge), f32)
    activations, keep_terms, send_terms = pl.pallas_call(
        middle_kernel,
        out_shape=(shape((node_dev, hidden), bf16), terms, terms),
        in_specs=[SMEM] + [VMEM] * 5,
        out_specs=(VMEM,) * 3,
        compiler_params=PARAMS,
    )(place, *middle_inputs)
    grads = keep_terms + lax.ppermute(send_terms, "row", swap)
    for pairs in (col_far, col_close, col_high):
        grads = grads + lax.ppermute(grads, ("row", "col"), pairs)
    spread_all, grads, activations = lax.optimization_barrier((spread_all, grads, activations))
    kept, sent = shape((half // 2, edge), f32), shape((half // 2, edge), bf16)
    keep, send = pl.pallas_call(
        backward_far_kernel,
        out_shape=(kept, sent),
        in_specs=[SMEM] + [VMEM] * 2,
        out_specs=(VMEM,) * 2,
        scratch_shapes=[pltpu.VMEM((half, edge), f32)],
        compiler_params=PARAMS,
        cost_estimate=tile_cost,
    )(slots, patterns, spread_all)
    got = lax.ppermute(send, "row", swap)
    far_sums, grads = pl.pallas_call(
        far_join_kernel,
        out_shape=(shape((half // 2 + extra, edge), bf16), shape((extra, edge), bf16)),
        in_specs=[VMEM] * 3,
        out_specs=(VMEM,) * 2,
        compiler_params=PARAMS,
    )(keep, got, grads)
    far_sums, spread_all = lax.optimization_barrier((far_sums, spread_all))
    far_got = lax.ppermute(far_sums, "row", row_far)
    keep, send = pl.pallas_call(
        backward_near_kernel,
        out_shape=(kept, sent),
        in_specs=[SMEM] + [VMEM] * 2,
        out_specs=(VMEM,) * 2,
        scratch_shapes=[pltpu.VMEM((half, edge), f32)],
        compiler_params=PARAMS,
        cost_estimate=tile_cost,
    )(slots, patterns, spread_all)
    got = lax.ppermute(send, "row", swap)
    got, far_got = lax.optimization_barrier((got, far_got))
    joined = pl.pallas_call(
        near_join_kernel,
        out_shape=shape((4, node_dev + extra, edge), bf16),
        in_specs=[VMEM] * 4,
        out_specs=VMEM,
        compiler_params=PARAMS,
    )(keep, got, far_got, grads)
    back_parts = exchange(joined, "row", axis_index_groups=row_near)
    scale_factor = 1.0 / math.sqrt(node_dev * row_devices * col_devices)
    mine = pl.pallas_call(
        functools.partial(total_kernel, scale_factor),
        out_shape=shape((feature_count + 8, edge), f32),
        in_specs=[VMEM],
        out_specs=VMEM,
        compiler_params=PARAMS,
    )(back_parts)
    other = lax.ppermute(mine, "row", swap)
    grad_features = pl.pallas_call(
        features_kernel,
        out_shape=shape((node_dev, feature_count), bf16),
        in_specs=[VMEM] * 2,
        out_specs=VMEM,
        compiler_params=PARAMS,
    )(back_parts, degree_tiles)
    grad_weight, grad_bias = pl.pallas_call(
        lay_out_kernel,
        out_shape=(shape((feature_count, hidden), f32), shape((1, hidden), f32)),
        in_specs=[SMEM] + [VMEM] * 2,
        out_specs=(VMEM,) * 2,
        compiler_params=PARAMS,
    )(place, mine, other)
    return (activations, grad_features, grad_weight, grad_bias[0])


def solution(mesh):
    in_specs = (
        P(("row", "col"), None),
        P(("row", "col")),
        P(("row", "col"), None),
        P(),
        P(),
        P(),
        P("row", "col", None),
        P("row", "col", None),
        P("row", "col", None),
        P("row", "col", None),
        P("row", "col"),
    )
    out_specs = (P(("row", "col"), None), P(("row", "col"), None), P(), P())
    return jax.shard_map(
        per_device, mesh=mesh, in_specs=in_specs, out_specs=out_specs, check_vma=False
    )
```

```python
import functools
import math

import jax
import jax.numpy as jnp
from jax import lax
from jax.experimental import pallas as pl
from jax.experimental.pallas import tpu as pltpu
from jax.sharding import PartitionSpec as P

GROUP = 64
VMEM_LIMIT = 20 * 1024 * 1024
ROOT_2_PI = math.sqrt(2.0 / math.pi)
CUBIC = 0.044715
BIAS_ROWS = 16
PER_SHARD = 4
CLASSES = 2
ORDERED = 640
BOUNDS = 600
PAIRS = (((0, 1), (2, 3)), ((0, 3), (1, 2)))
HBM = pl.BlockSpec(memory_space=pltpu.HBM)
VMEM = pl.BlockSpec(memory_space=pltpu.VMEM)
SMEM = pl.BlockSpec(memory_space=pltpu.SMEM)
PARAMS = pltpu.CompilerParams(vmem_limit_bytes=VMEM_LIMIT)


def pair_of(place, core):
    return jnp.where(core == 0, place >> 1, (place ^ (place >> 1)) & 1)


def pair_index(place, core):
    return jnp.where(core == 0, place & 1, place >> 1)


def far_neighbour(place, core):
    return place ^ 3 if core == 0 else place ^ 1


def order_kernel(
    place_ref, live_ref, row_hbm, col_hbm, pattern_hbm, weight_hbm, out_ref, fields, sems
):
    sources = (row_hbm, col_hbm, pattern_hbm, weight_hbm)
    copies = [
        pltpu.make_async_copy(source, fields.at[index], sems.at[index])
        for index, source in enumerate(sources)
    ]
    for copy in copies:
        copy.start()
    for copy in copies:
        copy.wait()
    row = place_ref[0]
    _, rows, edge = fields.shape
    tile_row, tile_col = fields[0], fields[1]
    shard = tile_col // PER_SHARD
    parity = shard % 2
    chip = shard // 2
    ring = chip % 4
    tile = tile_col % PER_SHARD
    half = parity ^ (row % 2)
    far = (pair_of(ring, parity) != pair_of((row // 2) % 4, parity)).astype(jnp.int32)
    rank = pair_index(ring, parity) * 2 + chip // 4
    place = (half * 4 + rank) * PER_SHARD + tile
    word = tile_row | (fields[2] << 5) | (fields[3] << 11) | (place << 14)
    slot = lax.broadcasted_iota(jnp.int32, (rows, edge), 0) * edge
    slot += lax.broadcasted_iota(jnp.int32, (rows, edge), 1)
    alive = slot < live_ref[0, 0]
    word = jnp.where(alive, word, 0)
    kind = jnp.where(alive, far, CLASSES)

    flags = [(kind == index).astype(jnp.float32) for index in range(CLASSES + 1)]
    stacked = jnp.concatenate(flags + [jnp.zeros((4, edge), jnp.float32)], 0)
    before = lax.broadcasted_iota(jnp.int32, (edge, edge), 0) < lax.broadcasted_iota(
        jnp.int32, (edge, edge), 1
    )
    earlier = jnp.dot(
        stacked.astype(jnp.bfloat16),
        before.astype(jnp.float32).astype(jnp.bfloat16),
        preferred_element_type=jnp.float32,
    )
    counts = jnp.sum(stacked, axis=1, keepdims=True)
    start = jnp.zeros((1, 1), jnp.float32)
    ends = []
    position = [jnp.zeros((1, edge), jnp.float32) for _ in range(rows)]
    for index in range(CLASSES + 1):
        for line in range(rows):
            at = index * rows + line
            position[line] += flags[index][line : line + 1] * (start + earlier[at : at + 1])
            start = start + counts[at : at + 1]
        ends.append(start)
    turned = jnp.concatenate(position + [jnp.zeros((8 - rows, edge), jnp.float32)], 0).T
    slots = rows * edge
    lanes = lax.broadcasted_iota(jnp.int32, (edge, slots), 1).astype(jnp.float32)
    pieces = jnp.zeros((8, slots), jnp.float32)
    for line in range(rows):
        chosen = (turned[:, line : line + 1] == lanes).astype(jnp.float32).astype(jnp.bfloat16)
        parts = [(word[line : line + 1] >> shift) & 127 for shift in (0, 7, 14)]
        parts = jnp.concatenate(parts + [jnp.zeros((5, edge), jnp.int32)], 0)
        parts = parts.astype(jnp.float32).astype(jnp.bfloat16)
        pieces += jnp.dot(parts, chosen, preferred_element_type=jnp.float32)
    pieces = pieces.astype(jnp.int32)
    out_ref[:, :slots] = pieces[0:1] | (pieces[1:2] << 7) | (pieces[2:3] << 14)
    lane = lax.broadcasted_iota(jnp.int32, (1, out_ref.shape[1] - slots), 1) + slots
    tail = jnp.zeros(lane.shape, jnp.int32)
    for index in range(CLASSES):
        tail = jnp.where(lane == BOUNDS + index, ends[index].astype(jnp.int32), tail)
    out_ref[:, slots:] = tail


def root_columns(degree):
    rows = lax.rsqrt(degree.astype(jnp.float32))
    rows = jnp.concatenate([rows, jnp.ones((8 - rows.shape[0], rows.shape[1]), jnp.float32)], 0)
    return rows.T


def scale_kernel(features_hbm, degree_hbm, out_ref, features_ref, degree_ref, sems):
    copies = (
        pltpu.make_async_copy(degree_hbm, degree_ref, sems.at[0]),
        pltpu.make_async_copy(features_hbm, features_ref, sems.at[1]),
    )
    for copy in copies:
        copy.start()
    copies[0].wait()
    roots = root_columns(degree_ref[...])
    copies[1].wait()
    edge = degree_ref.shape[1]
    for tile in range(degree_ref.shape[0]):
        rows = pl.ds(tile * edge, edge)
        scaled = features_ref[rows, :].astype(jnp.float32) * roots[:, tile : tile + 1]
        scaled = scaled.astype(jnp.bfloat16)
        for copy in range(out_ref.shape[0]):
            out_ref[copy, rows, :] = scaled


def add_products(slots_ref, first, end, product_of, place_of, sums):
    edge = sums.shape[1]

    def one_group(turn, carry):
        terms = []
        for member in range(GROUP):
            slot = first + turn * GROUP + member
            word = slots_ref[0, slot]
            factor = jnp.where(slot < end, (word >> 11) & 7, 0).astype(jnp.float32)
            terms.append((place_of(word), factor, product_of(word)))
        for place, factor, product in terms:
            rows = pl.ds(pl.multiple_of(place * edge, edge), edge)
            sums[rows, :] += factor * product
        return carry

    lax.fori_loop(0, (end - first + GROUP - 1) // GROUP, one_group, 0)


def tile_of(ref, place, edge):
    return ref[pl.ds(pl.multiple_of(place * edge, edge), edge), :]


def forward_sums(slots_ref, patterns_ref, own_ref, other_ref, panel, sums, far):
    edge = patterns_ref.shape[1]
    half = own_ref.shape[0]
    panel[:half, :] = own_ref[...]
    panel[half:, :] = other_ref[...]
    middle, end = slots_ref[0, BOUNDS], slots_ref[0, BOUNDS + 1]

    def product_of(word):
        return jnp.dot(
            patterns_ref[(word >> 5) & 63],
            tile_of(panel, (word >> 14) & 31, edge),
            preferred_element_type=jnp.float32,
        )

    first, end = (middle, end) if far else (0, middle)
    add_products(slots_ref, first, end, product_of, lambda word: word & 31, sums)


def forward_near_kernel(slots_ref, patterns_ref, own_ref, other_ref, out_ref, panel):
    out_ref[...] = jnp.zeros_like(out_ref)
    forward_sums(slots_ref, patterns_ref, own_ref, other_ref, panel, out_ref, False)


def forward_far_kernel(slots_ref, patterns_ref, own_ref, other_ref, so_far_ref, out_ref, panel, sums):
    sums[...] = so_far_ref[...]
    forward_sums(slots_ref, patterns_ref, own_ref, other_ref, panel, sums, True)
    out_ref[...] = sums[...].astype(jnp.bfloat16)


def backward_sums(slots_ref, patterns_ref, spread_ref, keep_ref, send_ref, sums, far):
    edge = patterns_ref.shape[1]
    half = sums.shape[0] // 2
    sums[...] = jnp.zeros_like(sums)
    middle, end = slots_ref[0, BOUNDS], slots_ref[0, BOUNDS + 1]

    def product_of(word):
        start = pl.multiple_of((word & 3) * edge, edge)
        return jnp.dot(
            spread_ref[(word >> 2) & 7, pl.ds(start, edge), :],
            patterns_ref[(word >> 5) & 63],
            preferred_element_type=jnp.float32,
        )

    first, end = (middle, end) if far else (0, middle)
    add_products(slots_ref, first, end, product_of, lambda word: (word >> 14) & 31, sums)
    keep_ref[...] = sums[:half, :]
    send_ref[...] = sums[half:, :].astype(jnp.bfloat16)


def backward_far_kernel(slots_ref, patterns_ref, spread_ref, keep_ref, send_ref, sums):
    backward_sums(slots_ref, patterns_ref, spread_ref, keep_ref, send_ref, sums, True)


def backward_near_kernel(slots_ref, patterns_ref, spread_ref, keep_ref, send_ref, sums):
    backward_sums(slots_ref, patterns_ref, spread_ref, keep_ref, send_ref, sums, False)


def split_product(left, right, dims):
    high = left.astype(jnp.bfloat16)
    low = (left - high.astype(jnp.float32)).astype(jnp.bfloat16)
    return lax.dot_general(
        high, right, (dims, ((), ())), preferred_element_type=jnp.float32
    ) + lax.dot_general(low, right, (dims, ((), ())), preferred_element_type=jnp.float32)


def activate(pre_act):
    square = pre_act * pre_act
    bent = jnp.tanh(ROOT_2_PI * (pre_act + CUBIC * (pre_act * square)))
    return square, bent, 0.5 * (1.0 + bent)


def middle_tile(tile, roots, parts_ref, cotangent_ref, weight, bias_ref):
    edge = roots.shape[0]
    rows = pl.ds(tile * edge, edge)
    sums = parts_ref[0, rows, :].astype(jnp.float32)
    for shard in range(1, parts_ref.shape[0]):
        sums += parts_ref[shard, rows, :].astype(jnp.float32)
    inv_root = roots[:, tile : tile + 1]
    pre_act = inv_root * split_product(sums, weight, ((1,), (0,))) + bias_ref[...]
    square, bent, half = activate(pre_act)
    rise = 0.5 * pre_act * (1.0 - bent * bent) * (ROOT_2_PI * (1.0 + 3.0 * CUBIC * square))
    slope = cotangent_ref[rows, :].astype(jnp.float32) * (half + rise)
    return sums, pre_act * half, slope, inv_root


def spread_kernel(
    parts_ref, degree_ref, cotangent_ref, weight_ref, bias_ref, out_ref, done_ref
):
    tiles, edge = degree_ref.shape
    weight = weight_ref[...]
    roots = root_columns(degree_ref[...])
    for tile in range(tiles):
        _, _, slope, inv_root = middle_tile(
            tile, roots, parts_ref, cotangent_ref, weight, bias_ref
        )
        upstream = inv_root * slope
        high = upstream.astype(jnp.bfloat16)
        low = (upstream - high.astype(jnp.float32)).astype(jnp.bfloat16)
        spread = sum(
            lax.dot_general(
                weight, part, (((1,), (1,)), ((), ())), preferred_element_type=jnp.float32
            )
            for part in (high, low)
        ).astype(jnp.bfloat16)
        for shard in range(out_ref.shape[0]):
            out_ref[shard, pl.ds(tile * edge, edge), :] = spread
    done_ref[...] = jnp.zeros_like(done_ref)


def middle_kernel(
    place_ref,
    parts_ref,
    degree_ref,
    cotangent_ref,
    weight_ref,
    bias_ref,
    act_ref,
    keep_ref,
    send_ref,
):
    tiles, edge = degree_ref.shape
    weight = weight_ref[...]
    height = weight.shape[0]
    roots = root_columns(degree_ref[...])
    grads = jnp.zeros(weight.shape, jnp.float32)
    bias_row = jnp.zeros(bias_ref.shape, jnp.float32)
    for tile in range(tiles):
        sums, activations, slope, inv_root = middle_tile(
            tile, roots, parts_ref, cotangent_ref, weight, bias_ref
        )
        act_ref[pl.ds(tile * edge, edge), :] = activations.astype(jnp.bfloat16)
        upstream = (inv_root * slope).astype(jnp.bfloat16)
        grads += split_product(sums, upstream, ((0,), (0,)))
        bias_row += jnp.sum(slope, axis=0, keepdims=True)
    width = keep_ref.shape[1]
    first = place_ref[0] % 2 == 0

    def put(target, left):
        pick = lambda whole: jnp.where(left, whole[:, :width], whole[:, width:])
        target[:height, :] = pick(grads)
        row_ids = lax.broadcasted_iota(jnp.int32, (BIAS_ROWS, width), 0)
        target[height:, :] = jnp.where(row_ids == 0, pick(bias_row), 0.0)

    put(keep_ref, first)
    put(send_ref, jnp.logical_not(first))


def sum_of_four(parts_ref, rows):
    part = lambda index: parts_ref[index, rows, :].astype(jnp.float32)
    return (part(0) + part(2)) + (part(1) + part(3))


def terms_to_send(grads_ref):
    height = grads_ref.shape[0] - BIAS_ROWS
    bias = grads_ref[height:, :]
    high = bias.astype(jnp.bfloat16).astype(jnp.float32)
    row_ids = lax.broadcasted_iota(jnp.int32, bias.shape, 0)
    low = jnp.broadcast_to((bias - high)[0:1, :], bias.shape)
    bias = jnp.where(row_ids == 1, low, high)
    return jnp.concatenate([grads_ref[:height, :], bias], 0).astype(jnp.bfloat16)


def far_join_kernel(keep_ref, got_ref, grads_ref, out_ref, terms_ref):
    half = keep_ref.shape[0]
    out_ref[:half, :] = (keep_ref[...] + got_ref[...].astype(jnp.float32)).astype(jnp.bfloat16)
    terms = terms_to_send(grads_ref)
    out_ref[half:, :] = terms
    terms_ref[...] = terms


def near_join_kernel(keep_ref, got_ref, far_ref, terms_ref, out_ref, grads_ref):
    shards, own, _ = out_ref.shape
    for shard in range(shards):
        rows = pl.ds(shard * own, own)
        total = keep_ref[rows, :] + got_ref[rows, :].astype(jnp.float32)
        out_ref[shard] = (total + far_ref[rows, :].astype(jnp.float32)).astype(jnp.bfloat16)
    grads = terms_ref[...].astype(jnp.float32)
    grads += far_ref[shards * own :, :].astype(jnp.float32)
    height = grads.shape[0] - BIAS_ROWS
    grads_ref[:height, :] = grads[:height, :]
    bias = grads[height : height + 1, :] + grads[height + 1 : height + 2, :]
    grads_ref[height:, :] = jnp.broadcast_to(bias, (BIAS_ROWS, bias.shape[1]))


def features_kernel(parts_ref, degree_ref, features_ref):
    tiles, edge = degree_ref.shape
    roots = lax.rsqrt(degree_ref[...].astype(jnp.float32))
    for tile in range(tiles):
        rows = pl.ds(tile * edge, edge)
        total = sum_of_four(parts_ref, rows)
        features_ref[rows, :] = (total * roots[tile : tile + 1, :]).T.astype(jnp.bfloat16)


def lay_out_kernel(place_ref, mine_ref, other_ref, grads_ref, bias_ref):
    first = place_ref[0] % 2 == 0
    height = grads_ref.shape[0]
    width = mine_ref.shape[1]
    mine, other = mine_ref[...], other_ref[...]
    halves = (jnp.where(first, mine, other), jnp.where(first, other, mine))
    for index, half in enumerate(halves):
        lanes = pl.ds(index * width, width)
        grads_ref[:, lanes] = half[:height, :]
        bias_ref[:, lanes] = half[height : height + 1, :]


def per_device(
    features,
    degree,
    cotangent,
    weight,
    layer_bias,
    patterns,
    tile_row,
    tile_col,
    tile_pattern,
    tile_weight,
    tile_count,
):
    node_dev, feature_count = features.shape
    hidden = weight.shape[1]
    row_devices = lax.axis_size("row")
    col_devices = lax.axis_size("col")
    chips = row_devices // 2
    edge = patterns.shape[1]
    per_shard = node_dev // edge
    row = lax.axis_index("row")
    swap = [(index, index ^ 1) for index in range(row_devices)]
    row_near = [
        [(low * 4 + ring) * 2 + core_index for ring in pair for low in range(2)]
        for core_index in range(2)
        for pair in PAIRS[core_index]
    ]
    row_far = [
        (index, (index // 8 * 4 + far_neighbour(index // 2 % 4, index % 2)) * 2 + index % 2)
        for index in range(row_devices)
    ]
    col_steps = [
        [
            (index * col_devices + place, index * col_devices + peer(place, index % 2))
            for index in range(row_devices)
            for place in range(col_devices)
        ]
        for peer in (
            lambda place, core: far_neighbour(place // 2, core) * 2 + place % 2,
            lambda place, core: far_neighbour(place // 2, 1 - core) * 2 + place % 2,
            lambda place, core: place ^ 1,
        )
    ]
    row_close = [
        (index, (index // 8 * 4 + far_neighbour(index // 2 % 4, 1 - index % 2)) * 2 + index % 2)
        for index in range(row_devices)
    ]
    row_low = [(index, index ^ 8) for index in range(row_devices)]
    both = ("row", "col")
    exchange = functools.partial(lax.all_to_all, split_axis=0, concat_axis=0)
    extra = feature_count + BIAS_ROWS
    half = chips * node_dev
    bf16, f32 = jnp.bfloat16, jnp.float32
    shape = jax.ShapeDtypeStruct
    degree_tiles = degree.reshape(per_shard, edge)
    tile_cost = pl.CostEstimate(
        flops=tile_row.size // (row_devices * col_devices) * edge * edge * feature_count,
        bytes_accessed=patterns.size * 2 + 4 * half * feature_count * 2,
        transcendentals=0,
    )

    scaled = pl.pallas_call(
        scale_kernel,
        out_shape=shape((4, node_dev, feature_count), bf16),
        in_specs=[HBM] * 2,
        out_specs=VMEM,
        scratch_shapes=[
            pltpu.VMEM(features.shape, bf16),
            pltpu.VMEM(degree_tiles.shape, jnp.int32),
            pltpu.SemaphoreType.DMA((2,)),
        ],
        compiler_params=PARAMS,
    )(features, degree_tiles)
    near_own = exchange(scaled, "row", axis_index_groups=row_near).reshape(half // 2, feature_count)
    near_other = lax.ppermute(near_own, "row", swap)
    far_own = lax.ppermute(near_own, "row", row_far)
    row_tiles, near_own = lax.optimization_barrier((tile_row.reshape(per_shard, edge), near_own))
    place = row.astype(jnp.int32).reshape(1)
    slots = pl.pallas_call(
        order_kernel,
        out_shape=shape((1, ORDERED), jnp.int32),
        in_specs=[SMEM] * 2 + [HBM] * 4,
        out_specs=VMEM,
        scratch_shapes=[
            pltpu.VMEM((4, per_shard, edge), jnp.int32),
            pltpu.SemaphoreType.DMA((4,)),
        ],
        compiler_params=PARAMS,
    )(
        place,
        tile_count,
        row_tiles,
        tile_col.reshape(per_shard, edge),
        tile_pattern.reshape(per_shard, edge),
        tile_weight.reshape(per_shard, edge),
    )
    forward_panel = pltpu.VMEM((half, feature_count), bf16)
    row_sums = shape((col_devices * node_dev, feature_count), f32)
    near_sums = pl.pallas_call(
        forward_near_kernel,
        out_shape=row_sums,
        in_specs=[SMEM] + [VMEM] * 3,
        out_specs=VMEM,
        scratch_shapes=[forward_panel],
        compiler_params=PARAMS,
        cost_estimate=tile_cost,
    )(slots, patterns, near_own, near_other)
    far_own, near_sums = lax.optimization_barrier((far_own, near_sums))
    far_other = lax.ppermute(far_own, "row", swap)
    row_part = pl.pallas_call(
        forward_far_kernel,
        out_shape=shape(row_sums.shape, bf16),
        in_specs=[SMEM] + [VMEM] * 4,
        out_specs=VMEM,
        scratch_shapes=[forward_panel, pltpu.VMEM(row_sums.shape, f32)],
        compiler_params=PARAMS,
        cost_estimate=tile_cost,
    )(slots, patterns, far_own, far_other, near_sums)
    parts = exchange(row_part.reshape(col_devices, node_dev, feature_count), "col")
    middle_inputs = (parts, degree_tiles, cotangent, weight, layer_bias[None, :])
    spread, done = pl.pallas_call(
        spread_kernel,
        out_shape=(shape((col_devices, node_dev, edge), bf16), shape((8, edge), f32)),
        in_specs=[VMEM] * 5,
        out_specs=(VMEM,) * 2,
        compiler_params=PARAMS,
    )(*middle_inputs)
    spread_all = exchange(spread, "col")
    middle_inputs, _ = lax.optimization_barrier((middle_inputs, done))
    terms = shape((extra, edge), f32)
    activations, keep_terms, send_terms = pl.pallas_call(
        middle_kernel,
        out_shape=(shape((node_dev, hidden), bf16), terms, terms),
        in_specs=[SMEM] + [VMEM] * 5,
        out_specs=(VMEM,) * 3,
        compiler_params=PARAMS,
    )(place, *middle_inputs)
    grads = keep_terms + lax.ppermute(send_terms, "row", swap)
    for pairs in (row_close, row_low):
        grads = grads + lax.ppermute(grads, "row", pairs)
    spread_all, grads, activations = lax.optimization_barrier((spread_all, grads, activations))
    kept, sent = shape((half // 2, edge), f32), shape((half // 2, edge), bf16)
    keep, send = pl.pallas_call(
        backward_far_kernel,
        out_shape=(kept, sent),
        in_specs=[SMEM] + [VMEM] * 2,
        out_specs=(VMEM,) * 2,
        scratch_shapes=[pltpu.VMEM((half, edge), f32)],
        compiler_params=PARAMS,
        cost_estimate=tile_cost,
    )(slots, patterns, spread_all)
    send, step = lax.optimization_barrier((send, lax.ppermute(grads, both, col_steps[0])))
    grads = grads + step
    got = lax.ppermute(send, "row", swap)
    step = lax.ppermute(grads, both, col_steps[1])
    got, step = lax.optimization_barrier((got, step))
    far_sums, own_terms = pl.pallas_call(
        far_join_kernel,
        out_shape=(shape((half // 2 + extra, edge), bf16), shape((extra, edge), bf16)),
        in_specs=[VMEM] * 3,
        out_specs=(VMEM,) * 2,
        compiler_params=PARAMS,
    )(keep, got, grads + step)
    far_sums, spread_all = lax.optimization_barrier((far_sums, spread_all))
    far_got = lax.ppermute(far_sums, "row", row_far)
    keep, send = pl.pallas_call(
        backward_near_kernel,
        out_shape=(kept, sent),
        in_specs=[SMEM] + [VMEM] * 2,
        out_specs=(VMEM,) * 2,
        scratch_shapes=[pltpu.VMEM((half, edge), f32)],
        compiler_params=PARAMS,
        cost_estimate=tile_cost,
    )(slots, patterns, spread_all)
    got = lax.ppermute(send, "row", swap)
    got, far_got = lax.optimization_barrier((got, far_got))
    joined, grads = pl.pallas_call(
        near_join_kernel,
        out_shape=(shape((4, node_dev, edge), bf16), terms),
        in_specs=[VMEM] * 4,
        out_specs=(VMEM,) * 2,
        compiler_params=PARAMS,
    )(keep, got, far_got, own_terms)
    step = lax.ppermute(grads, both, col_steps[2])
    back_parts = exchange(joined, "row", axis_index_groups=row_near)
    back_parts, step = lax.optimization_barrier((back_parts, step))
    scale_factor = 1.0 / math.sqrt(node_dev * row_devices * col_devices)
    mine = (grads + step) * scale_factor
    other = lax.ppermute(mine, "row", swap)
    grad_features = pl.pallas_call(
        features_kernel,
        out_shape=shape((node_dev, feature_count), bf16),
        in_specs=[VMEM] * 2,
        out_specs=VMEM,
        compiler_params=PARAMS,
    )(back_parts, degree_tiles)
    grad_weight, grad_bias = pl.pallas_call(
        lay_out_kernel,
        out_shape=(shape((feature_count, hidden), f32), shape((1, hidden), f32)),
        in_specs=[SMEM] + [VMEM] * 2,
        out_specs=(VMEM,) * 2,
        compiler_params=PARAMS,
    )(place, mine, other)
    return (activations, grad_features, grad_weight, grad_bias[0])


def solution(mesh):
    in_specs = (
        P(("row", "col"), None),
        P(("row", "col")),
        P(("row", "col"), None),
        P(),
        P(),
        P(),
        P("row", "col", None),
        P("row", "col", None),
        P("row", "col", None),
        P("row", "col", None),
        P("row", "col"),
    )
    out_specs = (P(("row", "col"), None), P(("row", "col"), None), P(), P())
    return jax.shard_map(
        per_device, mesh=mesh, in_specs=in_specs, out_specs=out_specs, check_vma=False
    )
```

```python
import functools
import math

import jax
import jax.numpy as jnp
from jax import lax
from jax.experimental import pallas as pl
from jax.experimental.pallas import tpu as pltpu
from jax.sharding import PartitionSpec as P

GROUP = 64
VMEM_LIMIT = 20 * 1024 * 1024
ROOT_2_PI = math.sqrt(2.0 / math.pi)
CUBIC = 0.044715
BIAS_ROWS = 16
PER_SHARD = 4
CLASSES = 4
ORDERED = 640
BOUNDS = 600
PAIRS = (((0, 1), (2, 3)), ((0, 3), (1, 2)))
HBM = pl.BlockSpec(memory_space=pltpu.HBM)
VMEM = pl.BlockSpec(memory_space=pltpu.VMEM)
SMEM = pl.BlockSpec(memory_space=pltpu.SMEM)
PARAMS = pltpu.CompilerParams(vmem_limit_bytes=VMEM_LIMIT)


def pair_of(place, core):
    return jnp.where(core == 0, place >> 1, (place ^ (place >> 1)) & 1)


def pair_index(place, core):
    return jnp.where(core == 0, place & 1, place >> 1)


def far_neighbour(place, core):
    return place ^ 3 if core == 0 else place ^ 1


def order_kernel(
    place_ref, live_ref, row_hbm, col_hbm, pattern_hbm, weight_hbm, out_ref, fields, sems
):
    sources = (row_hbm, col_hbm, pattern_hbm, weight_hbm)
    copies = [
        pltpu.make_async_copy(source, fields.at[index], sems.at[index])
        for index, source in enumerate(sources)
    ]
    for copy in copies:
        copy.start()
    for copy in copies:
        copy.wait()
    row = place_ref[0]
    _, rows, edge = fields.shape
    tile_row, tile_col = fields[0], fields[1]
    shard = tile_col // PER_SHARD
    parity = shard % 2
    chip = shard // 2
    ring = chip % 4
    tile = tile_col % PER_SHARD
    half = parity ^ (row % 2)
    far = (pair_of(ring, parity) != pair_of((row // 2) % 4, parity)).astype(jnp.int32)
    rank = pair_index(ring, parity) * 2 + chip // 4
    place = (half * 4 + rank) * PER_SHARD + tile
    word = tile_row | (fields[2] << 5) | (fields[3] << 11) | (place << 14)
    slot = lax.broadcasted_iota(jnp.int32, (rows, edge), 0) * edge
    slot += lax.broadcasted_iota(jnp.int32, (rows, edge), 1)
    alive = slot < live_ref[0, 0]
    word = jnp.where(alive, word, 0)
    kind = jnp.where(alive, far * 2 + half, CLASSES)

    flags = [(kind == index).astype(jnp.float32) for index in range(CLASSES + 1)]
    stacked = jnp.concatenate(flags + [jnp.zeros((4, edge), jnp.float32)], 0)
    before = lax.broadcasted_iota(jnp.int32, (edge, edge), 0) < lax.broadcasted_iota(
        jnp.int32, (edge, edge), 1
    )
    earlier = jnp.dot(
        stacked.astype(jnp.bfloat16),
        before.astype(jnp.float32).astype(jnp.bfloat16),
        preferred_element_type=jnp.float32,
    )
    counts = jnp.sum(stacked, axis=1, keepdims=True)
    start = jnp.zeros((1, 1), jnp.float32)
    ends = []
    position = [jnp.zeros((1, edge), jnp.float32) for _ in range(rows)]
    for index in range(CLASSES + 1):
        for line in range(rows):
            at = index * rows + line
            position[line] += flags[index][line : line + 1] * (start + earlier[at : at + 1])
            start = start + counts[at : at + 1]
        ends.append(start)
    turned = jnp.concatenate(position + [jnp.zeros((8 - rows, edge), jnp.float32)], 0).T
    slots = rows * edge
    lanes = lax.broadcasted_iota(jnp.int32, (edge, slots), 1).astype(jnp.float32)
    pieces = jnp.zeros((8, slots), jnp.float32)
    for line in range(rows):
        chosen = (turned[:, line : line + 1] == lanes).astype(jnp.float32).astype(jnp.bfloat16)
        parts = [(word[line : line + 1] >> shift) & 127 for shift in (0, 7, 14)]
        parts = jnp.concatenate(parts + [jnp.zeros((5, edge), jnp.int32)], 0)
        parts = parts.astype(jnp.float32).astype(jnp.bfloat16)
        pieces += jnp.dot(parts, chosen, preferred_element_type=jnp.float32)
    pieces = pieces.astype(jnp.int32)
    out_ref[:, :slots] = pieces[0:1] | (pieces[1:2] << 7) | (pieces[2:3] << 14)
    lane = lax.broadcasted_iota(jnp.int32, (1, out_ref.shape[1] - slots), 1) + slots
    tail = jnp.zeros(lane.shape, jnp.int32)
    for index in range(CLASSES):
        tail = jnp.where(lane == BOUNDS + index, ends[index].astype(jnp.int32), tail)
    out_ref[:, slots:] = tail


def root_columns(degree):
    rows = lax.rsqrt(degree.astype(jnp.float32))
    rows = jnp.concatenate([rows, jnp.ones((8 - rows.shape[0], rows.shape[1]), jnp.float32)], 0)
    return rows.T


def scale_kernel(features_hbm, degree_hbm, out_ref, features_ref, degree_ref, sems):
    copies = (
        pltpu.make_async_copy(degree_hbm, degree_ref, sems.at[0]),
        pltpu.make_async_copy(features_hbm, features_ref, sems.at[1]),
    )
    for copy in copies:
        copy.start()
    copies[0].wait()
    roots = root_columns(degree_ref[...])
    copies[1].wait()
    edge = degree_ref.shape[1]
    for tile in range(degree_ref.shape[0]):
        rows = pl.ds(tile * edge, edge)
        scaled = features_ref[rows, :].astype(jnp.float32) * roots[:, tile : tile + 1]
        scaled = scaled.astype(jnp.bfloat16)
        for copy in range(out_ref.shape[0]):
            out_ref[copy, rows, :] = scaled


def add_products(slots_ref, first, end, product_of, place_of, sums):
    edge = sums.shape[1]

    def one_group(turn, carry):
        terms = []
        for member in range(GROUP):
            slot = first + turn * GROUP + member
            word = slots_ref[0, slot]
            factor = jnp.where(slot < end, (word >> 11) & 7, 0).astype(jnp.float32)
            terms.append((place_of(word), factor, product_of(word)))
        for place, factor, product in terms:
            rows = pl.ds(pl.multiple_of(place * edge, edge), edge)
            sums[rows, :] += factor * product
        return carry

    lax.fori_loop(0, (end - first + GROUP - 1) // GROUP, one_group, 0)


def class_end(slots_ref, index):
    return slots_ref[0, BOUNDS + index]


def tile_of(ref, place, edge):
    return ref[pl.ds(pl.multiple_of(place * edge, edge), edge), :]


def forward_sums(slots_ref, patterns_ref, panel, sums, first, end):
    edge = patterns_ref.shape[1]

    def product_of(word):
        return jnp.dot(
            patterns_ref[(word >> 5) & 63],
            tile_of(panel, (word >> 14) & 31, edge),
            preferred_element_type=jnp.float32,
        )

    add_products(slots_ref, first, end, product_of, lambda word: word & 31, sums)


def forward_near_kernel(
    slots_from, patterns_ref, own_ref, other_ref, out_ref, slots_ref, sem, panel
):
    copy = pltpu.make_async_copy(slots_from, slots_ref, sem)
    copy.start()
    half = own_ref.shape[0]
    panel[:half, :] = own_ref[...]
    panel[half:, :] = other_ref[...]
    out_ref[...] = jnp.zeros_like(out_ref)
    copy.wait()
    forward_sums(slots_ref, patterns_ref, panel, out_ref, 0, class_end(slots_ref, 1))


def forward_far_kernel(
    slots_from, patterns_ref, own_ref, other_ref, so_far_ref, out_ref, slots_ref, sem, panel, sums
):
    copy = pltpu.make_async_copy(slots_from, slots_ref, sem)
    copy.start()
    half = own_ref.shape[0]
    panel[:half, :] = own_ref[...]
    panel[half:, :] = other_ref[...]
    sums[...] = so_far_ref[...]
    copy.wait()
    first, end = class_end(slots_ref, 1), class_end(slots_ref, 3)
    forward_sums(slots_ref, patterns_ref, panel, sums, first, end)
    out_ref[...] = sums[...].astype(jnp.bfloat16)


def backward_sums(slots_ref, patterns_ref, spread_ref, sums, first, end):
    edge = patterns_ref.shape[1]
    mask = sums.shape[0] // edge - 1

    def product_of(word):
        start = pl.multiple_of((word & 3) * edge, edge)
        return jnp.dot(
            spread_ref[(word >> 2) & 7, pl.ds(start, edge), :],
            patterns_ref[(word >> 5) & 63],
            preferred_element_type=jnp.float32,
        )

    add_products(slots_ref, first, end, product_of, lambda word: (word >> 14) & mask, sums)


def backward_send_kernel(
    slots_from, patterns_ref, spread_ref, send_ref, grads_ref, slots_ref, sem, sums
):
    copy = pltpu.make_async_copy(slots_from, slots_ref, sem)
    copy.start()
    sums[...] = jnp.zeros_like(sums)
    own = spread_ref.shape[1] - grads_ref.shape[0]
    grads = spread_ref[0, own:, :].astype(jnp.float32)
    for shard in range(1, spread_ref.shape[0]):
        grads += spread_ref[shard, own:, :].astype(jnp.float32)
    grads_ref[...] = grads.astype(jnp.bfloat16)
    copy.wait()
    first, end = class_end(slots_ref, 2), class_end(slots_ref, 3)
    backward_sums(slots_ref, patterns_ref, spread_ref, sums, first, end)
    send_ref[...] = sums[...].astype(jnp.bfloat16)


def backward_keep_kernel(slots_from, patterns_ref, spread_ref, keep_ref, slots_ref, sem):
    copy = pltpu.make_async_copy(slots_from, slots_ref, sem)
    copy.start()
    keep_ref[...] = jnp.zeros_like(keep_ref)
    copy.wait()
    first, end = class_end(slots_ref, 1), class_end(slots_ref, 2)
    backward_sums(slots_ref, patterns_ref, spread_ref, keep_ref, first, end)


def backward_near_kernel(
    slots_from, patterns_ref, spread_ref, keep_ref, send_ref, slots_ref, sem, sums
):
    copy = pltpu.make_async_copy(slots_from, slots_ref, sem)
    copy.start()
    sums[...] = jnp.zeros_like(sums)
    copy.wait()
    backward_sums(slots_ref, patterns_ref, spread_ref, sums, 0, class_end(slots_ref, 1))
    half = keep_ref.shape[0]
    keep_ref[...] = sums[:half, :]
    send_ref[...] = sums[half:, :].astype(jnp.bfloat16)


def split_product(left, right, dims):
    high = left.astype(jnp.bfloat16)
    low = (left - high.astype(jnp.float32)).astype(jnp.bfloat16)
    return lax.dot_general(
        high, right, (dims, ((), ())), preferred_element_type=jnp.float32
    ) + lax.dot_general(low, right, (dims, ((), ())), preferred_element_type=jnp.float32)


def activate(pre_act):
    square = pre_act * pre_act
    bent = jnp.tanh(ROOT_2_PI * (pre_act + CUBIC * (pre_act * square)))
    return square, bent, 0.5 * (1.0 + bent)


def middle_kernel(
    place_ref,
    parts_ref,
    degree_ref,
    cotangent_ref,
    weight_ref,
    bias_ref,
    pre_ref,
    upstream_ref,
    keep_ref,
    send_ref,
):
    tiles, edge = degree_ref.shape
    shards = parts_ref.shape[0]
    weight = weight_ref[...]
    height = weight.shape[0]
    roots = root_columns(degree_ref[...])
    grads = jnp.zeros(weight.shape, jnp.float32)
    bias_row = jnp.zeros(bias_ref.shape, jnp.float32)
    for tile in range(tiles):
        rows = pl.ds(tile * edge, edge)
        sums = parts_ref[0, rows, :].astype(jnp.float32)
        for shard in range(1, shards):
            sums += parts_ref[shard, rows, :].astype(jnp.float32)
        inv_root = roots[:, tile : tile + 1]
        pre_act = inv_root * split_product(sums, weight, ((1,), (0,))) + bias_ref[...]
        pre_ref[rows, :] = pre_act
        square, bent, half = activate(pre_act)
        rise = 0.5 * pre_act * (1.0 - bent * bent) * (ROOT_2_PI * (1.0 + 3.0 * CUBIC * square))
        slope = cotangent_ref[rows, :].astype(jnp.float32) * (half + rise)
        upstream = inv_root * slope
        upstream_ref[rows, :] = upstream
        grads += split_product(sums, upstream.astype(jnp.bfloat16), ((0,), (0,)))
        bias_row += jnp.sum(slope, axis=0, keepdims=True)
    width = keep_ref.shape[1]
    bias_high = bias_row.astype(jnp.bfloat16).astype(jnp.float32)
    bias_low = bias_row - bias_high
    first = place_ref[0] % 2 == 0

    def put(target, left):
        pick = lambda whole: jnp.where(left, whole[:, :width], whole[:, width:])
        target[:height, :] = pick(grads).astype(target.dtype)
        row_ids = lax.broadcasted_iota(jnp.int32, (BIAS_ROWS, width), 0)
        block = jnp.where(row_ids == 0, pick(bias_high), 0.0)
        block = jnp.where(row_ids == 1, pick(bias_low), block)
        target[height:, :] = block.astype(target.dtype)

    put(keep_ref, first)
    put(send_ref, jnp.logical_not(first))


def activation_kernel(pre_ref, act_ref):
    pre_act = pre_ref[...]
    act_ref[...] = (pre_act * activate(pre_act)[2]).astype(jnp.bfloat16)


def spread_kernel(upstream_ref, weight_ref, out_ref):
    edge = out_ref.shape[2]
    for tile in range(upstream_ref.shape[0] // edge):
        rows = pl.ds(tile * edge, edge)
        upstream = upstream_ref[rows, :]
        high = upstream.astype(jnp.bfloat16)
        low = (upstream - high.astype(jnp.float32)).astype(jnp.bfloat16)
        spread = sum(
            lax.dot_general(
                weight_ref[...], part, (((1,), (1,)), ((), ())), preferred_element_type=jnp.float32
            )
            for part in (high, low)
        ).astype(jnp.bfloat16)
        for shard in range(out_ref.shape[0]):
            out_ref[shard, rows, :] = spread


def append_kernel(keep_ref, got_ref, spread_ref, out_ref):
    terms = (keep_ref[...] + got_ref[...].astype(jnp.float32)).astype(jnp.bfloat16)
    rows = pl.ds(out_ref.shape[1] - terms.shape[0], terms.shape[0])
    for shard in range(out_ref.shape[0]):
        out_ref[shard, rows, :] = terms


def sum_of_four(parts_ref, rows):
    part = lambda index: parts_ref[index, rows, :].astype(jnp.float32)
    return (part(0) + part(2)) + (part(1) + part(3))


def far_join_kernel(keep_ref, got_ref, grads_ref, out_ref):
    half = keep_ref.shape[0]
    out_ref[:half, :] = (keep_ref[...] + got_ref[...].astype(jnp.float32)).astype(jnp.bfloat16)
    out_ref[half:, :] = grads_ref[...]


def near_join_kernel(keep_ref, got_ref, far_ref, grads_ref, out_ref):
    shards = out_ref.shape[0]
    half = keep_ref.shape[0]
    own = half // shards
    grads = grads_ref[...].astype(jnp.float32) + far_ref[half:, :].astype(jnp.float32)
    grads = grads.astype(jnp.bfloat16)
    for shard in range(shards):
        rows = pl.ds(shard * own, own)
        total = keep_ref[rows, :] + got_ref[rows, :].astype(jnp.float32)
        total += far_ref[rows, :].astype(jnp.float32)
        out_ref[shard, pl.ds(0, own), :] = total.astype(jnp.bfloat16)
        out_ref[shard, pl.ds(own, grads.shape[0]), :] = grads


def total_kernel(scale_factor, parts_ref, half_ref):
    extra = half_ref.shape[0] - 8 + BIAS_ROWS
    tail = sum_of_four(parts_ref, pl.ds(parts_ref.shape[1] - extra, extra))
    tail = tail * scale_factor
    height = half_ref.shape[0] - 8
    half_ref[:height, :] = tail[:height, :]
    bias_row = tail[height : height + 1, :] + tail[height + 1 : height + 2, :]
    half_ref[height:, :] = jnp.broadcast_to(bias_row, (8, bias_row.shape[1]))


def features_kernel(parts_ref, degree_ref, features_ref):
    tiles, edge = degree_ref.shape
    roots = lax.rsqrt(degree_ref[...].astype(jnp.float32))
    for tile in range(tiles):
        rows = pl.ds(tile * edge, edge)
        total = sum_of_four(parts_ref, rows)
        features_ref[rows, :] = (total * roots[tile : tile + 1, :]).T.astype(jnp.bfloat16)


def lay_out_kernel(place_ref, mine_ref, other_ref, grads_ref, bias_ref):
    first = place_ref[0] % 2 == 0
    height = grads_ref.shape[0]
    width = mine_ref.shape[1]
    mine, other = mine_ref[...], other_ref[...]
    halves = (jnp.where(first, mine, other), jnp.where(first, other, mine))
    for index, half in enumerate(halves):
        lanes = pl.ds(index * width, width)
        grads_ref[:, lanes] = half[:height, :]
        bias_ref[:, lanes] = half[height : height + 1, :]


def per_device(
    features,
    degree,
    cotangent,
    weight,
    layer_bias,
    patterns,
    tile_row,
    tile_col,
    tile_pattern,
    tile_weight,
    tile_count,
):
    node_dev, feature_count = features.shape
    hidden = weight.shape[1]
    row_devices = lax.axis_size("row")
    col_devices = lax.axis_size("col")
    chips = row_devices // 2
    edge = patterns.shape[1]
    per_shard = node_dev // edge
    row = lax.axis_index("row")
    swap = [(index, index ^ 1) for index in range(row_devices)]
    row_near = [
        [(low * 4 + ring) * 2 + core_index for ring in pair for low in range(2)]
        for core_index in range(2)
        for pair in PAIRS[core_index]
    ]
    row_far = [
        (index, (index // 8 * 4 + far_neighbour(index // 2 % 4, index % 2)) * 2 + index % 2)
        for index in range(row_devices)
    ]
    exchange = functools.partial(lax.all_to_all, split_axis=0, concat_axis=0)
    extra = feature_count + BIAS_ROWS
    half = chips * node_dev
    bf16, f32 = jnp.bfloat16, jnp.float32
    shape = jax.ShapeDtypeStruct
    degree_tiles = degree.reshape(per_shard, edge)
    tile_cost = pl.CostEstimate(
        flops=tile_row.size // (row_devices * col_devices) * edge * edge * feature_count,
        bytes_accessed=patterns.size * 2 + 4 * half * feature_count * 2,
        transcendentals=0,
    )

    scaled = pl.pallas_call(
        scale_kernel,
        out_shape=shape((4, node_dev, feature_count), bf16),
        in_specs=[HBM] * 2,
        out_specs=VMEM,
        scratch_shapes=[
            pltpu.VMEM(features.shape, bf16),
            pltpu.VMEM(degree_tiles.shape, jnp.int32),
            pltpu.SemaphoreType.DMA((2,)),
        ],
        compiler_params=pltpu.CompilerParams(vmem_limit_bytes=62 * 1024 * 1024),
    )(features, degree_tiles)
    near_own = exchange(scaled, "row", axis_index_groups=row_near).reshape(half // 2, feature_count)
    near_other = lax.ppermute(near_own, "row", swap)
    far_own = lax.ppermute(near_own, "row", row_far)
    row_tiles, near_own = lax.optimization_barrier((tile_row.reshape(per_shard, edge), near_own))
    place = row.astype(jnp.int32).reshape(1)
    slots = pl.pallas_call(
        order_kernel,
        out_shape=shape((1, ORDERED), jnp.int32),
        in_specs=[SMEM] * 2 + [HBM] * 4,
        out_specs=VMEM,
        scratch_shapes=[
            pltpu.VMEM((4, per_shard, edge), jnp.int32),
            pltpu.SemaphoreType.DMA((4,)),
        ],
        compiler_params=PARAMS,
    )(
        place,
        tile_count,
        row_tiles,
        tile_col.reshape(per_shard, edge),
        tile_pattern.reshape(per_shard, edge),
        tile_weight.reshape(per_shard, edge),
    )
    slots_scratch = [pltpu.SMEM((1, ORDERED), jnp.int32), pltpu.SemaphoreType.DMA]
    forward_panel = pltpu.VMEM((half, feature_count), bf16)
    row_sums = shape((col_devices * node_dev, feature_count), f32)
    near_sums = pl.pallas_call(
        forward_near_kernel,
        out_shape=row_sums,
        in_specs=[HBM] + [VMEM] * 3,
        out_specs=VMEM,
        scratch_shapes=[*slots_scratch, forward_panel],
        compiler_params=PARAMS,
        cost_estimate=tile_cost,
    )(slots, patterns, near_own, near_other)
    far_own, near_sums = lax.optimization_barrier((far_own, near_sums))
    far_other = lax.ppermute(far_own, "row", swap)
    row_part = pl.pallas_call(
        forward_far_kernel,
        out_shape=shape(row_sums.shape, bf16),
        in_specs=[HBM] + [VMEM] * 4,
        out_specs=VMEM,
        scratch_shapes=[*slots_scratch, forward_panel, pltpu.VMEM(row_sums.shape, f32)],
        compiler_params=PARAMS,
        cost_estimate=tile_cost,
    )(slots, patterns, far_own, far_other, near_sums)
    parts = exchange(row_part.reshape(col_devices, node_dev, feature_count), "col")
    pre_act, upstream, keep_terms, send_terms = pl.pallas_call(
        middle_kernel,
        out_shape=(
            shape((node_dev, hidden), f32),
            shape((node_dev, hidden), f32),
            shape((extra, edge), f32),
            shape((extra, edge), bf16),
        ),
        in_specs=[SMEM] + [VMEM] * 5,
        out_specs=(VMEM,) * 4,
        compiler_params=PARAMS,
    )(place, parts, degree_tiles, cotangent, weight, layer_bias[None, :])
    got_terms = lax.ppermute(send_terms, "row", swap)
    spread = pl.pallas_call(
        spread_kernel,
        out_shape=shape((col_devices, node_dev + extra, edge), bf16),
        in_specs=[VMEM] * 2,
        out_specs=VMEM,
        compiler_params=PARAMS,
    )(upstream, weight)
    spread = pl.pallas_call(
        append_kernel,
        out_shape=shape(spread.shape, bf16),
        in_specs=[VMEM] * 3,
        out_specs=VMEM,
        input_output_aliases={2: 0},
        compiler_params=PARAMS,
    )(keep_terms, got_terms, spread)
    spread_all = exchange(spread, "col")
    kept, sent = shape((half // 2, edge), f32), shape((half // 2, edge), bf16)
    send, grads = pl.pallas_call(
        backward_send_kernel,
        out_shape=(sent, shape((extra, edge), bf16)),
        in_specs=[HBM] + [VMEM] * 2,
        out_specs=(VMEM,) * 2,
        scratch_shapes=[*slots_scratch, pltpu.VMEM(kept.shape, f32)],
        compiler_params=PARAMS,
        cost_estimate=tile_cost,
    )(slots, patterns, spread_all)
    send, spread_all = lax.optimization_barrier((send, spread_all))
    got = lax.ppermute(send, "row", swap)
    keep = pl.pallas_call(
        backward_keep_kernel,
        out_shape=kept,
        in_specs=[HBM] + [VMEM] * 2,
        out_specs=VMEM,
        scratch_shapes=slots_scratch,
        compiler_params=PARAMS,
        cost_estimate=tile_cost,
    )(slots, patterns, spread_all)
    far_sums = pl.pallas_call(
        far_join_kernel,
        out_shape=shape((half // 2 + extra, edge), bf16),
        in_specs=[VMEM] * 3,
        out_specs=VMEM,
        compiler_params=PARAMS,
    )(keep, got, grads)
    far_sums, spread_all = lax.optimization_barrier((far_sums, spread_all))
    far_got = lax.ppermute(far_sums, "row", row_far)
    keep, send = pl.pallas_call(
        backward_near_kernel,
        out_shape=(kept, sent),
        in_specs=[HBM] + [VMEM] * 2,
        out_specs=(VMEM,) * 2,
        scratch_shapes=[*slots_scratch, pltpu.VMEM((half, edge), f32)],
        compiler_params=PARAMS,
        cost_estimate=tile_cost,
    )(slots, patterns, spread_all)
    got = lax.ppermute(send, "row", swap)
    pre_act, keep = lax.optimization_barrier((pre_act, keep))
    activations = pl.pallas_call(
        activation_kernel,
        out_shape=shape((node_dev, hidden), bf16),
        in_specs=[VMEM],
        out_specs=VMEM,
        compiler_params=PARAMS,
    )(pre_act)
    got, far_got, activations = lax.optimization_barrier((got, far_got, activations))
    joined = pl.pallas_call(
        near_join_kernel,
        out_shape=shape((4, node_dev + extra, edge), bf16),
        in_specs=[VMEM] * 4,
        out_specs=VMEM,
        compiler_params=PARAMS,
    )(keep, got, far_got, grads)
    back_parts = exchange(joined, "row", axis_index_groups=row_near)
    scale_factor = 1.0 / math.sqrt(node_dev * row_devices * col_devices)
    mine = pl.pallas_call(
        functools.partial(total_kernel, scale_factor),
        out_shape=shape((feature_count + 8, edge), f32),
        in_specs=[VMEM],
        out_specs=VMEM,
        compiler_params=PARAMS,
    )(back_parts)
    other = lax.ppermute(mine, "row", swap)
    grad_features = pl.pallas_call(
        features_kernel,
        out_shape=shape((node_dev, feature_count), bf16),
        in_specs=[VMEM] * 2,
        out_specs=VMEM,
        compiler_params=PARAMS,
    )(back_parts, degree_tiles)
    grad_weight, grad_bias = pl.pallas_call(
        lay_out_kernel,
        out_shape=(shape((feature_count, hidden), f32), shape((1, hidden), f32)),
        in_specs=[SMEM] + [VMEM] * 2,
        out_specs=(VMEM,) * 2,
        compiler_params=PARAMS,
    )(place, mine, other)
    return (activations, grad_features, grad_weight, grad_bias[0])


def solution(mesh):
    in_specs = (
        P(("row", "col"), None),
        P(("row", "col")),
        P(("row", "col"), None),
        P(),
        P(),
        P(),
        P("row", "col", None),
        P("row", "col", None),
        P("row", "col", None),
        P("row", "col", None),
        P("row", "col"),
    )
    out_specs = (P(("row", "col"), None), P(("row", "col"), None), P(), P())
    return jax.shard_map(
        per_device, mesh=mesh, in_specs=in_specs, out_specs=out_specs, check_vma=False
    )
```

```python
import functools
import math

import jax
import jax.numpy as jnp
from jax import lax
from jax.experimental import pallas as pl
from jax.experimental.pallas import tpu as pltpu
from jax.sharding import PartitionSpec as P

GROUP = 64
VMEM_LIMIT = 20 * 1024 * 1024
ROOT_2_PI = math.sqrt(2.0 / math.pi)
CUBIC = 0.044715
BIAS_ROWS = 16
PER_SHARD = 4
CLASSES = 4
ORDERED = 640
BOUNDS = 600
PAIRS = (((0, 1), (2, 3)), ((0, 3), (1, 2)))
HBM = pl.BlockSpec(memory_space=pltpu.HBM)
VMEM = pl.BlockSpec(memory_space=pltpu.VMEM)
SMEM = pl.BlockSpec(memory_space=pltpu.SMEM)
PARAMS = pltpu.CompilerParams(vmem_limit_bytes=VMEM_LIMIT)


def pair_of(place, core):
    return jnp.where(core == 0, place >> 1, (place ^ (place >> 1)) & 1)


def pair_index(place, core):
    return jnp.where(core == 0, place & 1, place >> 1)


def far_neighbour(place, core):
    return place ^ 3 if core == 0 else place ^ 1


def order_kernel(
    place_ref, live_ref, row_hbm, col_hbm, pattern_hbm, weight_hbm, out_ref, fields, sems
):
    sources = (row_hbm, col_hbm, pattern_hbm, weight_hbm)
    copies = [
        pltpu.make_async_copy(source, fields.at[index], sems.at[index])
        for index, source in enumerate(sources)
    ]
    for copy in copies:
        copy.start()
    for copy in copies:
        copy.wait()
    row = place_ref[0]
    _, rows, edge = fields.shape
    tile_row, tile_col = fields[0], fields[1]
    shard = tile_col // PER_SHARD
    parity = shard % 2
    chip = shard // 2
    ring = chip % 4
    tile = tile_col % PER_SHARD
    half = parity ^ (row % 2)
    far = (pair_of(ring, parity) != pair_of((row // 2) % 4, parity)).astype(jnp.int32)
    rank = pair_index(ring, parity) * 2 + chip // 4
    place = (half * 4 + rank) * PER_SHARD + tile
    word = tile_row | (fields[2] << 5) | (fields[3] << 11) | (place << 14)
    slot = lax.broadcasted_iota(jnp.int32, (rows, edge), 0) * edge
    slot += lax.broadcasted_iota(jnp.int32, (rows, edge), 1)
    alive = slot < live_ref[0, 0]
    word = jnp.where(alive, word, 0)
    kind = jnp.where(alive, far * 2 + half, CLASSES)

    flags = [(kind == index).astype(jnp.float32) for index in range(CLASSES + 1)]
    stacked = jnp.concatenate(flags + [jnp.zeros((4, edge), jnp.float32)], 0)
    before = lax.broadcasted_iota(jnp.int32, (edge, edge), 0) < lax.broadcasted_iota(
        jnp.int32, (edge, edge), 1
    )
    earlier = jnp.dot(
        stacked.astype(jnp.bfloat16),
        before.astype(jnp.float32).astype(jnp.bfloat16),
        preferred_element_type=jnp.float32,
    )
    counts = jnp.sum(stacked, axis=1, keepdims=True)
    start = jnp.zeros((1, 1), jnp.float32)
    ends = []
    position = [jnp.zeros((1, edge), jnp.float32) for _ in range(rows)]
    for index in range(CLASSES + 1):
        for line in range(rows):
            at = index * rows + line
            position[line] += flags[index][line : line + 1] * (start + earlier[at : at + 1])
            start = start + counts[at : at + 1]
        ends.append(start)
    turned = jnp.concatenate(position + [jnp.zeros((8 - rows, edge), jnp.float32)], 0).T
    slots = rows * edge
    lanes = lax.broadcasted_iota(jnp.int32, (edge, slots), 1).astype(jnp.float32)
    pieces = jnp.zeros((8, slots), jnp.float32)
    for line in range(rows):
        chosen = (turned[:, line : line + 1] == lanes).astype(jnp.float32).astype(jnp.bfloat16)
        parts = [(word[line : line + 1] >> shift) & 127 for shift in (0, 7, 14)]
        parts = jnp.concatenate(parts + [jnp.zeros((5, edge), jnp.int32)], 0)
        parts = parts.astype(jnp.float32).astype(jnp.bfloat16)
        pieces += jnp.dot(parts, chosen, preferred_element_type=jnp.float32)
    pieces = pieces.astype(jnp.int32)
    out_ref[:, :slots] = pieces[0:1] | (pieces[1:2] << 7) | (pieces[2:3] << 14)
    lane = lax.broadcasted_iota(jnp.int32, (1, out_ref.shape[1] - slots), 1) + slots
    tail = jnp.zeros(lane.shape, jnp.int32)
    for index in range(CLASSES):
        tail = jnp.where(lane == BOUNDS + index, ends[index].astype(jnp.int32), tail)
    out_ref[:, slots:] = tail


def root_columns(degree):
    rows = lax.rsqrt(degree.astype(jnp.float32))
    rows = jnp.concatenate([rows, jnp.ones((8 - rows.shape[0], rows.shape[1]), jnp.float32)], 0)
    return rows.T


def scale_kernel(features_hbm, degree_hbm, out_ref, features_ref, degree_ref, sems):
    copies = (
        pltpu.make_async_copy(degree_hbm, degree_ref, sems.at[0]),
        pltpu.make_async_copy(features_hbm, features_ref, sems.at[1]),
    )
    for copy in copies:
        copy.start()
    copies[0].wait()
    roots = root_columns(degree_ref[...])
    copies[1].wait()
    edge = degree_ref.shape[1]
    for tile in range(degree_ref.shape[0]):
        rows = pl.ds(tile * edge, edge)
        scaled = features_ref[rows, :].astype(jnp.float32) * roots[:, tile : tile + 1]
        scaled = scaled.astype(jnp.bfloat16)
        for copy in range(out_ref.shape[0]):
            out_ref[copy, rows, :] = scaled


def add_products(slots_ref, first, end, product_of, place_of, sums):
    edge = sums.shape[1]

    def one_group(turn, carry):
        terms = []
        for member in range(GROUP):
            slot = first + turn * GROUP + member
            word = slots_ref[0, slot]
            factor = jnp.where(slot < end, (word >> 11) & 7, 0).astype(jnp.float32)
            terms.append((place_of(word), factor, product_of(word)))
        for place, factor, product in terms:
            rows = pl.ds(pl.multiple_of(place * edge, edge), edge)
            sums[rows, :] += factor * product
        return carry

    lax.fori_loop(0, (end - first + GROUP - 1) // GROUP, one_group, 0)


def class_end(slots_ref, index):
    return slots_ref[0, BOUNDS + index]


def tile_of(ref, place, edge):
    return ref[pl.ds(pl.multiple_of(place * edge, edge), edge), :]


def forward_sums(slots_ref, patterns_ref, panel, sums, first, end):
    edge = patterns_ref.shape[1]

    def product_of(word):
        return jnp.dot(
            patterns_ref[(word >> 5) & 63],
            tile_of(panel, (word >> 14) & 31, edge),
            preferred_element_type=jnp.float32,
        )

    add_products(slots_ref, first, end, product_of, lambda word: word & 31, sums)


def forward_near_kernel(
    slots_from, patterns_ref, own_ref, other_ref, out_ref, slots_ref, sem, panel
):
    copy = pltpu.make_async_copy(slots_from, slots_ref, sem)
    copy.start()
    half = own_ref.shape[0]
    panel[:half, :] = own_ref[...]
    panel[half:, :] = other_ref[...]
    out_ref[...] = jnp.zeros_like(out_ref)
    copy.wait()
    forward_sums(slots_ref, patterns_ref, panel, out_ref, 0, class_end(slots_ref, 1))


def forward_far_kernel(
    slots_from, patterns_ref, own_ref, other_ref, so_far_ref, out_ref, slots_ref, sem, panel, sums
):
    copy = pltpu.make_async_copy(slots_from, slots_ref, sem)
    copy.start()
    half = own_ref.shape[0]
    panel[:half, :] = own_ref[...]
    panel[half:, :] = other_ref[...]
    sums[...] = so_far_ref[...]
    copy.wait()
    first, end = class_end(slots_ref, 1), class_end(slots_ref, 3)
    forward_sums(slots_ref, patterns_ref, panel, sums, first, end)
    out_ref[...] = sums[...].astype(jnp.bfloat16)


def backward_sums(slots_ref, patterns_ref, spread_ref, sums, first, end):
    edge = patterns_ref.shape[1]
    mask = sums.shape[0] // edge - 1

    def product_of(word):
        start = pl.multiple_of((word & 3) * edge, edge)
        return jnp.dot(
            spread_ref[(word >> 2) & 7, pl.ds(start, edge), :],
            patterns_ref[(word >> 5) & 63],
            preferred_element_type=jnp.float32,
        )

    add_products(slots_ref, first, end, product_of, lambda word: (word >> 14) & mask, sums)


def backward_send_kernel(
    slots_from, patterns_ref, spread_ref, send_ref, grads_ref, slots_ref, sem, sums
):
    copy = pltpu.make_async_copy(slots_from, slots_ref, sem)
    copy.start()
    sums[...] = jnp.zeros_like(sums)
    own = spread_ref.shape[1] - grads_ref.shape[0]
    grads = spread_ref[0, own:, :].astype(jnp.float32)
    for shard in range(1, spread_ref.shape[0]):
        grads += spread_ref[shard, own:, :].astype(jnp.float32)
    grads_ref[...] = grads.astype(jnp.bfloat16)
    copy.wait()
    first, end = class_end(slots_ref, 2), class_end(slots_ref, 3)
    backward_sums(slots_ref, patterns_ref, spread_ref, sums, first, end)
    send_ref[...] = sums[...].astype(jnp.bfloat16)


def backward_keep_kernel(slots_from, patterns_ref, spread_ref, keep_ref, slots_ref, sem):
    copy = pltpu.make_async_copy(slots_from, slots_ref, sem)
    copy.start()
    keep_ref[...] = jnp.zeros_like(keep_ref)
    copy.wait()
    first, end = class_end(slots_ref, 1), class_end(slots_ref, 2)
    backward_sums(slots_ref, patterns_ref, spread_ref, keep_ref, first, end)


def backward_near_kernel(
    slots_from, patterns_ref, spread_ref, keep_ref, send_ref, slots_ref, sem, sums
):
    copy = pltpu.make_async_copy(slots_from, slots_ref, sem)
    copy.start()
    sums[...] = jnp.zeros_like(sums)
    copy.wait()
    backward_sums(slots_ref, patterns_ref, spread_ref, sums, 0, class_end(slots_ref, 1))
    half = keep_ref.shape[0]
    keep_ref[...] = sums[:half, :]
    send_ref[...] = sums[half:, :].astype(jnp.bfloat16)


def split_product(left, right, dims):
    high = left.astype(jnp.bfloat16)
    low = (left - high.astype(jnp.float32)).astype(jnp.bfloat16)
    return lax.dot_general(
        high, right, (dims, ((), ())), preferred_element_type=jnp.float32
    ) + lax.dot_general(low, right, (dims, ((), ())), preferred_element_type=jnp.float32)


def activate(pre_act):
    square = pre_act * pre_act
    bent = jnp.tanh(ROOT_2_PI * (pre_act + CUBIC * (pre_act * square)))
    return square, bent, 0.5 * (1.0 + bent)


def middle_kernel(
    place_ref,
    parts_ref,
    degree_ref,
    cotangent_ref,
    weight_ref,
    bias_ref,
    pre_ref,
    upstream_ref,
    keep_ref,
    send_ref,
):
    tiles, edge = degree_ref.shape
    shards = parts_ref.shape[0]
    weight = weight_ref[...]
    height = weight.shape[0]
    roots = root_columns(degree_ref[...])
    grads = jnp.zeros(weight.shape, jnp.float32)
    bias_row = jnp.zeros(bias_ref.shape, jnp.float32)
    for tile in range(tiles):
        rows = pl.ds(tile * edge, edge)
        sums = parts_ref[0, rows, :].astype(jnp.float32)
        for shard in range(1, shards):
            sums += parts_ref[shard, rows, :].astype(jnp.float32)
        inv_root = roots[:, tile : tile + 1]
        pre_act = inv_root * split_product(sums, weight, ((1,), (0,))) + bias_ref[...]
        pre_ref[rows, :] = pre_act
        square, bent, half = activate(pre_act)
        rise = 0.5 * pre_act * (1.0 - bent * bent) * (ROOT_2_PI * (1.0 + 3.0 * CUBIC * square))
        slope = cotangent_ref[rows, :].astype(jnp.float32) * (half + rise)
        upstream = inv_root * slope
        upstream_ref[rows, :] = upstream
        grads += split_product(sums, upstream.astype(jnp.bfloat16), ((0,), (0,)))
        bias_row += jnp.sum(slope, axis=0, keepdims=True)
    width = keep_ref.shape[1]
    bias_high = bias_row.astype(jnp.bfloat16).astype(jnp.float32)
    bias_low = bias_row - bias_high
    first = place_ref[0] % 2 == 0

    def put(target, left):
        pick = lambda whole: jnp.where(left, whole[:, :width], whole[:, width:])
        target[:height, :] = pick(grads).astype(target.dtype)
        row_ids = lax.broadcasted_iota(jnp.int32, (BIAS_ROWS, width), 0)
        block = jnp.where(row_ids == 0, pick(bias_high), 0.0)
        block = jnp.where(row_ids == 1, pick(bias_low), block)
        target[height:, :] = block.astype(target.dtype)

    put(keep_ref, first)
    put(send_ref, jnp.logical_not(first))


def activation_kernel(pre_ref, act_ref):
    pre_act = pre_ref[...]
    act_ref[...] = (pre_act * activate(pre_act)[2]).astype(jnp.bfloat16)


def spread_kernel(upstream_ref, weight_ref, out_ref):
    edge = out_ref.shape[2]
    for tile in range(upstream_ref.shape[0] // edge):
        rows = pl.ds(tile * edge, edge)
        upstream = upstream_ref[rows, :]
        high = upstream.astype(jnp.bfloat16)
        low = (upstream - high.astype(jnp.float32)).astype(jnp.bfloat16)
        spread = sum(
            lax.dot_general(
                weight_ref[...], part, (((1,), (1,)), ((), ())), preferred_element_type=jnp.float32
            )
            for part in (high, low)
        ).astype(jnp.bfloat16)
        for shard in range(out_ref.shape[0]):
            out_ref[shard, rows, :] = spread


def append_kernel(keep_ref, got_ref, spread_ref, out_ref):
    terms = (keep_ref[...] + got_ref[...].astype(jnp.float32)).astype(jnp.bfloat16)
    rows = pl.ds(out_ref.shape[1] - terms.shape[0], terms.shape[0])
    for shard in range(out_ref.shape[0]):
        out_ref[shard, rows, :] = terms


def sum_of_four(parts_ref, rows):
    part = lambda index: parts_ref[index, rows, :].astype(jnp.float32)
    return (part(0) + part(2)) + (part(1) + part(3))


def far_join_kernel(keep_ref, got_ref, grads_ref, out_ref):
    half = keep_ref.shape[0]
    out_ref[:half, :] = (keep_ref[...] + got_ref[...].astype(jnp.float32)).astype(jnp.bfloat16)
    out_ref[half:, :] = grads_ref[...]


def near_join_kernel(keep_ref, got_ref, far_ref, grads_ref, out_ref):
    shards = out_ref.shape[0]
    half = keep_ref.shape[0]
    own = half // shards
    grads = grads_ref[...].astype(jnp.float32) + far_ref[half:, :].astype(jnp.float32)
    grads = grads.astype(jnp.bfloat16)
    for shard in range(shards):
        rows = pl.ds(shard * own, own)
        total = keep_ref[rows, :] + got_ref[rows, :].astype(jnp.float32)
        total += far_ref[rows, :].astype(jnp.float32)
        out_ref[shard, pl.ds(0, own), :] = total.astype(jnp.bfloat16)
        out_ref[shard, pl.ds(own, grads.shape[0]), :] = grads


def total_kernel(scale_factor, parts_ref, half_ref):
    extra = half_ref.shape[0] - 8 + BIAS_ROWS
    tail = sum_of_four(parts_ref, pl.ds(parts_ref.shape[1] - extra, extra))
    tail = tail * scale_factor
    height = half_ref.shape[0] - 8
    half_ref[:height, :] = tail[:height, :]
    bias_row = tail[height : height + 1, :] + tail[height + 1 : height + 2, :]
    half_ref[height:, :] = jnp.broadcast_to(bias_row, (8, bias_row.shape[1]))


def features_kernel(parts_ref, degree_ref, features_ref):
    tiles, edge = degree_ref.shape
    roots = lax.rsqrt(degree_ref[...].astype(jnp.float32))
    for tile in range(tiles):
        rows = pl.ds(tile * edge, edge)
        total = sum_of_four(parts_ref, rows)
        features_ref[rows, :] = (total * roots[tile : tile + 1, :]).T.astype(jnp.bfloat16)


def lay_out_kernel(place_ref, mine_ref, other_ref, grads_ref, bias_ref):
    first = place_ref[0] % 2 == 0
    height = grads_ref.shape[0]
    width = mine_ref.shape[1]
    mine, other = mine_ref[...], other_ref[...]
    halves = (jnp.where(first, mine, other), jnp.where(first, other, mine))
    for index, half in enumerate(halves):
        lanes = pl.ds(index * width, width)
        grads_ref[:, lanes] = half[:height, :]
        bias_ref[:, lanes] = half[height : height + 1, :]


def per_device(
    features,
    degree,
    cotangent,
    weight,
    layer_bias,
    patterns,
    tile_row,
    tile_col,
    tile_pattern,
    tile_weight,
    tile_count,
):
    node_dev, feature_count = features.shape
    hidden = weight.shape[1]
    row_devices = lax.axis_size("row")
    col_devices = lax.axis_size("col")
    chips = row_devices // 2
    edge = patterns.shape[1]
    per_shard = node_dev // edge
    row = lax.axis_index("row")
    swap = [(index, index ^ 1) for index in range(row_devices)]
    row_near = [
        [(low * 4 + ring) * 2 + core_index for ring in pair for low in range(2)]
        for core_index in range(2)
        for pair in PAIRS[core_index]
    ]
    row_far = [
        (index, (index // 8 * 4 + far_neighbour(index // 2 % 4, index % 2)) * 2 + index % 2)
        for index in range(row_devices)
    ]
    exchange = functools.partial(lax.all_to_all, split_axis=0, concat_axis=0)
    extra = feature_count + BIAS_ROWS
    half = chips * node_dev
    bf16, f32 = jnp.bfloat16, jnp.float32
    shape = jax.ShapeDtypeStruct
    degree_tiles = degree.reshape(per_shard, edge)
    tile_cost = pl.CostEstimate(
        flops=tile_row.size // (row_devices * col_devices) * edge * edge * feature_count,
        bytes_accessed=patterns.size * 2 + 4 * half * feature_count * 2,
        transcendentals=0,
    )

    scaled = pl.pallas_call(
        scale_kernel,
        out_shape=shape((4, node_dev, feature_count), bf16),
        in_specs=[HBM] * 2,
        out_specs=VMEM,
        scratch_shapes=[
            pltpu.VMEM(features.shape, bf16),
            pltpu.VMEM(degree_tiles.shape, jnp.int32),
            pltpu.SemaphoreType.DMA((2,)),
        ],
        compiler_params=pltpu.CompilerParams(vmem_limit_bytes=62 * 1024 * 1024),
    )(features, degree_tiles)
    near_own = exchange(scaled, "row", axis_index_groups=row_near).reshape(half // 2, feature_count)
    near_other = lax.ppermute(near_own, "row", swap)
    far_own = lax.ppermute(near_own, "row", row_far)
    row_tiles, near_own = lax.optimization_barrier((tile_row.reshape(per_shard, edge), near_own))
    place = row.astype(jnp.int32).reshape(1)
    slots = pl.pallas_call(
        order_kernel,
        out_shape=shape((1, ORDERED), jnp.int32),
        in_specs=[SMEM] * 2 + [HBM] * 4,
        out_specs=VMEM,
        scratch_shapes=[
            pltpu.VMEM((4, per_shard, edge), jnp.int32),
            pltpu.SemaphoreType.DMA((4,)),
        ],
        compiler_params=PARAMS,
        cost_estimate=pl.CostEstimate(flops=1 << 31, bytes_accessed=8 << 20, transcendentals=0),
    )(
        place,
        tile_count,
        row_tiles,
        tile_col.reshape(per_shard, edge),
        tile_pattern.reshape(per_shard, edge),
        tile_weight.reshape(per_shard, edge),
    )
    slots_scratch = [pltpu.SMEM((1, ORDERED), jnp.int32), pltpu.SemaphoreType.DMA]
    forward_panel = pltpu.VMEM((half, feature_count), bf16)
    row_sums = shape((col_devices * node_dev, feature_count), f32)
    near_sums = pl.pallas_call(
        forward_near_kernel,
        out_shape=row_sums,
        in_specs=[HBM] + [VMEM] * 3,
        out_specs=VMEM,
        scratch_shapes=[*slots_scratch, forward_panel],
        compiler_params=PARAMS,
        cost_estimate=tile_cost,
    )(slots, patterns, near_own, near_other)
    far_own, near_sums = lax.optimization_barrier((far_own, near_sums))
    far_other = lax.ppermute(far_own, "row", swap)
    row_part = pl.pallas_call(
        forward_far_kernel,
        out_shape=shape(row_sums.shape, bf16),
        in_specs=[HBM] + [VMEM] * 4,
        out_specs=VMEM,
        scratch_shapes=[*slots_scratch, forward_panel, pltpu.VMEM(row_sums.shape, f32)],
        compiler_params=PARAMS,
        cost_estimate=tile_cost,
    )(slots, patterns, far_own, far_other, near_sums)
    parts = exchange(row_part.reshape(col_devices, node_dev, feature_count), "col")
    pre_act, upstream, keep_terms, send_terms = pl.pallas_call(
        middle_kernel,
        out_shape=(
            shape((node_dev, hidden), f32),
            shape((node_dev, hidden), f32),
            shape((extra, edge), f32),
            shape((extra, edge), bf16),
        ),
        in_specs=[SMEM] + [VMEM] * 5,
        out_specs=(VMEM,) * 4,
        compiler_params=PARAMS,
    )(place, parts, degree_tiles, cotangent, weight, layer_bias[None, :])
    got_terms = lax.ppermute(send_terms, "row", swap)
    spread = pl.pallas_call(
        spread_kernel,
        out_shape=shape((col_devices, node_dev + extra, edge), bf16),
        in_specs=[VMEM] * 2,
        out_specs=VMEM,
        compiler_params=PARAMS,
    )(upstream, weight)
    spread = pl.pallas_call(
        append_kernel,
        out_shape=shape(spread.shape, bf16),
        in_specs=[VMEM] * 3,
        out_specs=VMEM,
        input_output_aliases={2: 0},
        compiler_params=PARAMS,
    )(keep_terms, got_terms, spread)
    spread_all = exchange(spread, "col")
    kept, sent = shape((half // 2, edge), f32), shape((half // 2, edge), bf16)
    send, grads = pl.pallas_call(
        backward_send_kernel,
        out_shape=(sent, shape((extra, edge), bf16)),
        in_specs=[HBM] + [VMEM] * 2,
        out_specs=(VMEM,) * 2,
        scratch_shapes=[*slots_scratch, pltpu.VMEM(kept.shape, f32)],
        compiler_params=PARAMS,
        cost_estimate=tile_cost,
    )(slots, patterns, spread_all)
    send, spread_all = lax.optimization_barrier((send, spread_all))
    got = lax.ppermute(send, "row", swap)
    keep = pl.pallas_call(
        backward_keep_kernel,
        out_shape=kept,
        in_specs=[HBM] + [VMEM] * 2,
        out_specs=VMEM,
        scratch_shapes=slots_scratch,
        compiler_params=PARAMS,
        cost_estimate=tile_cost,
    )(slots, patterns, spread_all)
    far_sums = pl.pallas_call(
        far_join_kernel,
        out_shape=shape((half // 2 + extra, edge), bf16),
        in_specs=[VMEM] * 3,
        out_specs=VMEM,
        compiler_params=PARAMS,
    )(keep, got, grads)
    far_sums, spread_all = lax.optimization_barrier((far_sums, spread_all))
    far_got = lax.ppermute(far_sums, "row", row_far)
    keep, send = pl.pallas_call(
        backward_near_kernel,
        out_shape=(kept, sent),
        in_specs=[HBM] + [VMEM] * 2,
        out_specs=(VMEM,) * 2,
        scratch_shapes=[*slots_scratch, pltpu.VMEM((half, edge), f32)],
        compiler_params=PARAMS,
        cost_estimate=tile_cost,
    )(slots, patterns, spread_all)
    got = lax.ppermute(send, "row", swap)
    pre_act, keep = lax.optimization_barrier((pre_act, keep))
    activations = pl.pallas_call(
        activation_kernel,
        out_shape=shape((node_dev, hidden), bf16),
        in_specs=[VMEM],
        out_specs=VMEM,
        compiler_params=PARAMS,
    )(pre_act)
    got, far_got, activations = lax.optimization_barrier((got, far_got, activations))
    joined = pl.pallas_call(
        near_join_kernel,
        out_shape=shape((4, node_dev + extra, edge), bf16),
        in_specs=[VMEM] * 4,
        out_specs=VMEM,
        compiler_params=PARAMS,
    )(keep, got, far_got, grads)
    back_parts = exchange(joined, "row", axis_index_groups=row_near)
    scale_factor = 1.0 / math.sqrt(node_dev * row_devices * col_devices)
    mine = pl.pallas_call(
        functools.partial(total_kernel, scale_factor),
        out_shape=shape((feature_count + 8, edge), f32),
        in_specs=[VMEM],
        out_specs=VMEM,
        compiler_params=PARAMS,
    )(back_parts)
    other = lax.ppermute(mine, "row", swap)
    grad_features = pl.pallas_call(
        features_kernel,
        out_shape=shape((node_dev, feature_count), bf16),
        in_specs=[VMEM] * 2,
        out_specs=VMEM,
        compiler_params=PARAMS,
    )(back_parts, degree_tiles)
    grad_weight, grad_bias = pl.pallas_call(
        lay_out_kernel,
        out_shape=(shape((feature_count, hidden), f32), shape((1, hidden), f32)),
        in_specs=[SMEM] + [VMEM] * 2,
        out_specs=(VMEM,) * 2,
        compiler_params=PARAMS,
    )(place, mine, other)
    return (activations, grad_features, grad_weight, grad_bias[0])


def solution(mesh):
    in_specs = (
        P(("row", "col"), None),
        P(("row", "col")),
        P(("row", "col"), None),
        P(),
        P(),
        P(),
        P("row", "col", None),
        P("row", "col", None),
        P("row", "col", None),
        P("row", "col", None),
        P("row", "col"),
    )
    out_specs = (P(("row", "col"), None), P(("row", "col"), None), P(), P())
    return jax.shard_map(
        per_device, mesh=mesh, in_specs=in_specs, out_specs=out_specs, check_vma=False
    )
```

```python
import functools
import math

import jax
import jax.numpy as jnp
from jax import lax
from jax.experimental import pallas as pl
from jax.experimental.pallas import tpu as pltpu
from jax.sharding import PartitionSpec as P

GROUP = 64
VMEM_LIMIT = 20 * 1024 * 1024
ROOT_2_PI = math.sqrt(2.0 / math.pi)
CUBIC = 0.044715
BIAS_ROWS = 16
PER_SHARD = 4
CLASSES = 4
ORDERED = 640
BOUNDS = 600
PAIRS = (((0, 1), (2, 3)), ((0, 3), (1, 2)))
HBM = pl.BlockSpec(memory_space=pltpu.HBM)
VMEM = pl.BlockSpec(memory_space=pltpu.VMEM)
SMEM = pl.BlockSpec(memory_space=pltpu.SMEM)
PARAMS = pltpu.CompilerParams(vmem_limit_bytes=VMEM_LIMIT)


def pair_of(place, core):
    return jnp.where(core == 0, place >> 1, (place ^ (place >> 1)) & 1)


def pair_index(place, core):
    return jnp.where(core == 0, place & 1, place >> 1)


def far_neighbour(place, core):
    return place ^ 3 if core == 0 else place ^ 1


def order_kernel(
    place_ref, live_ref, row_hbm, col_hbm, pattern_hbm, weight_hbm, out_ref, fields, sems
):
    sources = (row_hbm, col_hbm, pattern_hbm, weight_hbm)
    copies = [
        pltpu.make_async_copy(source, fields.at[index], sems.at[index])
        for index, source in enumerate(sources)
    ]
    for copy in copies:
        copy.start()
    for copy in copies:
        copy.wait()
    row = place_ref[0]
    _, rows, edge = fields.shape
    tile_row, tile_col = fields[0], fields[1]
    shard = tile_col // PER_SHARD
    parity = shard % 2
    chip = shard // 2
    ring = chip % 4
    tile = tile_col % PER_SHARD
    half = parity ^ (row % 2)
    far = (pair_of(ring, parity) != pair_of((row // 2) % 4, parity)).astype(jnp.int32)
    rank = pair_index(ring, parity) * 2 + chip // 4
    place = (half * 4 + rank) * PER_SHARD + tile
    word = tile_row | (fields[2] << 5) | (fields[3] << 11) | (place << 14)
    slot = lax.broadcasted_iota(jnp.int32, (rows, edge), 0) * edge
    slot += lax.broadcasted_iota(jnp.int32, (rows, edge), 1)
    alive = slot < live_ref[0, 0]
    word = jnp.where(alive, word, 0)
    kind = jnp.where(alive, far * 2 + half, CLASSES)

    flags = [(kind == index).astype(jnp.float32) for index in range(CLASSES + 1)]
    stacked = jnp.concatenate(flags + [jnp.zeros((4, edge), jnp.float32)], 0)
    before = lax.broadcasted_iota(jnp.int32, (edge, edge), 0) < lax.broadcasted_iota(
        jnp.int32, (edge, edge), 1
    )
    earlier = jnp.dot(
        stacked.astype(jnp.bfloat16),
        before.astype(jnp.float32).astype(jnp.bfloat16),
        preferred_element_type=jnp.float32,
    )
    counts = jnp.sum(stacked, axis=1, keepdims=True)
    start = jnp.zeros((1, 1), jnp.float32)
    ends = []
    position = [jnp.zeros((1, edge), jnp.float32) for _ in range(rows)]
    for index in range(CLASSES + 1):
        for line in range(rows):
            at = index * rows + line
            position[line] += flags[index][line : line + 1] * (start + earlier[at : at + 1])
            start = start + counts[at : at + 1]
        ends.append(start)
    turned = jnp.concatenate(position + [jnp.zeros((8 - rows, edge), jnp.float32)], 0).T
    slots = rows * edge
    lanes = lax.broadcasted_iota(jnp.int32, (edge, slots), 1).astype(jnp.float32)
    pieces = jnp.zeros((8, slots), jnp.float32)
    for line in range(rows):
        chosen = (turned[:, line : line + 1] == lanes).astype(jnp.float32).astype(jnp.bfloat16)
        parts = [(word[line : line + 1] >> shift) & 127 for shift in (0, 7, 14)]
        parts = jnp.concatenate(parts + [jnp.zeros((5, edge), jnp.int32)], 0)
        parts = parts.astype(jnp.float32).astype(jnp.bfloat16)
        pieces += jnp.dot(parts, chosen, preferred_element_type=jnp.float32)
    pieces = pieces.astype(jnp.int32)
    out_ref[:, :slots] = pieces[0:1] | (pieces[1:2] << 7) | (pieces[2:3] << 14)
    lane = lax.broadcasted_iota(jnp.int32, (1, out_ref.shape[1] - slots), 1) + slots
    tail = jnp.zeros(lane.shape, jnp.int32)
    for index in range(CLASSES):
        tail = jnp.where(lane == BOUNDS + index, ends[index].astype(jnp.int32), tail)
    out_ref[:, slots:] = tail


def root_columns(degree):
    rows = lax.rsqrt(degree.astype(jnp.float32))
    rows = jnp.concatenate([rows, jnp.ones((8 - rows.shape[0], rows.shape[1]), jnp.float32)], 0)
    return rows.T


def scale_kernel(features_hbm, degree_hbm, out_ref, features_ref, degree_ref, sems):
    tiles, edge = degree_ref.shape
    degree_copy = pltpu.make_async_copy(degree_hbm, degree_ref, sems.at[tiles])
    degree_copy.start()
    copies = []
    for tile in range(tiles):
        rows = pl.ds(tile * edge, edge)
        copies.append(
            pltpu.make_async_copy(features_hbm.at[rows], features_ref.at[rows], sems.at[tile])
        )
        copies[-1].start()
    degree_copy.wait()
    roots = root_columns(degree_ref[...])
    for tile in range(tiles):
        rows = pl.ds(tile * edge, edge)
        copies[tile].wait()
        scaled = features_ref[rows, :].astype(jnp.float32) * roots[:, tile : tile + 1]
        scaled = scaled.astype(jnp.bfloat16)
        for copy in range(out_ref.shape[0]):
            out_ref[copy, rows, :] = scaled


def add_products(slots_ref, first, end, product_of, place_of, sums):
    edge = sums.shape[1]

    def one_group(turn, carry):
        terms = []
        for member in range(GROUP):
            slot = first + turn * GROUP + member
            word = slots_ref[0, slot]
            factor = jnp.where(slot < end, (word >> 11) & 7, 0).astype(jnp.float32)
            terms.append((place_of(word), factor, product_of(word)))
        for place, factor, product in terms:
            rows = pl.ds(pl.multiple_of(place * edge, edge), edge)
            sums[rows, :] += factor * product
        return carry

    lax.fori_loop(0, (end - first + GROUP - 1) // GROUP, one_group, 0)


def class_end(slots_ref, index):
    return slots_ref[0, BOUNDS + index]


def tile_of(ref, place, edge):
    return ref[pl.ds(pl.multiple_of(place * edge, edge), edge), :]


def forward_sums(slots_ref, patterns_ref, panel, sums, first, end):
    edge = patterns_ref.shape[1]

    def product_of(word):
        return jnp.dot(
            patterns_ref[(word >> 5) & 63],
            tile_of(panel, (word >> 14) & 31, edge),
            preferred_element_type=jnp.float32,
        )

    add_products(slots_ref, first, end, product_of, lambda word: word & 31, sums)


def forward_near_kernel(
    slots_from, patterns_ref, own_ref, other_ref, out_ref, slots_ref, sem, panel
):
    copy = pltpu.make_async_copy(slots_from, slots_ref, sem)
    copy.start()
    half = own_ref.shape[0]
    panel[:half, :] = own_ref[...]
    panel[half:, :] = other_ref[...]
    out_ref[...] = jnp.zeros_like(out_ref)
    copy.wait()
    forward_sums(slots_ref, patterns_ref, panel, out_ref, 0, class_end(slots_ref, 1))


def forward_far_kernel(
    slots_from, patterns_ref, own_ref, other_ref, so_far_ref, out_ref, slots_ref, sem, panel, sums
):
    copy = pltpu.make_async_copy(slots_from, slots_ref, sem)
    copy.start()
    half = own_ref.shape[0]
    panel[:half, :] = own_ref[...]
    panel[half:, :] = other_ref[...]
    sums[...] = so_far_ref[...]
    copy.wait()
    first, end = class_end(slots_ref, 1), class_end(slots_ref, 3)
    forward_sums(slots_ref, patterns_ref, panel, sums, first, end)
    out_ref[...] = sums[...].astype(jnp.bfloat16)


def backward_sums(slots_ref, patterns_ref, spread_ref, sums, first, end):
    edge = patterns_ref.shape[1]
    mask = sums.shape[0] // edge - 1

    def product_of(word):
        start = pl.multiple_of((word & 3) * edge, edge)
        return jnp.dot(
            spread_ref[(word >> 2) & 7, pl.ds(start, edge), :],
            patterns_ref[(word >> 5) & 63],
            preferred_element_type=jnp.float32,
        )

    add_products(slots_ref, first, end, product_of, lambda word: (word >> 14) & mask, sums)


def backward_send_kernel(
    slots_from, patterns_ref, spread_ref, send_ref, grads_ref, slots_ref, sem, sums
):
    copy = pltpu.make_async_copy(slots_from, slots_ref, sem)
    copy.start()
    sums[...] = jnp.zeros_like(sums)
    own = spread_ref.shape[1] - grads_ref.shape[0]
    grads = spread_ref[0, own:, :].astype(jnp.float32)
    for shard in range(1, spread_ref.shape[0]):
        grads += spread_ref[shard, own:, :].astype(jnp.float32)
    grads_ref[...] = grads.astype(jnp.bfloat16)
    copy.wait()
    first, end = class_end(slots_ref, 2), class_end(slots_ref, 3)
    backward_sums(slots_ref, patterns_ref, spread_ref, sums, first, end)
    send_ref[...] = sums[...].astype(jnp.bfloat16)


def backward_keep_kernel(slots_from, patterns_ref, spread_ref, keep_ref, slots_ref, sem):
    copy = pltpu.make_async_copy(slots_from, slots_ref, sem)
    copy.start()
    keep_ref[...] = jnp.zeros_like(keep_ref)
    copy.wait()
    first, end = class_end(slots_ref, 1), class_end(slots_ref, 2)
    backward_sums(slots_ref, patterns_ref, spread_ref, keep_ref, first, end)


def backward_near_kernel(
    slots_from, patterns_ref, spread_ref, keep_ref, send_ref, slots_ref, sem, sums
):
    copy = pltpu.make_async_copy(slots_from, slots_ref, sem)
    copy.start()
    sums[...] = jnp.zeros_like(sums)
    copy.wait()
    backward_sums(slots_ref, patterns_ref, spread_ref, sums, 0, class_end(slots_ref, 1))
    half = keep_ref.shape[0]
    keep_ref[...] = sums[:half, :]
    send_ref[...] = sums[half:, :].astype(jnp.bfloat16)


def split_product(left, right, dims):
    high = left.astype(jnp.bfloat16)
    low = (left - high.astype(jnp.float32)).astype(jnp.bfloat16)
    return lax.dot_general(
        high, right, (dims, ((), ())), preferred_element_type=jnp.float32
    ) + lax.dot_general(low, right, (dims, ((), ())), preferred_element_type=jnp.float32)


def activate(pre_act):
    square = pre_act * pre_act
    bent = jnp.tanh(ROOT_2_PI * (pre_act + CUBIC * (pre_act * square)))
    return square, bent, 0.5 * (1.0 + bent)


def middle_kernel(
    place_ref,
    parts_ref,
    degree_ref,
    cotangent_ref,
    weight_ref,
    bias_ref,
    pre_ref,
    upstream_ref,
    keep_ref,
    send_ref,
):
    tiles, edge = degree_ref.shape
    shards = parts_ref.shape[0]
    weight = weight_ref[...]
    height = weight.shape[0]
    roots = root_columns(degree_ref[...])
    grads = jnp.zeros(weight.shape, jnp.float32)
    bias_row = jnp.zeros(bias_ref.shape, jnp.float32)
    for tile in range(tiles):
        rows = pl.ds(tile * edge, edge)
        sums = parts_ref[0, rows, :].astype(jnp.float32)
        for shard in range(1, shards):
            sums += parts_ref[shard, rows, :].astype(jnp.float32)
        inv_root = roots[:, tile : tile + 1]
        pre_act = inv_root * split_product(sums, weight, ((1,), (0,))) + bias_ref[...]
        pre_ref[rows, :] = pre_act
        square, bent, half = activate(pre_act)
        rise = 0.5 * pre_act * (1.0 - bent * bent) * (ROOT_2_PI * (1.0 + 3.0 * CUBIC * square))
        slope = cotangent_ref[rows, :].astype(jnp.float32) * (half + rise)
        upstream = inv_root * slope
        upstream_ref[rows, :] = upstream
        grads += split_product(sums, upstream.astype(jnp.bfloat16), ((0,), (0,)))
        bias_row += jnp.sum(slope, axis=0, keepdims=True)
    width = keep_ref.shape[1]
    bias_high = bias_row.astype(jnp.bfloat16).astype(jnp.float32)
    bias_low = bias_row - bias_high
    first = place_ref[0] % 2 == 0

    def put(target, left):
        pick = lambda whole: jnp.where(left, whole[:, :width], whole[:, width:])
        target[:height, :] = pick(grads).astype(target.dtype)
        row_ids = lax.broadcasted_iota(jnp.int32, (BIAS_ROWS, width), 0)
        block = jnp.where(row_ids == 0, pick(bias_high), 0.0)
        block = jnp.where(row_ids == 1, pick(bias_low), block)
        target[height:, :] = block.astype(target.dtype)

    put(keep_ref, first)
    put(send_ref, jnp.logical_not(first))


def activation_kernel(pre_ref, act_ref):
    pre_act = pre_ref[...]
    act_ref[...] = (pre_act * activate(pre_act)[2]).astype(jnp.bfloat16)


def spread_kernel(upstream_ref, weight_ref, out_ref):
    edge = out_ref.shape[2]
    for tile in range(upstream_ref.shape[0] // edge):
        rows = pl.ds(tile * edge, edge)
        upstream = upstream_ref[rows, :]
        high = upstream.astype(jnp.bfloat16)
        low = (upstream - high.astype(jnp.float32)).astype(jnp.bfloat16)
        spread = sum(
            lax.dot_general(
                weight_ref[...], part, (((1,), (1,)), ((), ())), preferred_element_type=jnp.float32
            )
            for part in (high, low)
        ).astype(jnp.bfloat16)
        for shard in range(out_ref.shape[0]):
            out_ref[shard, rows, :] = spread


def append_kernel(keep_ref, got_ref, spread_ref, out_ref):
    terms = (keep_ref[...] + got_ref[...].astype(jnp.float32)).astype(jnp.bfloat16)
    rows = pl.ds(out_ref.shape[1] - terms.shape[0], terms.shape[0])
    for shard in range(out_ref.shape[0]):
        out_ref[shard, rows, :] = terms


def sum_of_four(parts_ref, rows):
    part = lambda index: parts_ref[index, rows, :].astype(jnp.float32)
    return (part(0) + part(2)) + (part(1) + part(3))


def far_join_kernel(keep_ref, got_ref, grads_ref, out_ref):
    half = keep_ref.shape[0]
    out_ref[:half, :] = (keep_ref[...] + got_ref[...].astype(jnp.float32)).astype(jnp.bfloat16)
    out_ref[half:, :] = grads_ref[...]


def near_join_kernel(keep_ref, got_ref, far_ref, grads_ref, out_ref):
    shards = out_ref.shape[0]
    half = keep_ref.shape[0]
    own = half // shards
    grads = grads_ref[...].astype(jnp.float32) + far_ref[half:, :].astype(jnp.float32)
    grads = grads.astype(jnp.bfloat16)
    for shard in range(shards):
        rows = pl.ds(shard * own, own)
        total = keep_ref[rows, :] + got_ref[rows, :].astype(jnp.float32)
        total += far_ref[rows, :].astype(jnp.float32)
        out_ref[shard, pl.ds(0, own), :] = total.astype(jnp.bfloat16)
        out_ref[shard, pl.ds(own, grads.shape[0]), :] = grads


def total_kernel(scale_factor, parts_ref, half_ref):
    extra = half_ref.shape[0] - 8 + BIAS_ROWS
    tail = sum_of_four(parts_ref, pl.ds(parts_ref.shape[1] - extra, extra))
    tail = tail * scale_factor
    height = half_ref.shape[0] - 8
    half_ref[:height, :] = tail[:height, :]
    bias_row = tail[height : height + 1, :] + tail[height + 1 : height + 2, :]
    half_ref[height:, :] = jnp.broadcast_to(bias_row, (8, bias_row.shape[1]))


def features_kernel(parts_ref, degree_ref, features_ref):
    tiles, edge = degree_ref.shape
    roots = lax.rsqrt(degree_ref[...].astype(jnp.float32))
    for tile in range(tiles):
        rows = pl.ds(tile * edge, edge)
        total = sum_of_four(parts_ref, rows)
        features_ref[rows, :] = (total * roots[tile : tile + 1, :]).T.astype(jnp.bfloat16)


def lay_out_kernel(place_ref, mine_ref, other_ref, grads_ref, bias_ref):
    first = place_ref[0] % 2 == 0
    height = grads_ref.shape[0]
    width = mine_ref.shape[1]
    mine, other = mine_ref[...], other_ref[...]
    halves = (jnp.where(first, mine, other), jnp.where(first, other, mine))
    for index, half in enumerate(halves):
        lanes = pl.ds(index * width, width)
        grads_ref[:, lanes] = half[:height, :]
        bias_ref[:, lanes] = half[height : height + 1, :]


def per_device(
    features,
    degree,
    cotangent,
    weight,
    layer_bias,
    patterns,
    tile_row,
    tile_col,
    tile_pattern,
    tile_weight,
    tile_count,
):
    node_dev, feature_count = features.shape
    hidden = weight.shape[1]
    row_devices = lax.axis_size("row")
    col_devices = lax.axis_size("col")
    chips = row_devices // 2
    edge = patterns.shape[1]
    per_shard = node_dev // edge
    row = lax.axis_index("row")
    swap = [(index, index ^ 1) for index in range(row_devices)]
    row_near = [
        [(low * 4 + ring) * 2 + core_index for ring in pair for low in range(2)]
        for core_index in range(2)
        for pair in PAIRS[core_index]
    ]
    row_far = [
        (index, (index // 8 * 4 + far_neighbour(index // 2 % 4, index % 2)) * 2 + index % 2)
        for index in range(row_devices)
    ]
    exchange = functools.partial(lax.all_to_all, split_axis=0, concat_axis=0)
    extra = feature_count + BIAS_ROWS
    half = chips * node_dev
    bf16, f32 = jnp.bfloat16, jnp.float32
    shape = jax.ShapeDtypeStruct
    degree_tiles = degree.reshape(per_shard, edge)
    tile_cost = pl.CostEstimate(
        flops=tile_row.size // (row_devices * col_devices) * edge * edge * feature_count,
        bytes_accessed=patterns.size * 2 + 4 * half * feature_count * 2,
        transcendentals=0,
    )

    scaled = pl.pallas_call(
        scale_kernel,
        out_shape=shape((4, node_dev, feature_count), bf16),
        in_specs=[HBM] * 2,
        out_specs=VMEM,
        scratch_shapes=[
            pltpu.VMEM(features.shape, bf16),
            pltpu.VMEM(degree_tiles.shape, jnp.int32),
            pltpu.SemaphoreType.DMA((per_shard + 1,)),
        ],
        compiler_params=pltpu.CompilerParams(vmem_limit_bytes=62 * 1024 * 1024),
    )(features, degree_tiles)
    near_own = exchange(scaled, "row", axis_index_groups=row_near).reshape(half // 2, feature_count)
    near_other = lax.ppermute(near_own, "row", swap)
    far_own = lax.ppermute(near_own, "row", row_far)
    row_tiles, near_own = lax.optimization_barrier((tile_row.reshape(per_shard, edge), near_own))
    place = row.astype(jnp.int32).reshape(1)
    slots = pl.pallas_call(
        order_kernel,
        out_shape=shape((1, ORDERED), jnp.int32),
        in_specs=[SMEM] * 2 + [HBM] * 4,
        out_specs=VMEM,
        scratch_shapes=[
            pltpu.VMEM((4, per_shard, edge), jnp.int32),
            pltpu.SemaphoreType.DMA((4,)),
        ],
        compiler_params=PARAMS,
    )(
        place,
        tile_count,
        row_tiles,
        tile_col.reshape(per_shard, edge),
        tile_pattern.reshape(per_shard, edge),
        tile_weight.reshape(per_shard, edge),
    )
    slots_scratch = [pltpu.SMEM((1, ORDERED), jnp.int32), pltpu.SemaphoreType.DMA]
    forward_panel = pltpu.VMEM((half, feature_count), bf16)
    row_sums = shape((col_devices * node_dev, feature_count), f32)
    near_sums = pl.pallas_call(
        forward_near_kernel,
        out_shape=row_sums,
        in_specs=[HBM] + [VMEM] * 3,
        out_specs=VMEM,
        scratch_shapes=[*slots_scratch, forward_panel],
        compiler_params=PARAMS,
        cost_estimate=tile_cost,
    )(slots, patterns, near_own, near_other)
    far_own, near_sums = lax.optimization_barrier((far_own, near_sums))
    far_other = lax.ppermute(far_own, "row", swap)
    row_part = pl.pallas_call(
        forward_far_kernel,
        out_shape=shape(row_sums.shape, bf16),
        in_specs=[HBM] + [VMEM] * 4,
        out_specs=VMEM,
        scratch_shapes=[*slots_scratch, forward_panel, pltpu.VMEM(row_sums.shape, f32)],
        compiler_params=PARAMS,
        cost_estimate=tile_cost,
    )(slots, patterns, far_own, far_other, near_sums)
    parts = exchange(row_part.reshape(col_devices, node_dev, feature_count), "col")
    pre_act, upstream, keep_terms, send_terms = pl.pallas_call(
        middle_kernel,
        out_shape=(
            shape((node_dev, hidden), f32),
            shape((node_dev, hidden), f32),
            shape((extra, edge), f32),
            shape((extra, edge), bf16),
        ),
        in_specs=[SMEM] + [VMEM] * 5,
        out_specs=(VMEM,) * 4,
        compiler_params=PARAMS,
    )(place, parts, degree_tiles, cotangent, weight, layer_bias[None, :])
    got_terms = lax.ppermute(send_terms, "row", swap)
    spread = pl.pallas_call(
        spread_kernel,
        out_shape=shape((col_devices, node_dev + extra, edge), bf16),
        in_specs=[VMEM] * 2,
        out_specs=VMEM,
        compiler_params=PARAMS,
    )(upstream, weight)
    spread = pl.pallas_call(
        append_kernel,
        out_shape=shape(spread.shape, bf16),
        in_specs=[VMEM] * 3,
        out_specs=VMEM,
        input_output_aliases={2: 0},
        compiler_params=PARAMS,
    )(keep_terms, got_terms, spread)
    spread_all = exchange(spread, "col")
    kept, sent = shape((half // 2, edge), f32), shape((half // 2, edge), bf16)
    send, grads = pl.pallas_call(
        backward_send_kernel,
        out_shape=(sent, shape((extra, edge), bf16)),
        in_specs=[HBM] + [VMEM] * 2,
        out_specs=(VMEM,) * 2,
        scratch_shapes=[*slots_scratch, pltpu.VMEM(kept.shape, f32)],
        compiler_params=PARAMS,
        cost_estimate=tile_cost,
    )(slots, patterns, spread_all)
    send, spread_all = lax.optimization_barrier((send, spread_all))
    got = lax.ppermute(send, "row", swap)
    keep = pl.pallas_call(
        backward_keep_kernel,
        out_shape=kept,
        in_specs=[HBM] + [VMEM] * 2,
        out_specs=VMEM,
        scratch_shapes=slots_scratch,
        compiler_params=PARAMS,
        cost_estimate=tile_cost,
    )(slots, patterns, spread_all)
    far_sums = pl.pallas_call(
        far_join_kernel,
        out_shape=shape((half // 2 + extra, edge), bf16),
        in_specs=[VMEM] * 3,
        out_specs=VMEM,
        compiler_params=PARAMS,
    )(keep, got, grads)
    far_sums, spread_all = lax.optimization_barrier((far_sums, spread_all))
    far_got = lax.ppermute(far_sums, "row", row_far)
    keep, send = pl.pallas_call(
        backward_near_kernel,
        out_shape=(kept, sent),
        in_specs=[HBM] + [VMEM] * 2,
        out_specs=(VMEM,) * 2,
        scratch_shapes=[*slots_scratch, pltpu.VMEM((half, edge), f32)],
        compiler_params=PARAMS,
        cost_estimate=tile_cost,
    )(slots, patterns, spread_all)
    got = lax.ppermute(send, "row", swap)
    pre_act, keep = lax.optimization_barrier((pre_act, keep))
    activations = pl.pallas_call(
        activation_kernel,
        out_shape=shape((node_dev, hidden), bf16),
        in_specs=[VMEM],
        out_specs=VMEM,
        compiler_params=PARAMS,
    )(pre_act)
    got, far_got, activations = lax.optimization_barrier((got, far_got, activations))
    joined = pl.pallas_call(
        near_join_kernel,
        out_shape=shape((4, node_dev + extra, edge), bf16),
        in_specs=[VMEM] * 4,
        out_specs=VMEM,
        compiler_params=PARAMS,
    )(keep, got, far_got, grads)
    back_parts = exchange(joined, "row", axis_index_groups=row_near)
    scale_factor = 1.0 / math.sqrt(node_dev * row_devices * col_devices)
    mine = pl.pallas_call(
        functools.partial(total_kernel, scale_factor),
        out_shape=shape((feature_count + 8, edge), f32),
        in_specs=[VMEM],
        out_specs=VMEM,
        compiler_params=PARAMS,
    )(back_parts)
    other = lax.ppermute(mine, "row", swap)
    grad_features = pl.pallas_call(
        features_kernel,
        out_shape=shape((node_dev, feature_count), bf16),
        in_specs=[VMEM] * 2,
        out_specs=VMEM,
        compiler_params=PARAMS,
    )(back_parts, degree_tiles)
    grad_weight, grad_bias = pl.pallas_call(
        lay_out_kernel,
        out_shape=(shape((feature_count, hidden), f32), shape((1, hidden), f32)),
        in_specs=[SMEM] + [VMEM] * 2,
        out_specs=(VMEM,) * 2,
        compiler_params=PARAMS,
    )(place, mine, other)
    return (activations, grad_features, grad_weight, grad_bias[0])


def solution(mesh):
    in_specs = (
        P(("row", "col"), None),
        P(("row", "col")),
        P(("row", "col"), None),
        P(),
        P(),
        P(),
        P("row", "col", None),
        P("row", "col", None),
        P("row", "col", None),
        P("row", "col", None),
        P("row", "col"),
    )
    out_specs = (P(("row", "col"), None), P(("row", "col"), None), P(), P())
    return jax.shard_map(
        per_device, mesh=mesh, in_specs=in_specs, out_specs=out_specs, check_vma=False
    )
```
